256 devices in a mesh: gx: 8 (over x, z_hi), gy: 32 (over y, z_lo, core).
Axes of the slice: x: 4, y: 4, z: 8 (z_hi: 2, z_lo: 4; z = z_hi * 4 + z_lo), core: 2. Of those that a mesh axis runs over, the one named last changes fastest.
Arguments:
- density: float32 [1, 2048, 2048], P(None, 'gy', 'gx'), may hold values from 0.35 to 2.5, as said below
- xmomentum: float32 [1, 2048, 2048], P(None, 'gy', 'gx'), may hold values from -2.5 to 2.5
- ymomentum: float32 [1, 2048, 2048], P(None, 'gy', 'gx'), may hold values from -2.5 to 2.5
- shear_shift: int32 [1], replicated, may hold values from 0 to 2047
Outputs:
- density_new: float32 [1, 2048, 2048], P(None, 'gy', 'gx')
- xmomentum_new: float32 [1, 2048, 2048], P(None, 'gy', 'gx')
- ymomentum_new: float32 [1, 2048, 2048], P(None, 'gy', 'gx')
- potential: float32 [1, 2048, 2048], P(None, 'gy', 'gx')
The draws below stay inside these ranges and needn't reach their ends.
Inputs may be any that keep to these rules, and one draw needn't show every extreme that they name: Every density is positive.
All inputs are finite; a program needn't handle non-finite values.
Results may differ from the reference program's by a relative error of at most 0.00065.
Values sent between devices are 32-bit elements; how exact they have to be, the bound alone decides.
No kernel may reach another device: no remote copies, remote signals or barrier semaphores. Data moves between devices by JAX's collectives and lax.ppermute only.
A program may use at most 64 MiB of HBM per device.

```python
import jax
import jax.numpy as jnp

NX = 2048
NY = 2048
PLANES = 1


def draw_density(key, part):
    rough = jax.random.uniform(jax.random.fold_in(key, 7), (PLANES, NY, NX), jnp.float32, -0.6, 0.6)
    values = jnp.exp(rough)
    return values


def block_levels(rng, extent, cuts, least, high):
    level, own = 1.0, jax.random.fold_in(rng, 6)
    for axis_at, blocks in cuts:
        heights = jnp.exp(jax.random.uniform(jax.random.fold_in(own, axis_at), (blocks,), jnp.float32, least / len(cuts), high / len(cuts)))
        level = level * jnp.repeat(heights, extent[axis_at] // blocks).reshape([-1 if axis == axis_at else 1 for axis in range(len(extent))])
    return level


def normal_values(own_key, shape, width, most, pieces=(), kind=jnp.bfloat16):
    gain = block_levels(own_key, shape, pieces, -0.22, 0.18) if pieces else 1.0
    result = jax.random.normal(own_key, shape, jnp.float32) * width * gain
    return jnp.minimum(jnp.maximum(result, -most), most).astype(kind)


def setup_inputs(seed: int = 0) -> dict:
    arg_keys = jax.random.split(jax.random.key(seed), 5)
    density = draw_density(jax.random.fold_in(arg_keys[4], 71), 0)
    xmomentum = normal_values(arg_keys[1], (PLANES, NY, NX), 0.4, 2.5, ((1, 32), (2, 8)), jnp.float32)
    ymomentum = normal_values(arg_keys[2], (PLANES, NY, NX), 0.4, 2.5, ((1, 32), (2, 8)), jnp.float32)
    shear_shift = jax.random.randint(arg_keys[3], (1,), 0, NY).astype(jnp.int32)
    return dict(density=density, xmomentum=xmomentum, ymomentum=ymomentum, shear_shift=shear_shift)


sound_speed = 1.0
time_step = 0.15
omega_rate = 0.5
shear_rate = 1.5
thickness = 0.5

def flux_of(state, normal):
    velocity = state[normal] / state[0]
    parts = [state[0] * velocity, state[1] * velocity, state[2] * velocity]
    parts[normal] = parts[normal] + sound_speed * sound_speed * state[0]
    return jnp.stack(parts)

def rusanov(left_state, right_state, normal):
    speed = jnp.maximum(jnp.abs(left_state[normal] / left_state[0]), jnp.abs(right_state[normal] / right_state[0])) + sound_speed
    return 0.5 * (flux_of(left_state, normal) + flux_of(right_state, normal)) - 0.5 * speed[None] * (right_state - left_state)

def advance(padded):
    flux_x = rusanov(padded[:, :, 1:-1, :-1], padded[:, :, 1:-1, 1:], 1)
    flux_y = rusanov(padded[:, :, :-1, 1:-1], padded[:, :, 1:, 1:-1], 2)
    state = padded[:, :, 1:-1, 1:-1]
    change = flux_x[..., 1:] - flux_x[..., :-1] + flux_y[:, :, 1:, :] - flux_y[:, :, :-1, :]
    updated = state - time_step * change
    density_new = updated[0]
    xmomentum_new = updated[1] + time_step * 2.0 * omega_rate * state[2]
    ymomentum_new = updated[2] - time_step * (2.0 - shear_rate) * omega_rate * state[1]
    return (density_new, xmomentum_new, ymomentum_new)

def kernel_table(y_waves, x_waves, shift):
    sigma = y_waves * shift % NY
    y_signed = jnp.where(y_waves < NY // 2, y_waves, y_waves - NY)
    x_signed = jnp.where(x_waves < NX // 2, x_waves, x_waves - NX)
    wave_x = 2.0 * jnp.pi / NX * (x_signed[None, :].astype(jnp.float32) + sigma[:, None].astype(jnp.float32) / NY)
    wave_y = 2.0 * jnp.pi / NY * y_signed[:, None].astype(jnp.float32)
    magnitude = jnp.sqrt(wave_x * wave_x + wave_y * wave_y)
    anchor = (y_waves[:, None] == 0) & (x_waves[None, :] == 0)
    safe_mag = jnp.where(anchor, 1.0, magnitude)
    return jnp.where(anchor, 0.0, -jnp.exp(-thickness * safe_mag) / safe_mag)

def reference(density, xmomentum, ymomentum, shear_shift):
    fields = jnp.stack([density, xmomentum, ymomentum])
    shift = shear_shift[0]
    left_col = jnp.roll(fields[..., -1], -shift, axis=2)
    right_col = jnp.roll(fields[..., 0], shift, axis=2)
    widened = jnp.concatenate([left_col[..., None], fields, right_col[..., None]], axis=3)
    padded = jnp.concatenate([widened[:, :, -1:], widened, widened[:, :, :1]], axis=2)
    density_new, xmomentum_new, ymomentum_new = advance(padded)
    y_waves = jnp.arange(NY, dtype=jnp.int32)
    x_waves = jnp.arange(NX, dtype=jnp.int32)
    sigma = y_waves * shift % NY
    angle = (sigma[:, None] * x_waves[None, :] % (NX * NY)).astype(jnp.float32) * (2.0 * jnp.pi / (NX * NY))
    spectrum = jnp.fft.fft(density_new, axis=1)
    sheared = spectrum * jnp.exp(-1j * angle)[None]
    modes = jnp.fft.fft(sheared, axis=2) * kernel_table(y_waves, x_waves, shift)[None]
    returned = jnp.fft.ifft(modes, axis=2) * jnp.exp(1j * angle)[None]
    potential = jnp.real(jnp.fft.ifft(returned, axis=1)).astype(jnp.float32)
    return (density_new, xmomentum_new, ymomentum_new, potential)
```

```python
import functools

import jax
import jax.numpy as jnp
import ml_dtypes
import numpy as np
from jax import lax
from jax.experimental import pallas as pl
from jax.experimental.pallas import tpu as pltpu
from jax.sharding import PartitionSpec as P

NX = 2048
NY = 2048
ROWS = 64
COLS = 256
GX = 8
GY = 32

time_step = 0.15
omega_rate = 0.5
shear_rate = 1.5
thickness = 0.5

BF = jnp.bfloat16
F32 = jnp.float32


def halves(table):
    table = np.asarray(table, np.float32)
    head = table.astype(ml_dtypes.bfloat16)
    rest = (table - head.astype(np.float32)).astype(ml_dtypes.bfloat16)
    return head, rest


def turn(index, length):
    angle = 2.0 * np.pi * (np.asarray(index) % length) / length
    return np.cos(angle), np.sin(angle)


@functools.cache
def host_tables():
    out = {}
    eye8 = np.eye(8)
    cos32, sin32 = turn(np.outer(np.arange(32), np.arange(32)), 32)
    out["blocks"] = halves(np.concatenate([np.kron(cos32, eye8), np.kron(-sin32, eye8)]))
    m1 = np.repeat(np.arange(32), 8)
    tc, ts = turn(np.outer(m1, np.arange(64)), NY)
    out["twist_re"] = np.concatenate([tc, -ts], 1).astype(np.float32)
    out["twist_im"] = np.concatenate([ts, tc], 1).astype(np.float32)
    c64, s64 = turn(np.outer(np.arange(32), np.arange(64)), 64)
    last = np.zeros((16, 128))
    last[0, :64] = 1.0 - 2.0 * (np.arange(64) % 2)
    out["inner"] = halves(
        np.concatenate([np.concatenate([c64, s64], 1), np.concatenate([-s64, c64], 1), last])
    )
    c256, s256 = turn(np.outer(np.arange(256), np.arange(256)), 256)
    out["groups"] = halves(np.concatenate([c256, s256]))
    lane = np.arange(128)
    sign = np.where(lane < 64, 1.0, -1.0)
    q = lane % 8
    tc, ts = turn(np.outer(np.arange(256), q), NX)
    out["radial_cos"] = tc.astype(np.float32)
    out["radial_sin"] = (ts * sign).astype(np.float32)
    c8, s8 = turn(np.outer(np.arange(8), np.arange(8)), 8)
    lines = np.eye(8)
    ck, sk = np.kron(lines, c8), np.kron(lines, s8)
    out["cells"] = halves(np.block([[ck, -sk], [sk, ck]]))
    out["cells_back"] = halves(np.block([[ck, sk], [-sk, ck]]))
    c64, s64 = turn(np.outer(np.arange(64), np.arange(32)), 64)
    out["inner_back"] = halves(np.concatenate([c64, s64]))
    pair = np.arange(512) // 128
    part = np.arange(512) % 128 // 64
    which = np.arange(512) % 64 // 8
    m1 = pair * 8 + which
    q = np.arange(512) % 8
    tc, ts = turn(np.outer(np.arange(64), m1), NY)
    out["back_cos"] = tc.astype(np.float32)
    out["back_sin"] = (ts * np.where(part == 0, 1.0, -1.0)).astype(np.float32)
    j = np.repeat(np.arange(32), 8)
    own = np.tile(np.arange(8), 32)
    c32, s32 = turn(np.outer(j, m1), 32)
    weight = np.where(part == 0, c32, -s32)
    weight = np.where((part == 1) & (m1 == 0), 1.0, weight)
    out["blocks_back"] = halves(weight * (own[:, None] == q[None, :]))
    return out


def split(value):
    head = value.astype(BF)
    rest = (value - head.astype(F32)).astype(BF)
    return head, rest


NN = (((1,), (0,)), ((), ()))
NT = (((1,), (1,)), ((), ()))


def product(table_head, table_rest, value, dims=NN):
    head, rest = split(value)
    dot = functools.partial(lax.dot_general, dimension_numbers=dims, preferred_element_type=F32)
    return dot(table_head, head) + (dot(table_head, rest) + dot(table_rest, head))


def product_right(value, table_head, table_rest):
    head, rest = split(value)
    dot = functools.partial(lax.dot_general, dimension_numbers=NN, preferred_element_type=F32)
    return dot(head, table_head) + (dot(rest, table_head) + dot(head, table_rest))


def roll(value, shift, axis):
    return pltpu.roll(value, shift % value.shape[axis], axis)


def lanes_of(shape):
    return lax.broadcasted_iota(jnp.int32, shape, 1)


def rows_of(shape):
    return lax.broadcasted_iota(jnp.int32, shape, 0)


def interface(left, right, normal):
    speed = jnp.maximum(jnp.abs(left[3]), jnp.abs(right[3])) + 1.0
    fluxes = []
    for part in range(3):
        f_left = left[part] * left[3]
        f_right = right[part] * right[3]
        if part == normal:
            f_left = f_left + left[0]
            f_right = f_right + right[0]
        fluxes.append(0.5 * (f_left + f_right) - 0.5 * speed * (right[part] - left[part]))
    return fluxes


def gas_kernel(rho, mx, my, left, right, below, above, rho_out, mx_out, my_out, packed):
    state = (rho[...], mx[...], my[...])
    lane = lanes_of((ROWS, COLS))
    row = rows_of((ROWS, COLS))

    def with_speed(fields, normal):
        return (*fields, fields[normal] / fields[0])

    on_left = [jnp.where(lane == 0, left[:, f : f + 1], roll(state[f], 1, 1)) for f in range(3)]
    on_right = [
        jnp.where(lane == COLS - 1, right[:, f : f + 1], roll(state[f], -1, 1)) for f in range(3)
    ]
    under = [jnp.where(row == 0, below[f : f + 1, :], roll(state[f], 1, 0)) for f in range(3)]
    over = [jnp.where(row == ROWS - 1, above[f : f + 1, :], roll(state[f], -1, 0)) for f in range(3)]
    mid_x = with_speed(state, 1)
    mid_y = with_speed(state, 2)
    west = interface(with_speed(on_left, 1), mid_x, 1)
    east = interface(mid_x, with_speed(on_right, 1), 1)
    south = interface(with_speed(under, 2), mid_y, 2)
    north = interface(mid_y, with_speed(over, 2), 2)
    change = [east[f] - west[f] + north[f] - south[f] for f in range(3)]
    new = [state[f] - time_step * change[f] for f in range(3)]
    new[1] = new[1] + time_step * 2.0 * omega_rate * state[2]
    new[2] = new[2] - time_step * (2.0 - shear_rate) * omega_rate * state[1]
    rho_out[...] = new[0]
    mx_out[...] = new[1]
    my_out[...] = new[2]
    packed[...] = jnp.concatenate([new[0], new[0]], 0).T


def forward_kernel(arrived, blocks_h, blocks_l, twist_re, twist_im, inner_h, inner_l, out):
    first = product(blocks_h[...], blocks_l[...], arrived[...])
    turned = first[:256] * twist_re[...] + first[256:] * twist_im[...]
    waves = product(inner_h[...], inner_l[...], turned, NT)
    lane = lanes_of((32, 128))
    row = rows_of((32, 128))
    for g in range(8):
        tile = slice(g // 4 * 128, g // 4 * 128 + 128)
        place = 32 * (g % 4)
        real = waves[0:32, tile]
        imag = waves[32:64, tile]
        if g == 0:
            imag = jnp.where((row == 0) & (lane < 8), waves[64:65, tile], imag)
        real = roll(real, -place, 1)
        imag = roll(imag, 64 - place, 1)
        both = jnp.where(lane < 32, real, 0.0) + jnp.where((lane >= 64) & (lane < 96), imag, 0.0)
        out[g * 32 : (g + 1) * 32, :] = both


def radial_kernel(
    flag,
    arrived,
    theta_cos,
    theta_sin,
    weights,
    groups_h,
    groups_l,
    radial_cos,
    radial_sin,
    cells_h,
    cells_l,
    back_h,
    back_l,
    out,
):
    shape = (256, 128)
    lane = lanes_of(shape)
    sign = jnp.where(lane < 64, 1.0, -1.0)
    value = arrived[...]
    first = jnp.zeros(shape, jnp.int32) + flag[0] == 1
    extra = (lane >= 32) & (lane < 40)
    slot = (lane >= 64) & (lane < 72)
    fifth = roll(value, -32, 1)
    value = jnp.where(extra, fifth, jnp.where(slot & first, 0.0, value))
    half = functools.partial(roll, shift=64, axis=1)
    ct = theta_cos[...]
    st = theta_sin[...]
    value = value * ct + half(value) * st
    both = product(groups_h[...], groups_l[...], value)
    value = both[:256] + sign * half(both[256:])
    value = value * radial_cos[...] + half(value) * radial_sin[...]
    value = product_right(value, cells_h[...], cells_l[...])
    value = value * weights[...]
    value = product_right(value, back_h[...], back_l[...])
    value = value * radial_cos[...] - half(value) * radial_sin[...]
    both = product(groups_h[...], groups_l[...], value)
    value = both[:256] - sign * half(both[256:])
    value = value * ct - half(value) * st
    out[...] = jnp.where(slot & first, roll(value, 32, 1), value)


def backward_kernel(arrived, inner_h, inner_l, back_cos, back_sin, blocks_h, blocks_l, out):
    lane = lanes_of((32, 128))
    low = lane % 64 < 32
    pairs = []
    for h in range(4):
        even = arrived[64 * h : 64 * h + 32, :]
        odd = arrived[64 * h + 32 : 64 * h + 64, :]
        pairs.append(jnp.where(low, even, roll(odd, 32, 1)))
    value = jnp.concatenate(pairs, 1)
    both = product(inner_h[...], inner_l[...], value)
    wide = lanes_of((64, 128))
    row = rows_of((64, 128))
    sign = jnp.where(wide < 64, 1.0, -1.0)
    parity = jnp.where(row % 2 == 0, 1.0, -1.0)
    turned = []
    for h in range(4):
        tile = slice(128 * h, 128 * h + 128)
        part = both[:64, tile] - sign * roll(both[64:, tile], 64, 1)
        part = part * back_cos[:, tile] - roll(part, 64, 1) * back_sin[:, tile]
        if h == 0:
            part = jnp.where((wide >= 64) & (wide < 72), parity * pairs[0][0:1, :], part)
        turned.append(part)
    turned = jnp.concatenate(turned, 1)
    turned = jnp.concatenate([turned, turned], 0)
    out[...] = product(blocks_h[...], blocks_l[...], turned, NT)


def last_kernel(arrived, out):
    out[...] = arrived[...].T[:ROWS]


VMEM = pl.BlockSpec(memory_space=pltpu.VMEM)
SMEM = pl.BlockSpec(memory_space=pltpu.SMEM)


def call(kernel, shapes, *args, name, smem=0):
    many = isinstance(shapes, list)
    outs = [jax.ShapeDtypeStruct(s, F32) for s in (shapes if many else [shapes])]
    return pl.pallas_call(
        kernel,
        out_shape=outs if many else outs[0],
        in_specs=[SMEM] * smem + [VMEM] * (len(args) - smem),
        out_specs=[VMEM] * len(outs) if many else VMEM,
        name=name,
        compiler_params=pltpu.CompilerParams(vmem_limit_bytes=32 * 1024 * 1024),
        cost_estimate=pl.CostEstimate(flops=100_000_000, bytes_accessed=1_000_000, transcendentals=0),
    )(*args)


def ghosts(columns_low, columns_high, shift):
    both = ("gx", "gy")

    def flat(i, j):
        return (i % GX) * GY + j % GY

    def branch(k):
        def run(low, high):
            near_left = [(flat(i, j), flat(i + 1, j)) for i in range(GX - 1) for j in range(GY)]
            near_right = [(flat(i + 1, j), flat(i, j)) for i in range(GX - 1) for j in range(GY)]
            wrap_left = [(flat(GX - 1, j + k), flat(0, j)) for j in range(GY)]
            wrap_right = [(flat(0, j - k), flat(GX - 1, j)) for j in range(GY)]
            next_left = [(flat(GX - 1, j + k + 1), flat(0, j)) for j in range(GY)]
            next_right = [(flat(0, j - k - 1), flat(GX - 1, j)) for j in range(GY)]
            return (
                lax.ppermute(high, both, near_left + wrap_left),
                lax.ppermute(low, both, near_right + wrap_right),
                lax.ppermute(high, both, next_left),
                lax.ppermute(low, both, next_right),
            )

        return run

    a_left, a_right, b_left, b_right = lax.switch(
        shift // ROWS, [branch(k) for k in range(GY)], columns_low, columns_high
    )
    off = shift % ROWS
    radial = lax.axis_index("gx")
    left_off = jnp.where(radial == 0, off, 0)
    right_off = jnp.where(radial == GX - 1, off, 0)
    left = lax.dynamic_slice_in_dim(jnp.concatenate([a_left, b_left]), left_off, ROWS, 0)
    right = lax.dynamic_slice_in_dim(
        jnp.concatenate([b_right, a_right]), ROWS - right_off, ROWS, 0
    )
    return left, right


def radial_tables(shift):
    shape = (256, 128)
    row = lax.broadcasted_iota(jnp.int32, shape, 0)
    lane = lax.broadcasted_iota(jnp.int32, shape, 1)
    line = lane % 64 // 8
    inside = lane % 8
    wave = lax.axis_index("gx") * 4 + line + GY * lax.axis_index("gy")
    wave = jnp.where(line < 4, wave, NY // 2)
    sigma = wave * shift % NY
    cell = row * 8 + inside
    angle = (sigma * cell % (NX * NY)).astype(F32) * (2.0 * jnp.pi / (NX * NY))
    sign = jnp.where(lane < 64, 1.0, -1.0)
    theta_cos = jnp.cos(angle)
    theta_sin = jnp.sin(angle) * sign
    n = row + 256 * inside
    n = jnp.where(n < NX // 2, n, n - NX)
    kx = 2.0 * jnp.pi / NX * (n.astype(F32) + sigma.astype(F32) / NY)
    ky = 2.0 * jnp.pi / NY * wave.astype(F32)
    size = jnp.sqrt(kx * kx + ky * ky)
    anchor = (wave == 0) & (n == 0)
    size = jnp.where(anchor, 1.0, size)
    single = (wave == 0) | (wave == NY // 2)
    scale = jnp.where(single, 1.0, 2.0) / (NX * NY)
    weights = jnp.where(anchor, 0.0, -jnp.exp(-thickness * size) / size) * scale
    return theta_cos, theta_sin, weights


def shards(density, xmomentum, ymomentum, shear_shift):
    t = {k: v for k, v in host_tables().items()}
    rho, mx, my = density[0], xmomentum[0], ymomentum[0]
    shift = shear_shift[0]
    fields = jnp.stack([rho, mx, my])
    low = fields[:, :, 0].T
    high = fields[:, :, COLS - 1].T
    up = [(j, (j + 1) % GY) for j in range(GY)]
    down = [((j + 1) % GY, j) for j in range(GY)]
    below = lax.ppermute(fields[:, ROWS - 1], "gy", up)
    above = lax.ppermute(fields[:, 0], "gy", down)
    left, right = ghosts(low, high, shift)
    block = (ROWS, COLS)
    rho_new, mx_new, my_new, packed = call(
        gas_kernel,
        [block, block, block, (COLS, 128)],
        rho,
        mx,
        my,
        left,
        right,
        below,
        above,
        name="gas",
    )
    lines = lax.all_to_all(packed, "gy", 0, 0, tiled=True)
    waves = call(
        forward_kernel,
        (256, 128),
        lines,
        *t["blocks"],
        t["twist_re"],
        t["twist_im"],
        *t["inner"],
        name="forward",
    )
    waves = lax.all_to_all(waves, ("gx", "gy"), 0, 0, tiled=True)
    theta_cos, theta_sin, weights = radial_tables(shift)
    flag = ((lax.axis_index("gx") == 0) & (lax.axis_index("gy") == 0)).astype(jnp.int32).reshape(1)
    solved = call(
        radial_kernel,
        (256, 128),
        flag,
        waves,
        theta_cos,
        theta_sin,
        weights,
        *t["groups"],
        t["radial_cos"],
        t["radial_sin"],
        *t["cells"],
        *t["cells_back"],
        name="radial",
        smem=1,
    )
    solved = lax.all_to_all(solved, ("gx", "gy"), 0, 0, tiled=True)
    lines = call(
        backward_kernel,
        (256, 128),
        solved,
        *t["inner_back"],
        t["back_cos"],
        t["back_sin"],
        *t["blocks_back"],
        name="backward",
    )
    lines = lax.all_to_all(lines, "gy", 0, 0, tiled=True)
    potential = call(last_kernel, block, lines, name="last")
    return rho_new[None], mx_new[None], my_new[None], potential[None]


def solution(mesh):
    spec = P(None, "gy", "gx")
    return jax.shard_map(
        shards,
        mesh=mesh,
        in_specs=(spec, spec, spec, P()),
        out_specs=(spec, spec, spec, spec),
        check_vma=False,
    )
```

```python
import functools

import jax
import jax.numpy as jnp
import ml_dtypes
import numpy as np
from jax import lax
from jax.experimental import pallas as pl
from jax.experimental.pallas import tpu as pltpu
from jax.sharding import PartitionSpec as P

NX = 2048
NY = 2048
ROWS = 64
COLS = 256
GX = 8
GY = 32

time_step = 0.15
omega_rate = 0.5
shear_rate = 1.5
thickness = 0.5

BF = jnp.bfloat16
F32 = jnp.float32


def halves(table):
    table = np.asarray(table, np.float32)
    head = table.astype(ml_dtypes.bfloat16)
    rest = (table - head.astype(np.float32)).astype(ml_dtypes.bfloat16)
    return head, rest


def turn(index, length):
    angle = 2.0 * np.pi * (np.asarray(index) % length) / length
    return np.cos(angle), np.sin(angle)


@functools.cache
def host_tables():
    out = {}
    eye8 = np.eye(8)
    cos32, sin32 = turn(np.outer(np.arange(32), np.arange(32)), 32)

    def spread(table):
        return np.einsum("jm,ab->ajmb", table, eye8).reshape(256, 256)

    out["blocks"] = halves(np.concatenate([spread(cos32), spread(-sin32)], 1))
    m1 = np.repeat(np.arange(32), 8)
    tc, ts = turn(np.outer(np.arange(64), m1), NY)
    out["twist_cos"] = tc.astype(np.float32)
    out["twist_sin"] = ts.astype(np.float32)
    c64, s64 = turn(np.outer(np.arange(32), np.arange(64)), 64)
    last = np.zeros((16, 128))
    last[0, :64] = 1.0 - 2.0 * (np.arange(64) % 2)
    out["inner"] = halves(
        np.concatenate([np.concatenate([c64, s64], 1), np.concatenate([-s64, c64], 1), last])
    )
    rows = np.arange(256)
    c256, s256 = turn(np.outer(rows, rows), 256)
    out["groups"] = halves(np.concatenate([c256, s256]))
    lane = np.arange(128)
    sign = np.where(lane < 64, 1.0, -1.0)
    tc, ts = turn(np.outer(rows, lane % 8), NX)
    out["radial_cos"] = tc.astype(np.float32)
    out["radial_sin"] = (ts * sign).astype(np.float32)
    c8, s8 = turn(np.outer(np.arange(8), np.arange(8)), 8)
    lines = np.eye(8)
    ck, sk = np.kron(lines, c8), np.kron(lines, s8)
    out["cells"] = halves(np.block([[ck, -sk], [sk, ck]]))
    out["cells_back"] = halves(np.block([[ck, sk], [-sk, ck]]))
    order = rows // 32 + 8 * (rows % 32)
    c256, s256 = turn(np.outer(rows, order), 256)
    out["groups_back"] = halves(np.concatenate([c256, s256]))
    tc, ts = turn(np.outer(order, lane % 8), NX)
    out["return_cos"] = tc.astype(np.float32)
    out["return_sin"] = (ts * sign).astype(np.float32)
    c64, s64 = turn(np.outer(np.arange(64), np.arange(32)), 64)
    out["inner_back"] = halves(np.concatenate([c64, s64]))
    pair = np.arange(512) // 128
    part = np.arange(512) % 128 // 64
    which = np.arange(512) % 64 // 8
    m1 = pair * 8 + which
    q = np.arange(512) % 8
    tc, ts = turn(np.outer(np.arange(64), m1), NY)
    out["back_cos"] = tc.astype(np.float32)
    out["back_sin"] = (ts * np.where(part == 0, 1.0, -1.0)).astype(np.float32)
    j = np.repeat(np.arange(32), 8)
    own = np.tile(np.arange(8), 32)
    c32, s32 = turn(np.outer(j, m1), 32)
    weight = np.where(part == 0, c32, -s32)
    weight = np.where((part == 1) & (m1 == 0), 1.0, weight)
    out["blocks_back"] = halves(weight * (own[:, None] == q[None, :]))
    return out


def split(value):
    head = value.astype(BF)
    rest = (value - head.astype(F32)).astype(BF)
    return head, rest


NN = (((1,), (0,)), ((), ()))
NT = (((1,), (1,)), ((), ()))


def product(table_head, table_rest, value, dims=NN):
    head, rest = split(value)
    dot = functools.partial(lax.dot_general, dimension_numbers=dims, preferred_element_type=F32)
    return dot(table_head, head) + (dot(table_head, rest) + dot(table_rest, head))


def product_right(value, table_head, table_rest):
    head, rest = split(value)
    dot = functools.partial(lax.dot_general, dimension_numbers=NN, preferred_element_type=F32)
    return dot(head, table_head) + (dot(rest, table_head) + dot(head, table_rest))


def roll(value, shift, axis):
    return pltpu.roll(value, shift % value.shape[axis], axis)


def lanes_of(shape):
    return lax.broadcasted_iota(jnp.int32, shape, 1)


def rows_of(shape):
    return lax.broadcasted_iota(jnp.int32, shape, 0)


def interface(left, right, normal, parts=3):
    speed = jnp.maximum(jnp.abs(left[3]), jnp.abs(right[3])) + 1.0
    fluxes = []
    for part in range(parts):
        f_left = left[part] * left[3]
        f_right = right[part] * right[3]
        if part == normal:
            f_left = f_left + left[0]
            f_right = f_right + right[0]
        fluxes.append(0.5 * (f_left + f_right) - 0.5 * speed * (right[part] - left[part]))
    return fluxes


def with_speed(fields, normal):
    return (*fields, fields[normal] / fields[0])


def inner_fluxes(state, parts):
    lane = lanes_of((ROWS, COLS))
    row = rows_of((ROWS, COLS))
    mid = with_speed(state, 1)
    west = interface([roll(v, 1, 1) for v in mid], mid, 1, parts)
    mid = with_speed(state, 2)
    south = interface([roll(v, 1, 0) for v in mid], mid, 2, parts)
    return [jnp.where(lane == 0, 0.0, v) for v in west], [jnp.where(row == 0, 0.0, v) for v in south]


def pack_kernel(scalars, rho, mx, my, out):
    state = (rho[...], mx[...], my[...])
    (west,), (south,) = inner_fluxes(state, 1)
    change = roll(west, -1, 1) - west + roll(south, -1, 0) - south
    partial = state[0] - time_step * change
    row = rows_of((8, COLS))
    edges = jnp.zeros((8, COLS), F32)
    for f in range(3):
        edges = jnp.where(row == f, state[f][0:1, :], edges)
        edges = jnp.where(row == 3 + f, state[f][ROWS - 1 : ROWS, :], edges)
    tall = jnp.concatenate([partial, edges, jnp.zeros((56, COLS), F32)], 0).T
    lane = lanes_of((ROWS, 128))
    low = jnp.zeros((ROWS, 128), F32)
    high = jnp.zeros((ROWS, 128), F32)
    for f in range(3):
        low = jnp.where(lane == 72 + f, state[f][:, 0:1], low)
        high = jnp.where(lane == 75 + f, state[f][:, COLS - 1 : COLS], high)
    out[0:ROWS, :] = tall[0:ROWS] + low + pltpu.roll(high, scalars[0], 0)
    out[ROWS:, :] = tall[ROWS:]


def finish_kernel(scalars, rho, mx, my, arrived, rho_out, mx_out, my_out):
    state = (rho[...], mx[...], my[...])
    lane = lanes_of((ROWS, COLS))
    row = rows_of((ROWS, COLS))
    west, south = inner_fluxes(state, 3)
    across = arrived[...].T[32:40]
    beside = arrived[0:ROWS, :]
    beside_high = pltpu.roll(beside, scalars[1], 0)
    new = []
    for f in range(3):
        east = jnp.where(lane == COLS - 1, beside_high[:, 41 + f : 42 + f], roll(west[f], -1, 1))
        north = jnp.where(row == ROWS - 1, across[3 + f : 4 + f, :], roll(south[f], -1, 0))
        west_f = jnp.where(lane == 0, beside[:, 38 + f : 39 + f], west[f])
        south_f = jnp.where(row == 0, across[f : f + 1, :], south[f])
        new.append(state[f] - time_step * (east - west_f + north - south_f))
    rho_out[...] = new[0]
    mx_out[...] = new[1] + time_step * 2.0 * omega_rate * state[2]
    my_out[...] = new[2] - time_step * (2.0 - shear_rate) * omega_rate * state[1]


def forward_kernel(
    scalars, arrived, blocks_h, blocks_l, twist_cos, twist_sin, inner_h, inner_l, out, ride
):
    row = scalars[4]
    narrow = lanes_of((32, 128))
    last = arrived[224:256, :]
    wrapped = pltpu.roll(last, scalars[2], 0)
    last = jnp.where((narrow >= 75) & (narrow < 78), wrapped, last)
    tall = jnp.concatenate([arrived[0:224, :], last], 0).T
    lane = lanes_of((8, 256))
    upper = tall[64:72]
    before = jnp.where(lane % 32 == 0, roll(upper, -31, 1), roll(upper, 1, 1))
    south = interface(
        with_speed([before[3 + f : 4 + f] for f in range(3)], 2),
        with_speed([upper[f : f + 1] for f in range(3)], 2),
        2,
    )
    valid = jnp.zeros((1, 256), jnp.int32) + row >= 0
    side = tall[72:80]
    before = roll(side, 32, 1)
    left = [before[3 + f : 4 + f] for f in range(3)]
    right = [side[f : f + 1] for f in range(3)]
    left[0] = jnp.where(valid, left[0], 1.0)
    right[0] = jnp.where(valid, right[0], 1.0)
    west = interface(with_speed(left, 1), with_speed(right, 1), 1)
    west = [jnp.where(valid, v, 0.0) for v in west]
    line = lanes_of((1, 256))
    north = [jnp.where(line % 32 == 31, roll(v, 31, 1), roll(v, -1, 1)) for v in south]
    east = [roll(v, -32, 1) for v in west]
    rows8 = rows_of((8, 256))
    rows16 = rows_of((16, 256))
    rows64 = rows_of((64, 256))
    fluxes = jnp.zeros((16, 256), F32)
    for at, value in enumerate(south + north + west + east):
        fluxes = jnp.where(rows16 == at, value, fluxes)
    back = jnp.concatenate([jnp.zeros((32, 256), F32), fluxes, jnp.zeros((80, 256), F32)], 0).T
    last = back[224:256]
    wrapped = pltpu.roll(last, scalars[3], 0)
    ride[0:224, :] = back[0:224]
    ride[224:256, :] = jnp.where((narrow >= 41) & (narrow < 44), wrapped, last)
    density = tall[0:64]
    density = density + jnp.where(rows64 == 0, time_step * south[0], 0.0)
    density = density - jnp.where(rows64 == 63, time_step * north[0], 0.0)
    edge = jnp.where(rows8 == 0, time_step * west[0], 0.0)
    first = product_right(jnp.concatenate([density, edge], 0), blocks_h[...], blocks_l[...])
    tc = twist_cos[...]
    ts = twist_sin[...]
    re, im = first[:64, :256], first[:64, 256:]
    main = jnp.concatenate([re * tc + im * ts, im * tc - re * ts], 0)
    re, im = first[64:65, :256], first[64:65, 256:]
    here = rows64 == row
    edge = jnp.concatenate(
        [jnp.where(here, re * tc + im * ts, 0.0), jnp.where(here, im * tc - re * ts, 0.0)], 0
    )
    waves = product(inner_h[...], inner_l[...], jnp.concatenate([main, edge], 1))
    rows32 = rows_of((32, 128))
    for g in range(8):
        place = 32 * (g % 4)
        pieces = []
        for start in (0, 256):
            tile = slice(start + g // 4 * 128, start + g // 4 * 128 + 128)
            real = waves[0:32, tile]
            imag = waves[32:64, tile]
            if g == 0:
                imag = jnp.where((rows32 == 0) & (narrow < 8), waves[64:65, tile], imag)
            pieces.append((real, imag))
        both = roll(pieces[1][1], 96 - place, 1)
        both = jnp.where(narrow < 96, roll(pieces[0][1], 64 - place, 1), both)
        both = jnp.where(narrow < 64, roll(pieces[1][0], 32 - place, 1), both)
        both = jnp.where(narrow < 32, roll(pieces[0][0], -place, 1), both)
        out[g * 32 : (g + 1) * 32, :] = both


def radial_kernel(
    scalars,
    arrived,
    ride,
    theta_cos,
    theta_sin,
    theta_cos_back,
    theta_sin_back,
    weights,
    wrap_cos,
    wrap_sin,
    groups_h,
    groups_l,
    radial_cos,
    radial_sin,
    cells_h,
    cells_l,
    cells_back_h,
    cells_back_l,
    groups_back_h,
    groups_back_l,
    return_cos,
    return_sin,
    out,
):
    shape = (256, 128)
    half = functools.partial(roll, shift=64, axis=1)

    def apart(value):
        lane = lanes_of(value.shape)
        first = jnp.zeros(value.shape, jnp.int32) + scalars[5] == 1
        value = jnp.where(lane % 64 < 32, value, 0.0)
        fifth = roll(value, -32, 1)
        slot = (lane >= 64) & (lane < 72) & first
        return jnp.where((lane >= 32) & (lane < 40), fifth, jnp.where(slot, 0.0, value))

    lane = lanes_of(shape)
    row = rows_of(shape)
    sign = jnp.where(lane < 64, 1.0, -1.0)
    value = arrived[...]
    edge = jnp.sum(value[0:ROWS], axis=0, keepdims=True)
    edge = apart(roll(jnp.broadcast_to(edge, (8, 128)), -32, 1))
    lane8 = lanes_of((8, 128))
    beside = jnp.where(lane8 % 8 == 7, roll(edge, 7, 1), roll(edge, -1, 1))
    beside = beside * wrap_cos[...] + half(beside) * wrap_sin[...]
    value = apart(value)
    value = value + jnp.where(row == 0, edge[0:1], 0.0) - jnp.where(row == 255, beside[0:1], 0.0)
    value = value * theta_cos[...] + half(value) * theta_sin[...]
    value = product_right(value, cells_h[...], cells_l[...])
    value = value * radial_cos[...] + half(value) * radial_sin[...]
    both = product(groups_h[...], groups_l[...], value)
    value = both[:256] + sign * half(both[256:])
    value = value * weights[...]
    blocks = [value[32 * k : 32 * k + 32] for k in range(8)]
    narrow = lanes_of((32, 128))
    for bit in (1, 2, 4):
        swapped = list(blocks)
        for k in range(8):
            if k & bit == 0:
                a, b = blocks[k], blocks[k + bit]
                low = narrow & bit == 0
                swapped[k] = jnp.where(low, a, roll(b, bit, 1))
                swapped[k + bit] = jnp.where(low, roll(a, -bit, 1), b)
        blocks = swapped
    value = jnp.concatenate(blocks, 0)
    value = product_right(value, cells_back_h[...], cells_back_l[...])
    value = value * return_cos[...] - half(value) * return_sin[...]
    both = product(groups_back_h[...], groups_back_l[...], value)
    value = both[:256] - sign * half(both[256:])
    value = value * theta_cos_back[...] - half(value) * theta_sin_back[...]
    first = jnp.zeros(shape, jnp.int32) + scalars[5] == 1
    value = jnp.where((lane >= 64) & (lane < 72) & first, roll(value, 32, 1), value)
    out[...] = jnp.where((lane >= 32) & (lane < 44), ride[...], value)


def backward_kernel(arrived, inner_h, inner_l, back_cos, back_sin, blocks_h, blocks_l, out):
    lane = lanes_of((32, 128))
    low = lane % 64 < 32
    pairs = []
    for h in range(4):
        even = arrived[64 * h : 64 * h + 32, :]
        odd = arrived[64 * h + 32 : 64 * h + 64, :]
        pairs.append(jnp.where(low, even, roll(odd, 32, 1)))
    value = jnp.concatenate(pairs, 1)
    both = product(inner_h[...], inner_l[...], value)
    wide = lanes_of((64, 128))
    row = rows_of((64, 128))
    sign = jnp.where(wide < 64, 1.0, -1.0)
    parity = jnp.where(row % 2 == 0, 1.0, -1.0)
    turned = []
    for h in range(4):
        tile = slice(128 * h, 128 * h + 128)
        part = both[:64, tile] - sign * roll(both[64:, tile], 64, 1)
        part = part * back_cos[:, tile] - roll(part, 64, 1) * back_sin[:, tile]
        if h == 0:
            part = jnp.where((wide >= 64) & (wide < 72), parity * pairs[0][0:1, :], part)
        turned.append(part)
    turned = jnp.concatenate(turned, 1)
    turned = jnp.concatenate([turned, turned], 0)
    out[...] = product(blocks_h[...], blocks_l[...], turned, NT)


def last_kernel(arrived, out):
    out[...] = arrived[...].T[:ROWS]


VMEM = pl.BlockSpec(memory_space=pltpu.VMEM)
SMEM = pl.BlockSpec(memory_space=pltpu.SMEM)


def call(kernel, shapes, *args, name, smem=0):
    many = isinstance(shapes, list)
    outs = [jax.ShapeDtypeStruct(s, F32) for s in (shapes if many else [shapes])]
    return pl.pallas_call(
        kernel,
        out_shape=outs if many else outs[0],
        in_specs=[SMEM] * smem + [VMEM] * (len(args) - smem),
        out_specs=[VMEM] * len(outs) if many else VMEM,
        name=name,
        compiler_params=pltpu.CompilerParams(vmem_limit_bytes=32 * 1024 * 1024),
        cost_estimate=pl.CostEstimate(flops=100_000_000, bytes_accessed=1_000_000, transcendentals=0),
    )(*args)


def radial_tables(shift):
    shape = (256, 128)
    row = lax.broadcasted_iota(jnp.int32, shape, 0)
    lane = lax.broadcasted_iota(jnp.int32, shape, 1)
    line = lane % 64 // 8
    inside = lane % 8
    wave = lax.axis_index("gx") * 4 + line + GY * lax.axis_index("gy")
    wave = jnp.where(line < 4, wave, NY // 2)
    sigma = wave * shift % NY
    sign = jnp.where(lane < 64, 1.0, -1.0)

    def phase(cell):
        angle = (sigma * cell % (NX * NY)).astype(F32) * (2.0 * jnp.pi / (NX * NY))
        return jnp.cos(angle), jnp.sin(angle) * sign

    there = phase(row + COLS * inside)
    back = phase(row * 8 + inside)
    n = inside + 8 * row
    n = jnp.where(n < NX // 2, n, n - NX)
    kx = 2.0 * jnp.pi / NX * (n.astype(F32) + sigma.astype(F32) / NY)
    ky = 2.0 * jnp.pi / NY * wave.astype(F32)
    size = jnp.sqrt(kx * kx + ky * ky)
    anchor = (wave == 0) & (n == 0)
    size = jnp.where(anchor, 1.0, size)
    single = (wave == 0) | (wave == NY // 2)
    scale = jnp.where(single, 1.0, 2.0) / (NX * NY)
    weights = jnp.where(anchor, 0.0, -jnp.exp(-thickness * size) / size) * scale
    angle = sigma[:8].astype(F32) * (2.0 * jnp.pi / NY)
    last = inside[:8] == 7
    wrap_cos = jnp.where(last, jnp.cos(angle), 1.0)
    wrap_sin = jnp.where(last, jnp.sin(angle) * sign[:8], 0.0)
    return *there, *back, weights, wrap_cos, wrap_sin


def shards(density, xmomentum, ymomentum, shear_shift):
    t = host_tables()
    rho, mx, my = density[0], xmomentum[0], ymomentum[0]
    shift = shear_shift[0]
    radial = lax.axis_index("gx")
    flat = radial * GY + lax.axis_index("gy")
    off = shift % ROWS
    wrap_off = jnp.where(radial == GX - 1, off, 0)
    hop = (shift // ROWS + (flat % ROWS + off) // ROWS) % GY
    scalars = jnp.stack(
        [
            (ROWS - wrap_off) % ROWS,
            wrap_off,
            (GY - hop) % GY,
            hop,
            jnp.where(flat < ROWS, flat, -1),
            (flat == 0).astype(jnp.int32),
        ]
    ).astype(jnp.int32)
    everyone = ("gx", "gy")
    block = (ROWS, COLS)
    table = (256, 128)
    columns = call(pack_kernel, table, scalars, rho, mx, my, name="pack", smem=1)
    columns = lax.all_to_all(columns, everyone, 0, 0, tiled=True)
    waves, ride = call(
        forward_kernel,
        [table, table],
        scalars,
        columns,
        *t["blocks"],
        t["twist_cos"],
        t["twist_sin"],
        *t["inner"],
        name="forward",
        smem=1,
    )
    waves = lax.all_to_all(waves, everyone, 0, 0, tiled=True)
    solved = call(
        radial_kernel,
        table,
        scalars,
        waves,
        ride,
        *radial_tables(shift),
        *t["groups"],
        t["radial_cos"],
        t["radial_sin"],
        *t["cells"],
        *t["cells_back"],
        *t["groups_back"],
        t["return_cos"],
        t["return_sin"],
        name="radial",
        smem=1,
    )
    solved = lax.all_to_all(solved, everyone, 0, 0, tiled=True)
    lines = call(
        backward_kernel,
        table,
        solved,
        *t["inner_back"],
        t["back_cos"],
        t["back_sin"],
        *t["blocks_back"],
        name="backward",
    )
    lines = lax.all_to_all(lines, "gy", 0, 0, tiled=True)
    rho_new, mx_new, my_new = call(
        finish_kernel, [block, block, block], scalars, rho, mx, my, solved, name="finish", smem=1
    )
    potential = call(last_kernel, block, lines, name="last")
    return rho_new[None], mx_new[None], my_new[None], potential[None]


def solution(mesh):
    spec = P(None, "gy", "gx")
    return jax.shard_map(
        shards,
        mesh=mesh,
        in_specs=(spec, spec, spec, P()),
        out_specs=(spec, spec, spec, spec),
        check_vma=False,
    )
```

```python
import functools

import jax
import jax.numpy as jnp
import ml_dtypes
import numpy as np
from jax import lax
from jax.experimental import pallas as pl
from jax.experimental.pallas import tpu as pltpu
from jax.sharding import PartitionSpec as P

NX = 2048
NY = 2048
ROWS = 64
COLS = 256
GX = 8
GY = 32

time_step = 0.15
omega_rate = 0.5
shear_rate = 1.5
thickness = 0.5

BF = jnp.bfloat16
F32 = jnp.float32


def halves(table):
    table = np.asarray(table, np.float32)
    head = table.astype(ml_dtypes.bfloat16)
    rest = (table - head.astype(np.float32)).astype(ml_dtypes.bfloat16)
    return head, rest


def both_parts(table):
    head, rest = halves(table)
    return np.block([[head, rest], [head, np.zeros_like(rest)]])


def turn(index, length):
    angle = 2.0 * np.pi * (np.asarray(index) % length) / length
    return np.cos(angle), np.sin(angle)


@functools.cache
def host_tables():
    out = {}
    eye8 = np.eye(8)
    cos32, sin32 = turn(np.outer(np.arange(32), np.arange(32)), 32)

    def spread(table):
        return np.einsum("jm,ab->ajmb", table, eye8).reshape(256, 256)

    out["blocks"] = halves(np.concatenate([spread(cos32), spread(-sin32)], 1))
    m1 = np.repeat(np.arange(32), 8)
    tc, ts = turn(np.outer(np.arange(64), m1), NY)
    out["twist_cos"] = tc.astype(np.float32)
    out["twist_sin"] = ts.astype(np.float32)
    c64, s64 = turn(np.outer(np.arange(32), np.arange(64)), 64)
    last = np.zeros((16, 128))
    last[0, :64] = 1.0 - 2.0 * (np.arange(64) % 2)
    head, rest = halves(
        np.concatenate([np.concatenate([c64, s64], 1), np.concatenate([-s64, c64], 1), last])
    )
    out["inner"] = np.concatenate([head, head], 1), rest
    rows = np.arange(256)
    c256, s256 = turn(np.outer(rows, rows), 256)
    out["groups"] = halves(np.concatenate([c256, s256]))
    lane = np.arange(128)
    sign = np.where(lane < 64, 1.0, -1.0)
    tc, ts = turn(np.outer(rows, lane % 8), NX)
    out["radial_cos"] = tc.astype(np.float32)
    out["radial_sin"] = (ts * sign).astype(np.float32)
    c8, s8 = turn(np.outer(np.arange(8), np.arange(8)), 8)
    lines = np.eye(8)
    ck, sk = np.kron(lines, c8), np.kron(lines, s8)
    out["cells"] = both_parts(np.block([[ck, -sk], [sk, ck]]))
    out["cells_back"] = both_parts(np.block([[ck, sk], [-sk, ck]]))
    order = rows // 128 * 128 + rows // 32 % 4 + 4 * (rows % 32)
    c256, s256 = turn(np.outer(order, rows), 256)
    out["groups_back"] = halves(np.concatenate([c256, s256]))
    tc, ts = turn(np.outer(order, lane % 8), NX)
    out["return_cos"] = tc.astype(np.float32)
    out["return_sin"] = (ts * sign).astype(np.float32)
    c64, s64 = turn(np.outer(np.arange(64), np.arange(32)), 64)
    head, rest = halves(np.concatenate([c64, s64]))
    out["inner_back"] = np.concatenate([head, head, rest], 1)
    pair = np.arange(512) // 128
    part = np.arange(512) % 128 // 64
    which = np.arange(512) % 64 // 8
    m1 = pair * 8 + which
    q = np.arange(512) % 8
    tc, ts = turn(np.outer(np.arange(64), m1), NY)
    out["back_cos"] = tc.astype(np.float32)
    out["back_sin"] = (ts * np.where(part == 0, 1.0, -1.0)).astype(np.float32)
    j = np.tile(np.repeat(np.arange(32), 4), 2)
    own = np.repeat([0, 4], 128) + np.tile(np.arange(4), 64)
    c32, s32 = turn(np.outer(j, m1), 32)
    weight = np.where(part == 0, c32, -s32)
    weight = np.where((part == 1) & (m1 == 0), 1.0, weight)
    out["blocks_back"] = halves(weight * (own[:, None] == q[None, :]))
    return out


def split(value):
    head = value.astype(BF)
    rest = (value - head.astype(F32)).astype(BF)
    return head, rest


NN = (((1,), (0,)), ((), ()))
NT = (((1,), (1,)), ((), ()))


def dot(left, right, dims=NN):
    return lax.dot_general(left, right, dims, preferred_element_type=F32)


def product_rows(table_head, table_rest, value):
    head, rest = split(value)
    both = dot(table_head, jnp.concatenate([head, rest], 1))
    return both[:, :128] + both[:, 128:] + dot(table_rest, head)


def product_lanes(value, table):
    both = dot(jnp.concatenate(split(value), 1), table)
    return both[:, :128] + both[:, 128:]


def product_right(value, table_head, table_rest):
    head, rest = split(value)
    return dot(head, table_head) + (dot(rest, table_head) + dot(head, table_rest))


def roll(value, shift, axis):
    return pltpu.roll(value, shift % value.shape[axis], axis)


def lanes_of(shape):
    return lax.broadcasted_iota(jnp.int32, shape, 1)


def rows_of(shape):
    return lax.broadcasted_iota(jnp.int32, shape, 0)


def interface(left, right, normal, parts=3):
    speed = jnp.maximum(jnp.abs(left[3]), jnp.abs(right[3])) + 1.0
    fluxes = []
    for part in range(parts):
        f_left = left[part] * left[3]
        f_right = right[part] * right[3]
        if part == normal:
            f_left = f_left + left[0]
            f_right = f_right + right[0]
        fluxes.append(0.5 * (f_left + f_right) - 0.5 * speed * (right[part] - left[part]))
    return fluxes


def with_speed(fields, normal):
    return (*fields, fields[normal] / fields[0])


def inner_fluxes(state, parts):
    lane = lanes_of((ROWS, COLS))
    row = rows_of((ROWS, COLS))
    mid = with_speed(state, 1)
    west = interface([roll(v, 1, 1) for v in mid], mid, 1, parts)
    mid = with_speed(state, 2)
    south = interface([roll(v, 1, 0) for v in mid], mid, 2, parts)
    return [jnp.where(lane == 0, 0.0, v) for v in west], [jnp.where(row == 0, 0.0, v) for v in south]


def pack_kernel(place, shift, rho, mx, my, out, held, shift_held, ready):
    copies = [
        pltpu.make_async_copy(source, held.at[f], ready.at[f])
        for f, source in enumerate((rho, mx, my))
    ]
    copies.append(pltpu.make_async_copy(shift, shift_held, ready.at[3]))
    for copy in copies:
        copy.start()
    for copy in copies:
        copy.wait()
    state = (held[0], held[1], held[2])
    (west,), (south,) = inner_fluxes(state, 1)
    change = roll(west, -1, 1) - west + roll(south, -1, 0) - south
    partial = state[0] - time_step * change
    row = rows_of((8, COLS))
    edges = jnp.zeros((8, COLS), F32)
    for f in range(3):
        edges = jnp.where(row == f, state[f][0:1, :], edges)
        edges = jnp.where(row == 3 + f, state[f][ROWS - 1 : ROWS, :], edges)
    tall = jnp.concatenate([partial, edges, jnp.zeros((56, COLS), F32)], 0).T
    lane = lanes_of((ROWS, 128))
    low = jnp.zeros((ROWS, 128), F32)
    high = jnp.zeros((ROWS, 128), F32)
    for f in range(3):
        low = jnp.where(lane == 72 + f, state[f][:, 0:1], low)
        high = jnp.where(lane == 75 + f, state[f][:, COLS - 1 : COLS], high)
    slide = jnp.where(place[0] == GX - 1, (ROWS - (shift_held[0] & (ROWS - 1))) & (ROWS - 1), 0)
    out[0:ROWS, :] = tall[0:ROWS] + low + pltpu.roll(high, slide, 0)
    out[ROWS:, :] = tall[ROWS:]


def finish_kernel(scalars, rho, mx, my, arrived, rho_out, mx_out, my_out):
    state = (rho[...], mx[...], my[...])
    lane = lanes_of((ROWS, COLS))
    row = rows_of((ROWS, COLS))
    west, south = inner_fluxes(state, 3)
    across = arrived[...].T[32:40]
    beside = arrived[0:ROWS, :]
    beside_high = pltpu.roll(beside, scalars[1], 0)
    new = []
    for f in range(3):
        east = jnp.where(lane == COLS - 1, beside_high[:, 41 + f : 42 + f], roll(west[f], -1, 1))
        north = jnp.where(row == ROWS - 1, across[3 + f : 4 + f, :], roll(south[f], -1, 0))
        west_f = jnp.where(lane == 0, beside[:, 38 + f : 39 + f], west[f])
        south_f = jnp.where(row == 0, across[f : f + 1, :], south[f])
        new.append(state[f] - time_step * (east - west_f + north - south_f))
    rho_out[...] = new[0]
    mx_out[...] = new[1] + time_step * 2.0 * omega_rate * state[2]
    my_out[...] = new[2] - time_step * (2.0 - shear_rate) * omega_rate * state[1]


def edge_fluxes(scalars, arrived, parts):
    row = scalars[4]
    narrow = lanes_of((32, 128))
    last = arrived[224:256, :]
    wrapped = pltpu.roll(last, scalars[2], 0)
    last = jnp.where((narrow >= 75) & (narrow < 78), wrapped, last)
    tall = jnp.concatenate([arrived[0:224, :], last], 0).T
    lane = lanes_of((8, 256))
    upper = tall[64:72]
    before = jnp.where(lane % 32 == 0, roll(upper, -31, 1), roll(upper, 1, 1))
    south = interface(
        with_speed([before[3 + f : 4 + f] for f in range(3)], 2),
        with_speed([upper[f : f + 1] for f in range(3)], 2),
        2,
        parts,
    )
    valid = jnp.zeros((1, 256), jnp.int32) + row >= 0
    side = tall[72:80]
    before = roll(side, 32, 1)
    left = [before[3 + f : 4 + f] for f in range(3)]
    right = [side[f : f + 1] for f in range(3)]
    left[0] = jnp.where(valid, left[0], 1.0)
    right[0] = jnp.where(valid, right[0], 1.0)
    west = interface(with_speed(left, 1), with_speed(right, 1), 1, parts)
    west = [jnp.where(valid, v, 0.0) for v in west]
    line = lanes_of((1, 256))
    north = [jnp.where(line % 32 == 31, roll(v, 31, 1), roll(v, -1, 1)) for v in south]
    return tall, west, south, north


def edges_kernel(scalars, arrived, ride):
    _, west, south, north = edge_fluxes(scalars, arrived, 3)
    east = [roll(v, -32, 1) for v in west]
    narrow = lanes_of((32, 128))
    rows16 = rows_of((16, 256))
    fluxes = jnp.zeros((16, 256), F32)
    for at, value in enumerate(south + north + west + east):
        fluxes = jnp.where(rows16 == at, value, fluxes)
    back = jnp.concatenate([jnp.zeros((32, 256), F32), fluxes, jnp.zeros((80, 256), F32)], 0).T
    last = back[224:256]
    wrapped = pltpu.roll(last, scalars[3], 0)
    ride[0:224, :] = back[0:224]
    ride[224:256, :] = jnp.where((narrow >= 41) & (narrow < 44), wrapped, last)


def forward_kernel(scalars, arrived, blocks_h, blocks_l, twist_cos, twist_sin, inner_h, inner_l, out):
    tall, west, south, north = edge_fluxes(scalars, arrived, 1)
    narrow = lanes_of((32, 128))
    rows8 = rows_of((8, 256))
    rows64 = rows_of((64, 256))
    density = tall[0:64]
    density = density + jnp.where(rows64 == 0, time_step * south[0], 0.0)
    density = density - jnp.where(rows64 == 63, time_step * north[0], 0.0)
    edge = jnp.where(rows8 == 0, time_step * west[0], 0.0)
    first = product_right(jnp.concatenate([density, edge], 0), blocks_h[...], blocks_l[...])
    tc = twist_cos[...]
    ts = twist_sin[...]
    re, im = first[:64, :256], first[:64, 256:]
    main = jnp.concatenate([re * tc + im * ts, im * tc - re * ts], 0)
    re, im = first[64:65, :256], first[64:65, 256:]
    here = rows64 == scalars[4]
    edge = jnp.concatenate(
        [jnp.where(here, re * tc + im * ts, 0.0), jnp.where(here, im * tc - re * ts, 0.0)], 0
    )
    head, rest = split(jnp.concatenate([main, edge], 1))
    waves = dot(inner_h[...], jnp.concatenate([head, rest], 0)) + dot(inner_l[...], head)
    rows32 = rows_of((32, 128))
    for g in range(8):
        place = 32 * (g % 4)
        pieces = []
        for start in (0, 256):
            tile = slice(start + g // 4 * 128, start + g // 4 * 128 + 128)
            real = waves[0:32, tile]
            imag = waves[32:64, tile]
            if g == 0:
                imag = jnp.where((rows32 == 0) & (narrow < 8), waves[64:65, tile], imag)
            pieces.append((real, imag))
        both = roll(pieces[1][1], 96 - place, 1)
        both = jnp.where(narrow < 96, roll(pieces[0][1], 64 - place, 1), both)
        both = jnp.where(narrow < 64, roll(pieces[1][0], 32 - place, 1), both)
        both = jnp.where(narrow < 32, roll(pieces[0][0], -place, 1), both)
        out[g * 32 : (g + 1) * 32, :] = both


def radial_kernel(
    scalars,
    arrived,
    ride,
    theta_cos,
    theta_sin,
    theta_cos_back,
    theta_sin_back,
    weights,
    wrap_cos,
    wrap_sin,
    groups_h,
    groups_l,
    radial_cos,
    radial_sin,
    cells,
    cells_back,
    groups_back_h,
    groups_back_l,
    return_cos,
    return_sin,
    out,
):
    shape = (256, 128)
    half = functools.partial(roll, shift=64, axis=1)

    def apart(value):
        lane = lanes_of(value.shape)
        first = jnp.zeros(value.shape, jnp.int32) + scalars[5] == 1
        value = jnp.where(lane % 64 < 32, value, 0.0)
        fifth = roll(value, -32, 1)
        slot = (lane >= 64) & (lane < 72) & first
        return jnp.where((lane >= 32) & (lane < 40), fifth, jnp.where(slot, 0.0, value))

    lane = lanes_of(shape)
    row = rows_of(shape)
    sign = jnp.where(lane < 64, 1.0, -1.0)
    value = arrived[...]
    edge = jnp.sum(value[0:ROWS], axis=0, keepdims=True)
    edge = apart(roll(jnp.broadcast_to(edge, (8, 128)), -32, 1))
    lane8 = lanes_of((8, 128))
    beside = jnp.where(lane8 % 8 == 7, roll(edge, 7, 1), roll(edge, -1, 1))
    beside = beside * wrap_cos[...] + half(beside) * wrap_sin[...]
    value = apart(value)
    value = value + jnp.where(row == 0, edge[0:1], 0.0) - jnp.where(row == 255, beside[0:1], 0.0)
    value = value * theta_cos[...] + half(value) * theta_sin[...]
    value = product_lanes(value, cells[...])
    value = value * radial_cos[...] + half(value) * radial_sin[...]
    both = product_rows(groups_h[...], groups_l[...], value)
    value = both[:256] + sign * half(both[256:])
    value = value * weights[...]
    both = product_rows(groups_back_h[...], groups_back_l[...], value)
    value = both[:256] - sign * half(both[256:])
    value = value * return_cos[...] - half(value) * return_sin[...]
    value = product_lanes(value, cells_back[...])
    value = value * theta_cos_back[...] - half(value) * theta_sin_back[...]
    first = jnp.zeros(shape, jnp.int32) + scalars[5] == 1
    value = jnp.where((lane >= 64) & (lane < 72) & first, roll(value, 32, 1), value)
    blocks = [value[32 * k : 32 * k + 32] for k in range(8)]
    narrow = lanes_of((32, 128))
    for bit in (1, 2, 4):
        swapped = list(blocks)
        for k in range(8):
            if k & bit == 0:
                a, b = blocks[k], blocks[k + bit]
                low = narrow & bit == 0
                swapped[k] = jnp.where(low, a, roll(b, bit, 1))
                swapped[k + bit] = jnp.where(low, roll(a, -bit, 1), b)
        blocks = swapped
    value = jnp.concatenate(blocks, 0)
    out[...] = jnp.where((lane >= 32) & (lane < 44), ride[...], value)


def backward_kernel(arrived, inner, back_cos, back_sin, blocks_h, blocks_l, out):
    lane = lanes_of((32, 128))
    low = lane % 64 < 32
    pairs = []
    for h in range(4):
        even = arrived[64 * h : 64 * h + 32, :]
        odd = arrived[64 * h + 32 : 64 * h + 64, :]
        pairs.append(jnp.where(low, even, roll(odd, 32, 1)))
    value = jnp.concatenate(pairs, 1)
    head, rest = split(value)
    both = dot(inner[...], jnp.concatenate([head, rest, head], 0))
    wide = lanes_of((64, 128))
    row = rows_of((64, 128))
    sign = jnp.where(wide < 64, 1.0, -1.0)
    parity = jnp.where(row % 2 == 0, 1.0, -1.0)
    turned = []
    for h in range(4):
        tile = slice(128 * h, 128 * h + 128)
        part = both[:64, tile] - sign * roll(both[64:, tile], 64, 1)
        part = part * back_cos[:, tile] - roll(part, 64, 1) * back_sin[:, tile]
        if h == 0:
            part = jnp.where((wide >= 64) & (wide < 72), parity * pairs[0][0:1, :], part)
        turned.append(part)
    head, rest = split(jnp.concatenate(turned, 1))
    full = dot(blocks_h[...], jnp.concatenate([head, rest], 0), NT)
    full = full + roll(full, 64, 1)
    full = full + dot(blocks_l[...], jnp.concatenate([head, head], 0), NT)
    square = lanes_of((128, 128))
    out[...] = jnp.where(square < 64, full[:128], full[128:])


def last_kernel(arrived, out):
    tall = arrived[...].T
    out[:, :128] = tall[:ROWS]
    out[:, 128:] = tall[ROWS:]


VMEM = pl.BlockSpec(memory_space=pltpu.VMEM)
SMEM = pl.BlockSpec(memory_space=pltpu.SMEM)
HBM = pl.BlockSpec(memory_space=pltpu.HBM)


def call(kernel, shapes, *args, name, smem=0, hbm=0, scratch=(), room=32):
    many = isinstance(shapes, list)
    outs = [jax.ShapeDtypeStruct(s, F32) for s in (shapes if many else [shapes])]
    return pl.pallas_call(
        kernel,
        out_shape=outs if many else outs[0],
        in_specs=[SMEM] * smem + [HBM] * hbm + [VMEM] * (len(args) - smem - hbm),
        out_specs=[VMEM] * len(outs) if many else VMEM,
        scratch_shapes=scratch,
        name=name,
        compiler_params=pltpu.CompilerParams(vmem_limit_bytes=room * 1024 * 1024),
        cost_estimate=pl.CostEstimate(flops=100_000_000, bytes_accessed=1_000_000, transcendentals=0),
    )(*args)


def radial_tables(shift):
    shape = (256, 128)
    row = lax.broadcasted_iota(jnp.int32, shape, 0)
    lane = lax.broadcasted_iota(jnp.int32, shape, 1)
    line = lane % 64 // 8
    inside = lane % 8
    wave = lax.axis_index("gx") * 4 + line + GY * lax.axis_index("gy")
    wave = jnp.where(line < 4, wave, NY // 2)
    sigma = wave * shift % NY
    sign = jnp.where(lane < 64, 1.0, -1.0)

    def phase(cell):
        angle = (sigma * cell % (NX * NY)).astype(F32) * (2.0 * jnp.pi / (NX * NY))
        return jnp.cos(angle), jnp.sin(angle) * sign

    there = phase(row + COLS * inside)
    back = phase(row // 128 * 128 + row // 32 % 4 + 4 * (row % 32) + COLS * inside)
    n = inside + 8 * row
    n = jnp.where(n < NX // 2, n, n - NX)
    kx = 2.0 * jnp.pi / NX * (n.astype(F32) + sigma.astype(F32) / NY)
    ky = 2.0 * jnp.pi / NY * wave.astype(F32)
    size = jnp.sqrt(kx * kx + ky * ky)
    anchor = (wave == 0) & (n == 0)
    size = jnp.where(anchor, 1.0, size)
    single = (wave == 0) | (wave == NY // 2)
    scale = jnp.where(single, 1.0, 2.0) / (NX * NY)
    weights = jnp.where(anchor, 0.0, -jnp.exp(-thickness * size) / size) * scale
    angle = sigma[:8].astype(F32) * (2.0 * jnp.pi / NY)
    last = inside[:8] == 7
    wrap_cos = jnp.where(last, jnp.cos(angle), 1.0)
    wrap_sin = jnp.where(last, jnp.sin(angle) * sign[:8], 0.0)
    return *there, *back, weights, wrap_cos, wrap_sin


def shards(density, xmomentum, ymomentum, shear_shift):
    t = host_tables()
    rho, mx, my = density[0], xmomentum[0], ymomentum[0]
    shift = shear_shift[0]
    radial = lax.axis_index("gx")
    flat = radial * GY + lax.axis_index("gy")
    off = shift % ROWS
    wrap_off = jnp.where(radial == GX - 1, off, 0)
    hop = (shift // ROWS + (flat % ROWS + off) // ROWS) % GY
    scalars = jnp.stack(
        [
            (ROWS - wrap_off) % ROWS,
            wrap_off,
            (GY - hop) % GY,
            hop,
            jnp.where(flat < ROWS, flat, -1),
            (flat == 0).astype(jnp.int32),
        ]
    ).astype(jnp.int32)
    everyone = ("gx", "gy")
    block = (ROWS, COLS)
    table = (256, 128)
    place = radial.astype(jnp.int32).reshape(1)
    columns = call(
        pack_kernel,
        table,
        place,
        shear_shift,
        rho,
        mx,
        my,
        name="pack",
        smem=1,
        hbm=4,
        room=62,
        scratch=(
            pltpu.VMEM((3, *block), F32),
            pltpu.SMEM((1,), jnp.int32),
            pltpu.SemaphoreType.DMA((4,)),
        ),
    )
    columns = lax.all_to_all(columns, everyone, 0, 0, tiled=True)
    waves = call(
        forward_kernel,
        table,
        scalars,
        columns,
        *t["blocks"],
        t["twist_cos"],
        t["twist_sin"],
        *t["inner"],
        name="forward",
        smem=1,
    )
    waves = lax.all_to_all(waves, everyone, 0, 0, tiled=True)
    ride = call(edges_kernel, table, scalars, columns, name="edges", smem=1)
    solved = call(
        radial_kernel,
        table,
        scalars,
        waves,
        ride,
        *radial_tables(shift),
        *t["groups"],
        t["radial_cos"],
        t["radial_sin"],
        t["cells"],
        t["cells_back"],
        *t["groups_back"],
        t["return_cos"],
        t["return_sin"],
        name="radial",
        smem=1,
    )
    solved = lax.all_to_all(solved, everyone, 0, 0, tiled=True)
    lines = call(
        backward_kernel,
        (128, 128),
        solved,
        t["inner_back"],
        t["back_cos"],
        t["back_sin"],
        *t["blocks_back"],
        name="backward",
    )
    lines = lax.all_to_all(lines, "gy", 0, 0, tiled=True)
    rho_new, mx_new, my_new = call(
        finish_kernel, [block, block, block], scalars, rho, mx, my, solved, name="finish", smem=1
    )
    potential = call(last_kernel, block, lines, name="last")
    return rho_new[None], mx_new[None], my_new[None], potential[None]


def solution(mesh):
    spec = P(None, "gy", "gx")
    return jax.shard_map(
        shards,
        mesh=mesh,
        in_specs=(spec, spec, spec, P()),
        out_specs=(spec, spec, spec, spec),
        check_vma=False,
    )
```

```python
import functools

import jax
import jax.numpy as jnp
import ml_dtypes
import numpy as np
from jax import lax
from jax.experimental import pallas as pl
from jax.experimental.pallas import tpu as pltpu
from jax.sharding import PartitionSpec as P

NX = 2048
NY = 2048
ROWS = 64
COLS = 256
GX = 8
GY = 32

time_step = 0.15
omega_rate = 0.5
shear_rate = 1.5
thickness = 0.5
middle = 1.0

BF = jnp.bfloat16
F32 = jnp.float32


def halves(table):
    table = np.asarray(table, np.float32)
    head = table.astype(ml_dtypes.bfloat16)
    rest = (table - head.astype(np.float32)).astype(ml_dtypes.bfloat16)
    return head, rest


def both_parts(table):
    head, rest = halves(table)
    return np.block([[head, rest], [head, np.zeros_like(rest)]])


def turn(index, length):
    angle = 2.0 * np.pi * (np.asarray(index) % length) / length
    return np.cos(angle), np.sin(angle)


@functools.cache
def host_tables():
    out = {}
    eye8 = np.eye(8)
    cos32, sin32 = turn(np.outer(np.arange(32), np.arange(32)), 32)

    def spread(table):
        return np.einsum("jm,ab->ajmb", table, eye8).reshape(256, 256)

    out["blocks"] = halves(np.concatenate([spread(cos32), spread(-sin32)], 1))
    m1 = np.repeat(np.arange(32), 8)
    tc, ts = turn(np.outer(np.arange(64), m1), NY)
    out["twist_cos"] = tc.astype(np.float32)
    out["twist_sin"] = ts.astype(np.float32)
    c64, s64 = turn(np.outer(np.arange(32), np.arange(64)), 64)
    last = np.zeros((16, 128))
    last[0, :64] = 1.0 - 2.0 * (np.arange(64) % 2)
    head, rest = halves(
        np.concatenate([np.concatenate([c64, s64], 1), np.concatenate([-s64, c64], 1), last])
    )
    out["inner"] = np.concatenate([head, head], 1), rest
    rows = np.arange(256)
    c256, s256 = turn(np.outer(rows, rows), 256)
    out["groups"] = halves(np.concatenate([c256, s256]))
    lane = np.arange(128)
    sign = np.where(lane < 64, 1.0, -1.0)
    tc, ts = turn(np.outer(rows, lane % 8), NX)
    out["radial_cos"] = tc.astype(np.float32)
    out["radial_sin"] = (ts * sign).astype(np.float32)
    c8, s8 = turn(np.outer(np.arange(8), np.arange(8)), 8)
    lines = np.eye(8)
    ck, sk = np.kron(lines, c8), np.kron(lines, s8)
    out["cells"] = both_parts(np.block([[ck, -sk], [sk, ck]]))
    out["cells_back"] = both_parts(np.block([[ck, sk], [-sk, ck]]))
    order = rows // 128 * 128 + rows // 32 % 4 + 4 * (rows % 32)
    c256, s256 = turn(np.outer(order, rows), 256)
    out["groups_back"] = halves(np.concatenate([c256, s256]))
    tc, ts = turn(np.outer(order, lane % 8), NX)
    out["return_cos"] = tc.astype(np.float32)
    out["return_sin"] = (ts * sign).astype(np.float32)
    c64, s64 = turn(np.outer(np.arange(64), np.arange(32)), 64)
    head, rest = halves(np.concatenate([c64, s64]))
    out["inner_back"] = np.concatenate([head, head, rest], 1)
    pair = np.arange(512) // 128
    part = np.arange(512) % 128 // 64
    which = np.arange(512) % 64 // 8
    m1 = pair * 8 + which
    q = np.arange(512) % 8
    tc, ts = turn(np.outer(np.arange(64), m1), NY)
    out["back_cos"] = tc.astype(np.float32)
    out["back_sin"] = (ts * np.where(part == 0, 1.0, -1.0)).astype(np.float32)
    j = np.tile(np.repeat(np.arange(32), 4), 2)
    own = np.repeat([0, 4], 128) + np.tile(np.arange(4), 64)
    c32, s32 = turn(np.outer(j, m1), 32)
    weight = np.where(part == 0, c32, -s32)
    weight = np.where((part == 1) & (m1 == 0), 1.0, weight)
    out["blocks_back"] = halves(weight * (own[:, None] == q[None, :]))
    return out


def split(value):
    head = value.astype(BF)
    rest = (value - head.astype(F32)).astype(BF)
    return head, rest


NN = (((1,), (0,)), ((), ()))
NT = (((1,), (1,)), ((), ()))


def dot(left, right, dims=NN):
    return lax.dot_general(left, right, dims, preferred_element_type=F32)


def product_rows(table_head, table_rest, value):
    head, rest = split(value)
    both = dot(table_head, jnp.concatenate([head, rest], 1))
    return both[:, :128] + both[:, 128:] + dot(table_rest, head)


def product_lanes(value, table):
    both = dot(jnp.concatenate(split(value), 1), table)
    return both[:, :128] + both[:, 128:]


def product_right(value, table_head, table_rest):
    head, rest = split(value)
    return dot(head, table_head) + (dot(rest, table_head) + dot(head, table_rest))


def roll(value, shift, axis):
    return pltpu.roll(value, shift % value.shape[axis], axis)


def lanes_of(shape):
    return lax.broadcasted_iota(jnp.int32, shape, 1)


def rows_of(shape):
    return lax.broadcasted_iota(jnp.int32, shape, 0)


def position():
    return lax.axis_index("gx") * GY + lax.axis_index("gy")


def wrap_hop(shifts):
    row = position() & (ROWS - 1)
    shifts = jnp.broadcast_to(shifts[0:1, :], (GY, 128))
    return ((shifts >> 6) + (((shifts & (ROWS - 1)) + row) >> 6)) & (GY - 1)


def turn_rows(block, hop, way):
    for bit in range(5):
        moved = roll(block, way << bit, 0)
        block = jnp.where((hop >> bit) & 1 == 1, moved, block)
    return block


def interface(left, right, normal, parts=3):
    speed = jnp.maximum(jnp.abs(left[3]), jnp.abs(right[3])) + 1.0
    fluxes = []
    for part in range(parts):
        f_left = left[part] * left[3]
        f_right = right[part] * right[3]
        if part == normal:
            f_left = f_left + left[0]
            f_right = f_right + right[0]
        fluxes.append(0.5 * (f_left + f_right) - 0.5 * speed * (right[part] - left[part]))
    return fluxes


def with_speed(fields, normal):
    return (*fields, fields[normal] / fields[0])


def inner_fluxes(state, parts):
    lane = lanes_of((ROWS, COLS))
    row = rows_of((ROWS, COLS))
    mid = with_speed(state, 1)
    west = interface([roll(v, 1, 1) for v in mid], mid, 1, parts)
    mid = with_speed(state, 2)
    south = interface([roll(v, 1, 0) for v in mid], mid, 2, parts)
    return [jnp.where(lane == 0, 0.0, v) for v in west], [jnp.where(row == 0, 0.0, v) for v in south]


def pack_kernel(shift, rho, mx, my, out, held, shift_held, ready):
    copies = [
        pltpu.make_async_copy(source, held.at[f], ready.at[f])
        for f, source in enumerate((rho, mx, my))
    ]
    copies.append(pltpu.make_async_copy(shift, shift_held, ready.at[3]))
    for copy in copies:
        copy.start()
    for copy in copies:
        copy.wait()
    state = (held[0], held[1], held[2])
    (west,), (south,) = inner_fluxes(state, 1)
    change = roll(west, -1, 1) - west + roll(south, -1, 0) - south
    partial = state[0] - time_step * change - middle
    row = rows_of((8, COLS))
    edges = jnp.zeros((8, COLS), F32)
    for f in range(3):
        edges = jnp.where(row == f, state[f][0:1, :], edges)
        edges = jnp.where(row == 3 + f, state[f][ROWS - 1 : ROWS, :], edges)
    tall = jnp.concatenate([partial, edges, jnp.zeros((56, COLS), F32)], 0).T
    lane = lanes_of((ROWS, 128))
    low = jnp.zeros((ROWS, 128), F32)
    high = jnp.zeros((ROWS, 128), F32)
    for f in range(3):
        low = jnp.where(lane == 72 + f, state[f][:, 0:1], low)
        high = jnp.where(lane == 75 + f, state[f][:, COLS - 1 : COLS], high)
    slide = jnp.where(lax.axis_index("gx") == GX - 1, (ROWS - (shift_held[0] & (ROWS - 1))) & (ROWS - 1), 0)
    out[0:ROWS, :] = tall[0:ROWS] + low + pltpu.roll(high, slide, 0)
    out[ROWS:, :] = tall[ROWS:]


def finish_kernel(scalars, rho, mx, my, arrived, rho_out, mx_out, my_out):
    state = (rho[...], mx[...], my[...])
    lane = lanes_of((ROWS, COLS))
    row = rows_of((ROWS, COLS))
    west, south = inner_fluxes(state, 3)
    across = arrived[...].T[32:40]
    beside = arrived[0:ROWS, :]
    beside_high = pltpu.roll(beside, scalars[0], 0)
    new = []
    for f in range(3):
        east = jnp.where(lane == COLS - 1, beside_high[:, 41 + f : 42 + f], roll(west[f], -1, 1))
        north = jnp.where(row == ROWS - 1, across[3 + f : 4 + f, :], roll(south[f], -1, 0))
        west_f = jnp.where(lane == 0, beside[:, 38 + f : 39 + f], west[f])
        south_f = jnp.where(row == 0, across[f : f + 1, :], south[f])
        new.append(state[f] - time_step * (east - west_f + north - south_f))
    rho_out[...] = new[0]
    mx_out[...] = new[1] + time_step * 2.0 * omega_rate * state[2]
    my_out[...] = new[2] - time_step * (2.0 - shear_rate) * omega_rate * state[1]


def edge_fluxes(shifts, arrived, parts):
    narrow = lanes_of((32, 128))
    last = arrived[224:256, :]
    wrapped = turn_rows(last, wrap_hop(shifts), -1)
    last = jnp.where((narrow >= 75) & (narrow < 78), wrapped, last)
    tall = jnp.concatenate([arrived[0:224, :], last], 0).T
    lane = lanes_of((8, 256))
    upper = tall[64:72]
    before = jnp.where(lane % 32 == 0, roll(upper, -31, 1), roll(upper, 1, 1))
    south = interface(
        with_speed([before[3 + f : 4 + f] for f in range(3)], 2),
        with_speed([upper[f : f + 1] for f in range(3)], 2),
        2,
        parts,
    )
    valid = jnp.zeros((1, 256), jnp.int32) + position() < ROWS
    side = tall[72:80]
    before = roll(side, 32, 1)
    left = [before[3 + f : 4 + f] for f in range(3)]
    right = [side[f : f + 1] for f in range(3)]
    left[0] = jnp.where(valid, left[0], 1.0)
    right[0] = jnp.where(valid, right[0], 1.0)
    west = interface(with_speed(left, 1), with_speed(right, 1), 1, parts)
    west = [jnp.where(valid, v, 0.0) for v in west]
    line = lanes_of((1, 256))
    north = [jnp.where(line % 32 == 31, roll(v, 31, 1), roll(v, -1, 1)) for v in south]
    return tall, west, south, north


def edges_kernel(shifts, arrived, ride):
    _, west, south, north = edge_fluxes(shifts, arrived, 3)
    east = [roll(v, -32, 1) for v in west]
    narrow = lanes_of((32, 128))
    rows16 = rows_of((16, 256))
    fluxes = jnp.zeros((16, 256), F32)
    for at, value in enumerate(south + north + west + east):
        fluxes = jnp.where(rows16 == at, value, fluxes)
    back = jnp.concatenate([jnp.zeros((32, 256), F32), fluxes, jnp.zeros((80, 256), F32)], 0).T
    last = back[224:256]
    wrapped = turn_rows(last, wrap_hop(shifts), 1)
    ride[0:224, :] = back[0:224]
    ride[224:256, :] = jnp.where((narrow >= 41) & (narrow < 44), wrapped, last)


def forward_kernel(shifts, arrived, blocks_h, blocks_l, twist_cos, twist_sin, inner_h, inner_l, out):
    tall, west, south, north = edge_fluxes(shifts, arrived, 1)
    narrow = lanes_of((32, 128))
    rows8 = rows_of((8, 256))
    rows64 = rows_of((64, 256))
    density = tall[0:64]
    density = density + jnp.where(rows64 == 0, time_step * south[0], 0.0)
    density = density - jnp.where(rows64 == 63, time_step * north[0], 0.0)
    edge = jnp.where(rows8 == 0, time_step * west[0], 0.0)
    first = product_right(jnp.concatenate([density, edge], 0), blocks_h[...], blocks_l[...])
    tc = twist_cos[...]
    ts = twist_sin[...]
    re, im = first[:64, :256], first[:64, 256:]
    main = jnp.concatenate([re * tc + im * ts, im * tc - re * ts], 0)
    re, im = first[64:65, :256], first[64:65, 256:]
    here = rows64 == position()
    edge = jnp.concatenate(
        [jnp.where(here, re * tc + im * ts, 0.0), jnp.where(here, im * tc - re * ts, 0.0)], 0
    )
    head, rest = split(jnp.concatenate([main, edge], 1))
    waves = dot(inner_h[...], jnp.concatenate([head, rest], 0)) + dot(inner_l[...], head)
    rows32 = rows_of((32, 128))
    for g in range(8):
        place = 32 * (g % 4)
        pieces = []
        for start in (0, 256):
            tile = slice(start + g // 4 * 128, start + g // 4 * 128 + 128)
            real = waves[0:32, tile]
            imag = waves[32:64, tile]
            if g == 0:
                imag = jnp.where((rows32 == 0) & (narrow < 8), waves[64:65, tile], imag)
            pieces.append((real, imag))
        both = roll(pieces[1][1], 96 - place, 1)
        both = jnp.where(narrow < 96, roll(pieces[0][1], 64 - place, 1), both)
        both = jnp.where(narrow < 64, roll(pieces[1][0], 32 - place, 1), both)
        both = jnp.where(narrow < 32, roll(pieces[0][0], -place, 1), both)
        out[g * 32 : (g + 1) * 32, :] = both


def radial_kernel(
    arrived,
    ride,
    theta_cos,
    theta_sin,
    theta_cos_back,
    theta_sin_back,
    weights,
    wrap_cos,
    wrap_sin,
    groups_h,
    groups_l,
    radial_cos,
    radial_sin,
    cells,
    cells_back,
    groups_back_h,
    groups_back_l,
    return_cos,
    return_sin,
    out,
):
    shape = (256, 128)
    half = functools.partial(roll, shift=64, axis=1)

    def apart(value):
        lane = lanes_of(value.shape)
        first = jnp.zeros(value.shape, jnp.int32) + position() == 0
        value = jnp.where(lane % 64 < 32, value, 0.0)
        fifth = roll(value, -32, 1)
        slot = (lane >= 64) & (lane < 72) & first
        return jnp.where((lane >= 32) & (lane < 40), fifth, jnp.where(slot, 0.0, value))

    lane = lanes_of(shape)
    row = rows_of(shape)
    sign = jnp.where(lane < 64, 1.0, -1.0)
    value = arrived[...]
    edge = jnp.sum(value[0:ROWS], axis=0, keepdims=True)
    edge = apart(roll(jnp.broadcast_to(edge, (8, 128)), -32, 1))
    lane8 = lanes_of((8, 128))
    beside = jnp.where(lane8 % 8 == 7, roll(edge, 7, 1), roll(edge, -1, 1))
    beside = beside * wrap_cos[...] + half(beside) * wrap_sin[...]
    value = apart(value)
    value = value + jnp.where(row == 0, edge[0:1], 0.0) - jnp.where(row == 255, beside[0:1], 0.0)
    value = value * theta_cos[...] + half(value) * theta_sin[...]
    value = product_lanes(value, cells[...])
    value = value * radial_cos[...] + half(value) * radial_sin[...]
    both = product_rows(groups_h[...], groups_l[...], value)
    value = both[:256] + sign * half(both[256:])
    mean_mode = (row == 0) & (lane == 0) & (jnp.zeros(shape, jnp.int32) + position() == 0)
    value = value + jnp.where(mean_mode, middle * NX * NY, 0.0)
    value = value * weights[...]
    both = product_rows(groups_back_h[...], groups_back_l[...], value)
    value = both[:256] - sign * half(both[256:])
    value = value * return_cos[...] - half(value) * return_sin[...]
    value = product_lanes(value, cells_back[...])
    value = value * theta_cos_back[...] - half(value) * theta_sin_back[...]
    first = jnp.zeros(shape, jnp.int32) + position() == 0
    value = jnp.where((lane >= 64) & (lane < 72) & first, roll(value, 32, 1), value)
    blocks = [value[32 * k : 32 * k + 32] for k in range(8)]
    narrow = lanes_of((32, 128))
    for bit in (1, 2, 4):
        swapped = list(blocks)
        for k in range(8):
            if k & bit == 0:
                a, b = blocks[k], blocks[k + bit]
                low = narrow & bit == 0
                swapped[k] = jnp.where(low, a, roll(b, bit, 1))
                swapped[k + bit] = jnp.where(low, roll(a, -bit, 1), b)
        blocks = swapped
    value = jnp.concatenate(blocks, 0)
    out[...] = jnp.where((lane >= 32) & (lane < 44), ride[...], value)


def backward_kernel(arrived, inner, back_cos, back_sin, blocks_h, blocks_l, out):
    lane = lanes_of((32, 128))
    low = lane % 64 < 32
    pairs = []
    for h in range(4):
        even = arrived[64 * h : 64 * h + 32, :]
        odd = arrived[64 * h + 32 : 64 * h + 64, :]
        pairs.append(jnp.where(low, even, roll(odd, 32, 1)))
    value = jnp.concatenate(pairs, 1)
    head, rest = split(value)
    both = dot(inner[...], jnp.concatenate([head, rest, head], 0))
    wide = lanes_of((64, 128))
    row = rows_of((64, 128))
    sign = jnp.where(wide < 64, 1.0, -1.0)
    parity = jnp.where(row % 2 == 0, 1.0, -1.0)
    turned = []
    for h in range(4):
        tile = slice(128 * h, 128 * h + 128)
        part = both[:64, tile] - sign * roll(both[64:, tile], 64, 1)
        part = part * back_cos[:, tile] - roll(part, 64, 1) * back_sin[:, tile]
        if h == 0:
            part = jnp.where((wide >= 64) & (wide < 72), parity * pairs[0][0:1, :], part)
        turned.append(part)
    head, rest = split(jnp.concatenate(turned, 1))
    full = dot(blocks_h[...], jnp.concatenate([head, rest], 0), NT)
    full = full + roll(full, 64, 1)
    full = full + dot(blocks_l[...], jnp.concatenate([head, head], 0), NT)
    square = lanes_of((128, 128))
    out[...] = jnp.where(square < 64, full[:128], full[128:])


def last_kernel(arrived, out):
    tall = arrived[...].T
    out[:, :128] = tall[:ROWS]
    out[:, 128:] = tall[ROWS:]


VMEM = pl.BlockSpec(memory_space=pltpu.VMEM)
SMEM = pl.BlockSpec(memory_space=pltpu.SMEM)
HBM = pl.BlockSpec(memory_space=pltpu.HBM)


def call(kernel, shapes, *args, name, smem=0, hbm=0, scratch=(), room=32):
    many = isinstance(shapes, list)
    outs = [jax.ShapeDtypeStruct(s, F32) for s in (shapes if many else [shapes])]
    return pl.pallas_call(
        kernel,
        out_shape=outs if many else outs[0],
        in_specs=[SMEM] * smem + [HBM] * hbm + [VMEM] * (len(args) - smem - hbm),
        out_specs=[VMEM] * len(outs) if many else VMEM,
        scratch_shapes=scratch,
        name=name,
        compiler_params=pltpu.CompilerParams(vmem_limit_bytes=room * 1024 * 1024),
        cost_estimate=pl.CostEstimate(flops=100_000_000, bytes_accessed=1_000_000, transcendentals=0),
    )(*args)


def radial_tables(shift):
    shape = (256, 128)
    row = lax.broadcasted_iota(jnp.int32, shape, 0)
    lane = lax.broadcasted_iota(jnp.int32, shape, 1)
    line = lane % 64 // 8
    inside = lane % 8
    wave = lax.axis_index("gx") * 4 + line + GY * lax.axis_index("gy")
    wave = jnp.where(line < 4, wave, NY // 2)
    sigma = wave * shift % NY
    sign = jnp.where(lane < 64, 1.0, -1.0)

    def phase(cell):
        angle = (sigma * cell % (NX * NY)).astype(F32) * (2.0 * jnp.pi / (NX * NY))
        return jnp.cos(angle), jnp.sin(angle) * sign

    there = phase(row + COLS * inside)
    back = phase(row // 128 * 128 + row // 32 % 4 + 4 * (row % 32) + COLS * inside)
    n = inside + 8 * row
    n = jnp.where(n < NX // 2, n, n - NX)
    kx = 2.0 * jnp.pi / NX * (n.astype(F32) + sigma.astype(F32) / NY)
    ky = 2.0 * jnp.pi / NY * wave.astype(F32)
    size = jnp.sqrt(kx * kx + ky * ky)
    anchor = (wave == 0) & (n == 0)
    size = jnp.where(anchor, 1.0, size)
    single = (wave == 0) | (wave == NY // 2)
    scale = jnp.where(single, 1.0, 2.0) / (NX * NY)
    weights = jnp.where(anchor, 0.0, -jnp.exp(-thickness * size) / size) * scale
    angle = sigma[:8].astype(F32) * (2.0 * jnp.pi / NY)
    last = inside[:8] == 7
    wrap_cos = jnp.where(last, jnp.cos(angle), 1.0)
    wrap_sin = jnp.where(last, jnp.sin(angle) * sign[:8], 0.0)
    return *there, *back, weights, wrap_cos, wrap_sin


def shards(density, xmomentum, ymomentum, shear_shift):
    t = host_tables()
    rho, mx, my = density[0], xmomentum[0], ymomentum[0]
    shift = shear_shift[0]
    radial = lax.axis_index("gx")
    scalars = jnp.where(radial == GX - 1, shift % ROWS, 0).astype(jnp.int32).reshape(1)
    shifts = jnp.broadcast_to(shift, (8, 128))
    everyone = ("gx", "gy")
    block = (ROWS, COLS)
    table = (256, 128)
    columns = call(
        pack_kernel,
        table,
        shear_shift,
        rho,
        mx,
        my,
        name="pack",
        hbm=4,
        room=62,
        scratch=(
            pltpu.VMEM((3, *block), F32),
            pltpu.SMEM((1,), jnp.int32),
            pltpu.SemaphoreType.DMA((4,)),
        ),
    )
    columns = lax.all_to_all(columns, everyone, 0, 0, tiled=True)
    waves = call(
        forward_kernel,
        table,
        shifts,
        columns,
        *t["blocks"],
        t["twist_cos"],
        t["twist_sin"],
        *t["inner"],
        name="forward",
    )
    waves = lax.all_to_all(waves, everyone, 0, 0, tiled=True)
    ride = call(edges_kernel, table, shifts, columns, name="edges")
    solved = call(
        radial_kernel,
        table,
        waves,
        ride,
        *radial_tables(shift),
        *t["groups"],
        t["radial_cos"],
        t["radial_sin"],
        t["cells"],
        t["cells_back"],
        *t["groups_back"],
        t["return_cos"],
        t["return_sin"],
        name="radial",
    )
    solved = lax.all_to_all(solved, everyone, 0, 0, tiled=True)
    lines = call(
        backward_kernel,
        (128, 128),
        solved,
        t["inner_back"],
        t["back_cos"],
        t["back_sin"],
        *t["blocks_back"],
        name="backward",
    )
    lines = lax.all_to_all(lines, "gy", 0, 0, tiled=True)
    rho_new, mx_new, my_new = call(
        finish_kernel, [block, block, block], scalars, rho, mx, my, solved, name="finish", smem=1
    )
    potential = call(last_kernel, block, lines, name="last")
    return rho_new[None], mx_new[None], my_new[None], potential[None]


def solution(mesh):
    spec = P(None, "gy", "gx")
    return jax.shard_map(
        shards,
        mesh=mesh,
        in_specs=(spec, spec, spec, P()),
        out_specs=(spec, spec, spec, spec),
        check_vma=False,
    )
```

```python
import functools

import jax
import jax.numpy as jnp
import ml_dtypes
import numpy as np
from jax import lax
from jax.experimental import pallas as pl
from jax.experimental.pallas import tpu as pltpu
from jax.sharding import PartitionSpec as P

NX = 2048
NY = 2048
ROWS = 64
COLS = 256
GX = 8
GY = 32

time_step = 0.15
omega_rate = 0.5
shear_rate = 1.5
thickness = 0.5
middle = 1.0

BF = jnp.bfloat16
F32 = jnp.float32


def halves(table):
    table = np.asarray(table, np.float32)
    head = table.astype(ml_dtypes.bfloat16)
    rest = (table - head.astype(np.float32)).astype(ml_dtypes.bfloat16)
    return head, rest


def both_parts(table):
    head, rest = halves(table)
    return np.block([[head, rest], [head, np.zeros_like(rest)]])


def turn(index, length):
    angle = 2.0 * np.pi * (np.asarray(index) % length) / length
    return np.cos(angle), np.sin(angle)


@functools.cache
def host_tables():
    out = {}
    eye8 = np.eye(8)
    cos32, sin32 = turn(np.outer(np.arange(32), np.arange(32)), 32)

    def spread(table):
        return np.einsum("jm,ab->ajmb", table, eye8).reshape(256, 256)

    out["blocks"] = halves(np.concatenate([spread(cos32), spread(-sin32)], 1))
    m1 = np.repeat(np.arange(32), 8)
    tc, ts = turn(np.outer(np.arange(64), m1), NY)
    out["twist_cos"] = tc.astype(np.float32)
    out["twist_sin"] = ts.astype(np.float32)
    c64, s64 = turn(np.outer(np.arange(32), np.arange(64)), 64)
    last = np.zeros((16, 128))
    last[0, :64] = 1.0 - 2.0 * (np.arange(64) % 2)
    head, rest = halves(
        np.concatenate([np.concatenate([c64, s64], 1), np.concatenate([-s64, c64], 1), last])
    )
    out["inner"] = np.concatenate([head, head], 1), rest
    rows = np.arange(256)
    c256, s256 = turn(np.outer(rows, rows), 256)
    out["groups"] = halves(np.concatenate([c256, s256]))
    lane = np.arange(128)
    sign = np.where(lane < 64, 1.0, -1.0)
    tc, ts = turn(np.outer(rows, lane % 8), NX)
    out["radial_cos"] = tc.astype(np.float32)
    out["radial_sin"] = (ts * sign).astype(np.float32)
    c8, s8 = turn(np.outer(np.arange(8), np.arange(8)), 8)
    lines = np.eye(8)
    ck, sk = np.kron(lines, c8), np.kron(lines, s8)
    out["cells"] = both_parts(np.block([[ck, -sk], [sk, ck]]))
    out["cells_back"] = both_parts(np.block([[ck, sk], [-sk, ck]]))
    order = rows // 128 * 128 + rows // 32 % 4 + 4 * (rows % 32)
    c256, s256 = turn(np.outer(order, rows), 256)
    out["groups_back"] = halves(np.concatenate([c256, s256]))
    tc, ts = turn(np.outer(order, lane % 8), NX)
    out["return_cos"] = tc.astype(np.float32)
    out["return_sin"] = (ts * sign).astype(np.float32)
    c64, s64 = turn(np.outer(np.arange(64), np.arange(32)), 64)
    head, rest = halves(np.concatenate([c64, s64]))
    out["inner_back"] = np.concatenate([head, head, rest], 1)
    pair = np.arange(512) // 128
    part = np.arange(512) % 128 // 64
    which = np.arange(512) % 64 // 8
    m1 = pair * 8 + which
    q = np.arange(512) % 8
    tc, ts = turn(np.outer(np.arange(64), m1), NY)
    out["back_cos"] = tc.astype(np.float32)
    out["back_sin"] = (ts * np.where(part == 0, 1.0, -1.0)).astype(np.float32)
    j = np.tile(np.repeat(np.arange(32), 4), 2)
    own = np.repeat([0, 4], 128) + np.tile(np.arange(4), 64)
    c32, s32 = turn(np.outer(j, m1), 32)
    weight = np.where(part == 0, c32, -s32)
    weight = np.where((part == 1) & (m1 == 0), 1.0, weight)
    out["blocks_back"] = halves(weight * (own[:, None] == q[None, :]))
    return out


def split(value):
    head = value.astype(BF)
    rest = (value - head.astype(F32)).astype(BF)
    return head, rest


NN = (((1,), (0,)), ((), ()))
NT = (((1,), (1,)), ((), ()))


def dot(left, right, dims=NN):
    return lax.dot_general(left, right, dims, preferred_element_type=F32)


def product_rows(table_head, table_rest, value):
    head, rest = split(value)
    both = dot(table_head, jnp.concatenate([head, rest], 1))
    return both[:, :128] + both[:, 128:] + dot(table_rest, head)


def product_lanes(value, table):
    both = dot(jnp.concatenate(split(value), 1), table)
    return both[:, :128] + both[:, 128:]


def product_right(value, table_head, table_rest):
    head, rest = split(value)
    return dot(head, table_head) + (dot(rest, table_head) + dot(head, table_rest))


def roll(value, shift, axis):
    return pltpu.roll(value, shift % value.shape[axis], axis)


def lanes_of(shape):
    return lax.broadcasted_iota(jnp.int32, shape, 1)


def rows_of(shape):
    return lax.broadcasted_iota(jnp.int32, shape, 0)


def position():
    return lax.axis_index("gx") * GY + lax.axis_index("gy")


def wrap_hop(shifts):
    row = position() & (ROWS - 1)
    shifts = jnp.broadcast_to(shifts[0:1, :], (GY, 128))
    return ((shifts >> 6) + (((shifts & (ROWS - 1)) + row) >> 6)) & (GY - 1)


def turn_rows(block, hop, way):
    for bit in range(5):
        moved = roll(block, way << bit, 0)
        block = jnp.where((hop >> bit) & 1 == 1, moved, block)
    return block


def interface(left, right, normal, parts=3):
    speed = jnp.maximum(jnp.abs(left[3]), jnp.abs(right[3])) + 1.0
    fluxes = []
    for part in range(parts):
        f_left = left[part] * left[3]
        f_right = right[part] * right[3]
        if part == normal:
            f_left = f_left + left[0]
            f_right = f_right + right[0]
        fluxes.append(0.5 * (f_left + f_right) - 0.5 * speed * (right[part] - left[part]))
    return fluxes


def with_speed(fields, normal):
    return (*fields, fields[normal] / fields[0])


def inner_fluxes(state, parts):
    lane = lanes_of((ROWS, COLS))
    row = rows_of((ROWS, COLS))
    mid = with_speed(state, 1)
    west = interface([roll(v, 1, 1) for v in mid], mid, 1, parts)
    mid = with_speed(state, 2)
    south = interface([roll(v, 1, 0) for v in mid], mid, 2, parts)
    return [jnp.where(lane == 0, 0.0, v) for v in west], [jnp.where(row == 0, 0.0, v) for v in south]


def pack_kernel(shift, rho, mx, my, out, held, shift_held, ready):
    copies = [
        pltpu.make_async_copy(source, held.at[f], ready.at[f])
        for f, source in enumerate((rho, mx, my))
    ]
    copies.append(pltpu.make_async_copy(shift, shift_held, ready.at[3]))
    for copy in copies:
        copy.start()
    for copy in copies:
        copy.wait()
    state = (held[0], held[1], held[2])
    (west,), (south,) = inner_fluxes(state, 1)
    change = roll(west, -1, 1) - west + roll(south, -1, 0) - south
    partial = state[0] - time_step * change - middle
    row = rows_of((8, COLS))
    edges = jnp.zeros((8, COLS), F32)
    for f in range(3):
        edges = jnp.where(row == f, state[f][0:1, :], edges)
        edges = jnp.where(row == 3 + f, state[f][ROWS - 1 : ROWS, :], edges)
    tall = jnp.concatenate([partial, edges, jnp.zeros((56, COLS), F32)], 0).T
    lane = lanes_of((ROWS, 128))
    low = jnp.zeros((ROWS, 128), F32)
    high = jnp.zeros((ROWS, 128), F32)
    for f in range(3):
        low = jnp.where(lane == 72 + f, state[f][:, 0:1], low)
        high = jnp.where(lane == 75 + f, state[f][:, COLS - 1 : COLS], high)
    slide = jnp.where(lax.axis_index("gx") == GX - 1, (ROWS - (shift_held[0] & (ROWS - 1))) & (ROWS - 1), 0)
    out[0:ROWS, :] = tall[0:ROWS] + low + pltpu.roll(high, slide, 0)
    out[ROWS:, :] = tall[ROWS:]


def finish_kernel(shifts, rho, mx, my, arrived, lines, rho_out, mx_out, my_out, potential):
    state = (rho[...], mx[...], my[...])
    lane = lanes_of((ROWS, COLS))
    row = rows_of((ROWS, COLS))
    west, south = inner_fluxes(state, 3)
    across = arrived[...].T[32:40]
    beside = arrived[0:ROWS, :]
    beside_high = beside
    off = jnp.broadcast_to(shifts[0:1, :], (ROWS, 128)) & (ROWS - 1)
    off = jnp.where(jnp.zeros((ROWS, 128), jnp.int32) + lax.axis_index("gx") == GX - 1, off, 0)
    for bit in range(6):
        moved = roll(beside_high, 1 << bit, 0)
        beside_high = jnp.where((off >> bit) & 1 == 1, moved, beside_high)
    new = []
    for f in range(3):
        east = jnp.where(lane == COLS - 1, beside_high[:, 41 + f : 42 + f], roll(west[f], -1, 1))
        north = jnp.where(row == ROWS - 1, across[3 + f : 4 + f, :], roll(south[f], -1, 0))
        west_f = jnp.where(lane == 0, beside[:, 38 + f : 39 + f], west[f])
        south_f = jnp.where(row == 0, across[f : f + 1, :], south[f])
        new.append(state[f] - time_step * (east - west_f + north - south_f))
    rho_out[...] = new[0]
    mx_out[...] = new[1] + time_step * 2.0 * omega_rate * state[2]
    tall = lines[...].T
    potential[:, :128] = tall[:ROWS]
    potential[:, 128:] = tall[ROWS:]
    my_out[...] = new[2] - time_step * (2.0 - shear_rate) * omega_rate * state[1]


def edge_fluxes(shifts, arrived, parts):
    narrow = lanes_of((32, 128))
    last = arrived[224:256, :]
    wrapped = turn_rows(last, wrap_hop(shifts), -1)
    last = jnp.where((narrow >= 75) & (narrow < 78), wrapped, last)
    tall = jnp.concatenate([arrived[0:224, :], last], 0).T
    lane = lanes_of((8, 256))
    upper = tall[64:72]
    before = jnp.where(lane % 32 == 0, roll(upper, -31, 1), roll(upper, 1, 1))
    south = interface(
        with_speed([before[3 + f : 4 + f] for f in range(3)], 2),
        with_speed([upper[f : f + 1] for f in range(3)], 2),
        2,
        parts,
    )
    valid = jnp.zeros((1, 256), jnp.int32) + position() < ROWS
    side = tall[72:80]
    before = roll(side, 32, 1)
    left = [before[3 + f : 4 + f] for f in range(3)]
    right = [side[f : f + 1] for f in range(3)]
    left[0] = jnp.where(valid, left[0], 1.0)
    right[0] = jnp.where(valid, right[0], 1.0)
    west = interface(with_speed(left, 1), with_speed(right, 1), 1, parts)
    west = [jnp.where(valid, v, 0.0) for v in west]
    line = lanes_of((1, 256))
    north = [jnp.where(line % 32 == 31, roll(v, 31, 1), roll(v, -1, 1)) for v in south]
    return tall, west, south, north


def forward_kernel(shifts, arrived, blocks_h, blocks_l, twist_cos, twist_sin, inner_h, inner_l, out, fluxes):
    tall, west, south, north = edge_fluxes(shifts, arrived, 3)
    rows16 = rows_of((16, 256))
    held = jnp.zeros((16, 256), F32)
    for at, value in enumerate(south + north + west + [roll(v, -32, 1) for v in west]):
        held = jnp.where(rows16 == at, value, held)
    fluxes[...] = held
    narrow = lanes_of((32, 128))
    rows8 = rows_of((8, 256))
    rows64 = rows_of((64, 256))
    density = tall[0:64]
    density = density + jnp.where(rows64 == 0, time_step * south[0], 0.0)
    density = density - jnp.where(rows64 == 63, time_step * north[0], 0.0)
    edge = jnp.where(rows8 == 0, time_step * west[0], 0.0)
    first = product_right(jnp.concatenate([density, edge], 0), blocks_h[...], blocks_l[...])
    tc = twist_cos[...]
    ts = twist_sin[...]
    re, im = first[:64, :256], first[:64, 256:]
    main = jnp.concatenate([re * tc + im * ts, im * tc - re * ts], 0)
    re, im = first[64:65, :256], first[64:65, 256:]
    here = rows64 == position()
    edge = jnp.concatenate(
        [jnp.where(here, re * tc + im * ts, 0.0), jnp.where(here, im * tc - re * ts, 0.0)], 0
    )
    head, rest = split(jnp.concatenate([main, edge], 1))
    waves = dot(inner_h[...], jnp.concatenate([head, rest], 0)) + dot(inner_l[...], head)
    rows32 = rows_of((32, 128))
    for g in range(8):
        place = 32 * (g % 4)
        pieces = []
        for start in (0, 256):
            tile = slice(start + g // 4 * 128, start + g // 4 * 128 + 128)
            real = waves[0:32, tile]
            imag = waves[32:64, tile]
            if g == 0:
                imag = jnp.where((rows32 == 0) & (narrow < 8), waves[64:65, tile], imag)
            pieces.append((real, imag))
        both = roll(pieces[1][1], 96 - place, 1)
        both = jnp.where(narrow < 96, roll(pieces[0][1], 64 - place, 1), both)
        both = jnp.where(narrow < 64, roll(pieces[1][0], 32 - place, 1), both)
        both = jnp.where(narrow < 32, roll(pieces[0][0], -place, 1), both)
        out[g * 32 : (g + 1) * 32, :] = both


def radial_kernel(
    shifts,
    arrived,
    fluxes,
    theta_cos,
    theta_sin,
    theta_cos_back,
    theta_sin_back,
    weights,
    wrap_cos,
    wrap_sin,
    groups_h,
    groups_l,
    radial_cos,
    radial_sin,
    cells,
    cells_back,
    groups_back_h,
    groups_back_l,
    return_cos,
    return_sin,
    out,
):
    shape = (256, 128)
    half = functools.partial(roll, shift=64, axis=1)

    def apart(value):
        lane = lanes_of(value.shape)
        first = jnp.zeros(value.shape, jnp.int32) + position() == 0
        value = jnp.where(lane % 64 < 32, value, 0.0)
        fifth = roll(value, -32, 1)
        slot = (lane >= 64) & (lane < 72) & first
        return jnp.where((lane >= 32) & (lane < 40), fifth, jnp.where(slot, 0.0, value))

    lane = lanes_of(shape)
    row = rows_of(shape)
    sign = jnp.where(lane < 64, 1.0, -1.0)
    value = arrived[...]
    edge = jnp.sum(value[0:ROWS], axis=0, keepdims=True)
    edge = apart(roll(jnp.broadcast_to(edge, (8, 128)), -32, 1))
    lane8 = lanes_of((8, 128))
    beside = jnp.where(lane8 % 8 == 7, roll(edge, 7, 1), roll(edge, -1, 1))
    beside = beside * wrap_cos[...] + half(beside) * wrap_sin[...]
    value = apart(value)
    value = value + jnp.where(row == 0, edge[0:1], 0.0) - jnp.where(row == 255, beside[0:1], 0.0)
    value = value * theta_cos[...] + half(value) * theta_sin[...]
    value = product_lanes(value, cells[...])
    value = value * radial_cos[...] + half(value) * radial_sin[...]
    both = product_rows(groups_h[...], groups_l[...], value)
    value = both[:256] + sign * half(both[256:])
    mean_mode = (row == 0) & (lane == 0) & (jnp.zeros(shape, jnp.int32) + position() == 0)
    value = value + jnp.where(mean_mode, middle * NX * NY, 0.0)
    value = value * weights[...]
    both = product_rows(groups_back_h[...], groups_back_l[...], value)
    value = both[:256] - sign * half(both[256:])
    value = value * return_cos[...] - half(value) * return_sin[...]
    value = product_lanes(value, cells_back[...])
    value = value * theta_cos_back[...] - half(value) * theta_sin_back[...]
    first = jnp.zeros(shape, jnp.int32) + position() == 0
    value = jnp.where((lane >= 64) & (lane < 72) & first, roll(value, 32, 1), value)
    narrow = lanes_of((32, 128))
    none = jnp.zeros((32, 128), F32)
    back = jnp.concatenate(
        [
            jnp.concatenate([none, fluxes[:, k : k + 128], none, none, none[:16]], 0).T
            for k in (0, 128)
        ],
        0,
    )
    last = back[224:256]
    wrapped = turn_rows(last, wrap_hop(shifts), 1)
    ride = [back[32 * k : 32 * k + 32] for k in range(7)]
    ride.append(jnp.where((narrow >= 41) & (narrow < 44), wrapped, last))
    blocks = [value[32 * k : 32 * k + 32] for k in range(8)]
    for bit in (1, 2, 4):
        swapped = list(blocks)
        for k in range(8):
            if k & bit == 0:
                a, b = blocks[k], blocks[k + bit]
                low = narrow & bit == 0
                swapped[k] = jnp.where(low, a, roll(b, bit, 1))
                swapped[k + bit] = jnp.where(low, roll(a, -bit, 1), b)
        blocks = swapped
    spare = (narrow >= 32) & (narrow < 44)
    for k in range(8):
        out[32 * k : 32 * k + 32, :] = jnp.where(spare, ride[k], blocks[k])


def backward_kernel(arrived, inner, back_cos, back_sin, blocks_h, blocks_l, out):
    lane = lanes_of((32, 128))
    low = lane % 64 < 32
    pairs = []
    for h in range(4):
        even = arrived[64 * h : 64 * h + 32, :]
        odd = arrived[64 * h + 32 : 64 * h + 64, :]
        pairs.append(jnp.where(low, even, roll(odd, 32, 1)))
    value = jnp.concatenate(pairs, 1)
    head, rest = split(value)
    both = dot(inner[...], jnp.concatenate([head, rest, head], 0))
    wide = lanes_of((64, 128))
    row = rows_of((64, 128))
    sign = jnp.where(wide < 64, 1.0, -1.0)
    parity = jnp.where(row % 2 == 0, 1.0, -1.0)
    turned = []
    for h in range(4):
        tile = slice(128 * h, 128 * h + 128)
        part = both[:64, tile] - sign * roll(both[64:, tile], 64, 1)
        part = part * back_cos[:, tile] - roll(part, 64, 1) * back_sin[:, tile]
        if h == 0:
            part = jnp.where((wide >= 64) & (wide < 72), parity * pairs[0][0:1, :], part)
        turned.append(part)
    head, rest = split(jnp.concatenate(turned, 1))
    full = dot(blocks_h[...], jnp.concatenate([head, rest], 0), NT)
    full = full + roll(full, 64, 1)
    full = full + dot(blocks_l[...], jnp.concatenate([head, head], 0), NT)
    square = lanes_of((128, 128))
    out[...] = jnp.where(square < 64, full[:128], full[128:])


VMEM = pl.BlockSpec(memory_space=pltpu.VMEM)
SMEM = pl.BlockSpec(memory_space=pltpu.SMEM)
HBM = pl.BlockSpec(memory_space=pltpu.HBM)


def call(kernel, shapes, *args, name, smem=0, hbm=0, scratch=(), room=32):
    many = isinstance(shapes, list)
    outs = [jax.ShapeDtypeStruct(s, F32) for s in (shapes if many else [shapes])]
    return pl.pallas_call(
        kernel,
        out_shape=outs if many else outs[0],
        in_specs=[SMEM] * smem + [HBM] * hbm + [VMEM] * (len(args) - smem - hbm),
        out_specs=[VMEM] * len(outs) if many else VMEM,
        scratch_shapes=scratch,
        name=name,
        compiler_params=pltpu.CompilerParams(vmem_limit_bytes=room * 1024 * 1024),
        cost_estimate=pl.CostEstimate(flops=100_000_000, bytes_accessed=1_000_000, transcendentals=0),
    )(*args)


def radial_tables(shift):
    shape = (256, 128)
    row = lax.broadcasted_iota(jnp.int32, shape, 0)
    lane = lax.broadcasted_iota(jnp.int32, shape, 1)
    line = lane % 64 // 8
    inside = lane % 8
    wave = lax.axis_index("gx") * 4 + line + GY * lax.axis_index("gy")
    wave = jnp.where(line < 4, wave, NY // 2)
    sigma = wave * shift % NY
    sign = jnp.where(lane < 64, 1.0, -1.0)

    def phase(cell):
        angle = (sigma * cell % (NX * NY)).astype(F32) * (2.0 * jnp.pi / (NX * NY))
        return jnp.cos(angle), jnp.sin(angle) * sign

    there = phase(row + COLS * inside)
    back = phase(row // 128 * 128 + row // 32 % 4 + 4 * (row % 32) + COLS * inside)
    n = inside + 8 * row
    n = jnp.where(n < NX // 2, n, n - NX)
    kx = 2.0 * jnp.pi / NX * (n.astype(F32) + sigma.astype(F32) / NY)
    ky = 2.0 * jnp.pi / NY * wave.astype(F32)
    size = jnp.sqrt(kx * kx + ky * ky)
    anchor = (wave == 0) & (n == 0)
    size = jnp.where(anchor, 1.0, size)
    single = (wave == 0) | (wave == NY // 2)
    scale = jnp.where(single, 1.0, 2.0) / (NX * NY)
    weights = jnp.where(anchor, 0.0, -jnp.exp(-thickness * size) / size) * scale
    angle = sigma[:8].astype(F32) * (2.0 * jnp.pi / NY)
    last = inside[:8] == 7
    wrap_cos = jnp.where(last, jnp.cos(angle), 1.0)
    wrap_sin = jnp.where(last, jnp.sin(angle) * sign[:8], 0.0)
    return *there, *back, weights, wrap_cos, wrap_sin


def shards(density, xmomentum, ymomentum, shear_shift):
    t = host_tables()
    rho, mx, my = density[0], xmomentum[0], ymomentum[0]
    shift = shear_shift[0]
    radial = lax.axis_index("gx")
    shifts = jnp.broadcast_to(shifts[0:1, :], (GY, 128))
    return ((shifts >> 6) + (((shifts & (ROWS - 1)) + row) >> 6)) & (GY - 1)


def turn_rows(block, hop, way):
    for bit in range(5):
        moved = roll(block, way << bit, 0)
        block = jnp.where((hop >> bit) & 1 == 1, moved, block)
    return block


def interface(left, right, normal, parts=3):
    speed = jnp.maximum(jnp.abs(left[3]), jnp.abs(right[3])) + 1.0
    fluxes = []
    for part in range(parts):
        f_left = left[part] * left[3]
        f_right = right[part] * right[3]
        if part == normal:
            f_left = f_left + left[0]
            f_right = f_right + right[0]
        fluxes.append(0.5 * (f_left + f_right) - 0.5 * speed * (right[part] - left[part]))
    return fluxes


def with_speed(fields, normal):
    return (*fields, fields[normal] / fields[0])


def inner_fluxes(state, parts):
    lane = lanes_of((ROWS, COLS))
    row = rows_of((ROWS, COLS))
    mid = with_speed(state, 1)
    west = interface([roll(v, 1, 1) for v in mid], mid, 1, parts)
    mid = with_speed(state, 2)
    south = interface([roll(v, 1, 0) for v in mid], mid, 2, parts)
    return [jnp.where(lane == 0, 0.0, v) for v in west], [jnp.where(row == 0, 0.0, v) for v in south]


def pack_kernel(shift, rho, mx, my, out, held, shift_held, ready):
    copies = [
        pltpu.make_async_copy(source, held.at[f], ready.at[f])
        for f, source in enumerate((rho, mx, my))
    ]
    copies.append(pltpu.make_async_copy(shift, shift_held, ready.at[3]))
    for copy in copies:
        copy.start()
    for copy in copies:
        copy.wait()
    state = (held[0], held[1], held[2])
    (west,), (south,) = inner_fluxes(state, 1)
    change = roll(west, -1, 1) - west + roll(south, -1, 0) - south
    partial = state[0] - time_step * change - middle
    row = rows_of((8, COLS))
    edges = jnp.zeros((8, COLS), F32)
    for f in range(3):
        edges = jnp.where(row == f, state[f][0:1, :], edges)
        edges = jnp.where(row == 3 + f, state[f][ROWS - 1 : ROWS, :], edges)
    tall = jnp.concatenate([partial, edges, jnp.zeros((56, COLS), F32)], 0).T
    lane = lanes_of((ROWS, 128))
    low = jnp.zeros((ROWS, 128), F32)
    high = jnp.zeros((ROWS, 128), F32)
    for f in range(3):
        low = jnp.where(lane == 72 + f, state[f][:, 0:1], low)
        high = jnp.where(lane == 75 + f, state[f][:, COLS - 1 : COLS], high)
    slide = jnp.where(lax.axis_index("gx") == GX - 1, (ROWS - (shift_held[0] & (ROWS - 1))) & (ROWS - 1), 0)
    out[0:ROWS, :] = tall[0:ROWS] + low + pltpu.roll(high, slide, 0)
    out[ROWS:, :] = tall[ROWS:]


def finish_kernel(shifts, rho, mx, my, arrived, lines, rho_out, mx_out, my_out, potential):
    state = (rho[...], mx[...], my[...])
    lane = lanes_of((ROWS, COLS))
    row = rows_of((ROWS, COLS))
    west, south = inner_fluxes(state, 3)
    across = arrived[...].T[32:40]
    beside = arrived[0:ROWS, :]
    beside_high = beside
    off = jnp.broadcast_to(shifts[0:1, :], (ROWS, 128)) & (ROWS - 1)
    off = jnp.where(jnp.zeros((ROWS, 128), jnp.int32) + lax.axis_index("gx") == GX - 1, off, 0)
    for bit in range(6):
        moved = roll(beside_high, 1 << bit, 0)
        beside_high = jnp.where((off >> bit) & 1 == 1, moved, beside_high)
    new = []
    for f in range(3):
        east = jnp.where(lane == COLS - 1, beside_high[:, 41 + f : 42 + f], roll(west[f], -1, 1))
        north = jnp.where(row == ROWS - 1, across[3 + f : 4 + f, :], roll(south[f], -1, 0))
        west_f = jnp.where(lane == 0, beside[:, 38 + f : 39 + f], west[f])
        south_f = jnp.where(row == 0, across[f : f + 1, :], south[f])
        new.append(state[f] - time_step * (east - west_f + north - south_f))
    rho_out[...] = new[0]
    mx_out[...] = new[1] + time_step * 2.0 * omega_rate * state[2]
    tall = lines[...].T
    potential[:, :128] = tall[:ROWS]
    potential[:, 128:] = tall[ROWS:]
    my_out[...] = new[2] - time_step * (2.0 - shear_rate) * omega_rate * state[1]


def edge_fluxes(shifts, arrived, parts):
    narrow = lanes_of((32, 128))
    last = arrived[224:256, :]
    wrapped = turn_rows(last, wrap_hop(shifts), -1)
    last = jnp.where((narrow >= 75) & (narrow < 78), wrapped, last)
    tall = jnp.concatenate([arrived[0:224, :], last], 0).T
    lane = lanes_of((8, 256))
    upper = tall[64:72]
    before = jnp.where(lane % 32 == 0, roll(upper, -31, 1), roll(upper, 1, 1))
    south = interface(
        with_speed([before[3 + f : 4 + f] for f in range(3)], 2),
        with_speed([upper[f : f + 1] for f in range(3)], 2),
        2,
        parts,
    )
    valid = jnp.zeros((1, 256), jnp.int32) + position() < ROWS
    side = tall[72:80]
    before = roll(side, 32, 1)
    left = [before[3 + f : 4 + f] for f in range(3)]
    right = [side[f : f + 1] for f in range(3)]
    left[0] = jnp.where(valid, left[0], 1.0)
    right[0] = jnp.where(valid, right[0], 1.0)
    west = interface(with_speed(left, 1), with_speed(right, 1), 1, parts)
    west = [jnp.where(valid, v, 0.0) for v in west]
    line = lanes_of((1, 256))
    north = [jnp.where(line % 32 == 31, roll(v, 31, 1), roll(v, -1, 1)) for v in south]
    return tall, west, south, north


def forward_kernel(shifts, arrived, blocks_h, blocks_l, twist_cos, twist_sin, inner_h, inner_l, out, fluxes):
    tall, west, south, north = edge_fluxes(shifts, arrived, 3)
    rows16 = rows_of((16, 256))
    held = jnp.zeros((16, 256), F32)
    for at, value in enumerate(south + north + west + [roll(v, -32, 1) for v in west]):
        held = jnp.where(rows16 == at, value, held)
    fluxes[...] = held
    narrow = lanes_of((32, 128))
    rows8 = rows_of((8, 256))
    rows64 = rows_of((64, 256))
    density = tall[0:64]
    density = density + jnp.where(rows64 == 0, time_step * south[0], 0.0)
    density = density - jnp.where(rows64 == 63, time_step * north[0], 0.0)
    edge = jnp.where(rows8 == 0, time_step * west[0], 0.0)
    first = product_right(jnp.concatenate([density, edge], 0), blocks_h[...], blocks_l[...])
    tc = twist_cos[...]
    ts = twist_sin[...]
    re, im = first[:64, :256], first[:64, 256:]
    main = jnp.concatenate([re * tc + im * ts, im * tc - re * ts], 0)
    re, im = first[64:65, :256], first[64:65, 256:]
    here = rows64 == position()
    edge = jnp.concatenate(
        [jnp.where(here, re * tc + im * ts, 0.0), jnp.where(here, im * tc - re * ts, 0.0)], 0
    )
    head, rest = split(jnp.concatenate([main, edge], 1))
    waves = dot(inner_h[...], jnp.concatenate([head, rest], 0)) + dot(inner_l[...], head)
    rows32 = rows_of((32, 128))
    for g in range(8):
        place = 32 * (g % 4)
        pieces = []
        for start in (0, 256):
            tile = slice(start + g // 4 * 128, start + g // 4 * 128 + 128)
            real = waves[0:32, tile]
            imag = waves[32:64, tile]
            if g == 0:
                imag = jnp.where((rows32 == 0) & (narrow < 8), waves[64:65, tile], imag)
            pieces.append((real, imag))
        both = roll(pieces[1][1], 96 - place, 1)
        both = jnp.where(narrow < 96, roll(pieces[0][1], 64 - place, 1), both)
        both = jnp.where(narrow < 64, roll(pieces[1][0], 32 - place, 1), both)
        both = jnp.where(narrow < 32, roll(pieces[0][0], -place, 1), both)
        out[g * 32 : (g + 1) * 32, :] = both


def radial_kernel(
    shifts,
    arrived,
    fluxes,
    theta_cos,
    theta_sin,
    theta_cos_back,
    theta_sin_back,
    weights,
    wrap_cos,
    wrap_sin,
    groups_h,
    groups_l,
    radial_cos,
    radial_sin,
    cells,
    cells_back,
    groups_back_h,
    groups_back_l,
    return_cos,
    return_sin,
    out,
):
    shape = (256, 128)
    half = functools.partial(roll, shift=64, axis=1)

    def apart(value):
        lane = lanes_of(value.shape)
        first = jnp.zeros(value.shape, jnp.int32) + position() == 0
        value = jnp.where(lane % 64 < 32, value, 0.0)
        fifth = roll(value, -32, 1)
        slot = (lane >= 64) & (lane < 72) & first
        return jnp.where((lane >= 32) & (lane < 40), fifth, jnp.where(slot, 0.0, value))

    lane = lanes_of(shape)
    row = rows_of(shape)
    sign = jnp.where(lane < 64, 1.0, -1.0)
    value = arrived[...]
    edge = jnp.sum(value[0:ROWS], axis=0, keepdims=True)
    edge = apart(roll(jnp.broadcast_to(edge, (8, 128)), -32, 1))
    lane8 = lanes_of((8, 128))
    beside = jnp.where(lane8 % 8 == 7, roll(edge, 7, 1), roll(edge, -1, 1))
    beside = beside * wrap_cos[...] + half(beside) * wrap_sin[...]
    value = apart(value)
    value = value + jnp.where(row == 0, edge[0:1], 0.0) - jnp.where(row == 255, beside[0:1], 0.0)
    value = value * theta_cos[...] + half(value) * theta_sin[...]
    value = product_lanes(value, cells[...])
    value = value * radial_cos[...] + half(value) * radial_sin[...]
    both = product_rows(groups_h[...], groups_l[...], value)
    value = both[:256] + sign * half(both[256:])
    mean_mode = (row == 0) & (lane == 0) & (jnp.zeros(shape, jnp.int32) + position() == 0)
    value = value + jnp.where(mean_mode, middle * NX * NY, 0.0)
    value = value * weights[...]
    both = product_rows(groups_back_h[...], groups_back_l[...], value)
    value = both[:256] - sign * half(both[256:])
    value = value * return_cos[...] - half(value) * return_sin[...]
    value = product_lanes(value, cells_back[...])
    value = value * theta_cos_back[...] - half(value) * theta_sin_back[...]
    first = jnp.zeros(shape, jnp.int32) + position() == 0
    value = jnp.where((lane >= 64) & (lane < 72) & first, roll(value, 32, 1), value)
    narrow = lanes_of((32, 128))
    none = jnp.zeros((32, 128), F32)
    back = jnp.concatenate(
        [
            jnp.concatenate([none, fluxes[:, k : k + 128], none, none, none[:16]], 0).T
            for k in (0, 128)
        ],
        0,
    )
    last = back[224:256]
    wrapped = turn_rows(last, wrap_hop(shifts), 1)
    ride = [back[32 * k : 32 * k + 32] for k in range(7)]
    ride.append(jnp.where((narrow >= 41) & (narrow < 44), wrapped, last))
    blocks = [value[32 * k : 32 * k + 32] for k in range(8)]
    for bit in (1, 2, 4):
        swapped = list(blocks)
        for k in range(8):
            if k & bit == 0:
                a, b = blocks[k], blocks[k + bit]
                low = narrow & bit == 0
                swapped[k] = jnp.where(low, a, roll(b, bit, 1))
                swapped[k + bit] = jnp.where(low, roll(a, -bit, 1), b)
        blocks = swapped
    spare = (narrow >= 32) & (narrow < 44)
    for k in range(8):
        out[32 * k : 32 * k + 32, :] = jnp.where(spare, ride[k], blocks[k])


def backward_kernel(arrived, inner, back_cos, back_sin, blocks_h, blocks_l, out):
    lane = lanes_of((32, 128))
    low = lane % 64 < 32
    pairs = []
    for h in range(4):
        even = arrived[64 * h : 64 * h + 32, :]
        odd = arrived[64 * h + 32 : 64 * h + 64, :]
        pairs.append(jnp.where(low, even, roll(odd, 32, 1)))
    value = jnp.concatenate(pairs, 1)
    head, rest = split(value)
    both = dot(inner[...], jnp.concatenate([head, rest, head], 0))
    wide = lanes_of((64, 128))
    row = rows_of((64, 128))
    sign = jnp.where(wide < 64, 1.0, -1.0)
    parity = jnp.where(row % 2 == 0, 1.0, -1.0)
    turned = []
    for h in range(4):
        tile = slice(128 * h, 128 * h + 128)
        part = both[:64, tile] - sign * roll(both[64:, tile], 64, 1)
        part = part * back_cos[:, tile] - roll(part, 64, 1) * back_sin[:, tile]
        if h == 0:
            part = jnp.where((wide >= 64) & (wide < 72), parity * pairs[0][0:1, :], part)
        turned.append(part)
    head, rest = split(jnp.concatenate(turned, 1))
    full = dot(blocks_h[...], jnp.concatenate([head, rest], 0), NT)
    full = full + roll(full, 64, 1)
    full = full + dot(blocks_l[...], jnp.concatenate([head, head], 0), NT)
    square = lanes_of((128, 128))
    out[...] = jnp.where(square < 64, full[:128], full[128:])


VMEM = pl.BlockSpec(memory_space=pltpu.VMEM)
SMEM = pl.BlockSpec(memory_space=pltpu.SMEM)
HBM = pl.BlockSpec(memory_space=pltpu.HBM)


def call(kernel, shapes, *args, name, smem=0, hbm=0, scratch=(), room=32):
    many = isinstance(shapes, list)
    outs = [jax.ShapeDtypeStruct(s, F32) for s in (shapes if many else [shapes])]
    return pl.pallas_call(
        kernel,
        out_shape=outs if many else outs[0],
        in_specs=[SMEM] * smem + [HBM] * hbm + [VMEM] * (len(args) - smem - hbm),
        out_specs=[VMEM] * len(outs) if many else VMEM,
        scratch_shapes=scratch,
        name=name,
        compiler_params=pltpu.CompilerParams(vmem_limit_bytes=room * 1024 * 1024),
        cost_estimate=pl.CostEstimate(flops=100_000_000, bytes_accessed=1_000_000, transcendentals=0),
    )(*args)


def radial_tables(shift):
    shape = (256, 128)
    row = lax.broadcasted_iota(jnp.int32, shape, 0)
    lane = lax.broadcasted_iota(jnp.int32, shape, 1)
    line = lane % 64 // 8
    inside = lane % 8
    wave = lax.axis_index("gx") * 4 + line + GY * lax.axis_index("gy")
    wave = jnp.where(line < 4, wave, NY // 2)
    sigma = wave * shift % NY
    sign = jnp.where(lane < 64, 1.0, -1.0)

    def phase(cell):
        angle = (sigma * cell % (NX * NY)).astype(F32) * (2.0 * jnp.pi / (NX * NY))
        return jnp.cos(angle), jnp.sin(angle) * sign

    there = phase(row + COLS * inside)
    back = phase(row // 128 * 128 + row // 32 % 4 + 4 * (row % 32) + COLS * inside)
    n = inside + 8 * row
    n = jnp.where(n < NX // 2, n, n - NX)
    kx = 2.0 * jnp.pi / NX * (n.astype(F32) + sigma.astype(F32) / NY)
    ky = 2.0 * jnp.pi / NY * wave.astype(F32)
    size = jnp.sqrt(kx * kx + ky * ky)
    anchor = (wave == 0) & (n == 0)
    size = jnp.where(anchor, 1.0, size)
    single = (wave == 0) | (wave == NY // 2)
    scale = jnp.where(single, 1.0, 2.0) / (NX * NY)
    weights = jnp.where(anchor, 0.0, -jnp.exp(-thickness * size) / size) * scale
    angle = sigma[:8].astype(F32) * (2.0 * jnp.pi / NY)
    last = inside[:8] == 7
    wrap_cos = jnp.where(last, jnp.cos(angle), 1.0)
    wrap_sin = jnp.where(last, jnp.sin(angle) * sign[:8], 0.0)
    return *there, *back, weights, wrap_cos, wrap_sin


def shards(density, xmomentum, ymomentum, shear_shift):
    t = host_tables()
    rho, mx, my = density[0], xmomentum[0], ymomentum[0]
    shift = shear_shift[0]
    radial = lax.axis_index("gx")
    scalars = jnp.where(radial == GX - 1, shift % ROWS, 0).astype(jnp.int32).reshape(1)
    shifts = jnp.broadcast_to(shift, (8, 128))
    everyone = ("gx", "gy")
    block = (ROWS, COLS)
    table = (256, 128)
    columns = call(
        pack_kernel,
        table,
        shear_shift,
        rho,
        mx,
        my,
        name="pack",
        hbm=4,
        room=62,
        scratch=(
            pltpu.VMEM((3, *block), F32),
            pltpu.SMEM((1,), jnp.int32),
            pltpu.SemaphoreType.DMA((4,)),
        ),
    )
    columns = lax.all_to_all(columns, everyone, 0, 0, tiled=True)
    columns, tables = lax.optimization_barrier((columns, radial_tables(shift)))
    waves, fluxes = call(
        forward_kernel,
        [table, (16, 256)],
        shifts,
        columns,
        *t["blocks"],
        t["twist_cos"],
        t["twist_sin"],
        *t["inner"],
        name="forward",
    )
    waves = lax.all_to_all(waves, everyone, 0, 0, tiled=True)
    solved = call(
        radial_kernel,
        table,
        shifts,
        waves,
        fluxes,
        *tables,
        *t["groups"],
        t["radial_cos"],
        t["radial_sin"],
        t["cells"],
        t["cells_back"],
        *t["groups_back"],
        t["return_cos"],
        t["return_sin"],
        name="radial",
    )
    solved = lax.all_to_all(solved, everyone, 0, 0, tiled=True)
    lines = call(
        backward_kernel,
        (128, 128),
        solved,
        t["inner_back"],
        t["back_cos"],
        t["back_sin"],
        *t["blocks_back"],
        name="backward",
    )
    lines = lax.all_to_all(lines, "gy", 0, 0, tiled=True)
    rho_new, mx_new, my_new, potential = call(
        finish_kernel, [block] * 4, shifts, rho, mx, my, solved, lines, name="finish"
    )
    return rho_new[None], mx_new[None], my_new[None], potential[None]


def solution(mesh):
    spec = P(None, "gy", "gx")
    return jax.shard_map(
        shards,
        mesh=mesh,
        in_specs=(spec, spec, spec, P()),
        out_specs=(spec, spec, spec, spec),
        check_vma=False,
    )
```

```python
import functools

import jax
import jax.numpy as jnp
import ml_dtypes
import numpy as np
from jax import lax
from jax.experimental import pallas as pl
from jax.experimental.pallas import tpu as pltpu
from jax.sharding import PartitionSpec as P

NX = 2048
NY = 2048
ROWS = 64
COLS = 256
GX = 8
GY = 32

time_step = 0.15
omega_rate = 0.5
shear_rate = 1.5
thickness = 0.5
middle = 1.0

BF = jnp.bfloat16
F32 = jnp.float32


def halves(table):
    table = np.asarray(table, np.float32)
    head = table.astype(ml_dtypes.bfloat16)
    rest = (table - head.astype(np.float32)).astype(ml_dtypes.bfloat16)
    return head, rest


def both_parts(table):
    head, rest = halves(table)
    return np.block([[head, rest], [head, np.zeros_like(rest)]])


def turn(index, length):
    angle = 2.0 * np.pi * (np.asarray(index) % length) / length
    return np.cos(angle), np.sin(angle)


@functools.cache
def host_tables():
    out = {}
    eye8 = np.eye(8)
    cos32, sin32 = turn(np.outer(np.arange(32), np.arange(32)), 32)

    def spread(table):
        return np.einsum("jm,ab->ajmb", table, eye8).reshape(256, 256)

    out["blocks"] = halves(np.concatenate([spread(cos32), spread(-sin32)], 1))
    m1 = np.repeat(np.arange(32), 8)
    tc, ts = turn(np.outer(np.arange(64), m1), NY)
    out["twist_cos"] = tc.astype(np.float32)
    out["twist_sin"] = ts.astype(np.float32)
    c64, s64 = turn(np.outer(np.arange(32), np.arange(64)), 64)
    last = np.zeros((16, 128))
    last[0, :64] = 1.0 - 2.0 * (np.arange(64) % 2)
    head, rest = halves(
        np.concatenate([np.concatenate([c64, s64], 1), np.concatenate([-s64, c64], 1), last])
    )
    out["inner"] = np.concatenate([head, head], 1), rest
    rows = np.arange(256)
    c256, s256 = turn(np.outer(rows, rows), 256)
    out["groups"] = halves(np.concatenate([c256, s256]))
    lane = np.arange(128)
    sign = np.where(lane < 64, 1.0, -1.0)
    tc, ts = turn(np.outer(rows, lane % 8), NX)
    out["radial_cos"] = tc.astype(np.float32)
    out["radial_sin"] = (ts * sign).astype(np.float32)
    c8, s8 = turn(np.outer(np.arange(8), np.arange(8)), 8)
    lines = np.eye(8)
    ck, sk = np.kron(lines, c8), np.kron(lines, s8)
    out["cells"] = both_parts(np.block([[ck, -sk], [sk, ck]]))
    out["cells_back"] = both_parts(np.block([[ck, sk], [-sk, ck]]))
    order = rows // 128 * 128 + rows // 32 % 4 + 4 * (rows % 32)
    c256, s256 = turn(np.outer(order, rows), 256)
    out["groups_back"] = halves(np.concatenate([c256, s256]))
    tc, ts = turn(np.outer(order, lane % 8), NX)
    out["return_cos"] = tc.astype(np.float32)
    out["return_sin"] = (ts * sign).astype(np.float32)
    c64, s64 = turn(np.outer(np.arange(64), np.arange(32)), 64)
    head, rest = halves(np.concatenate([c64, s64]))
    out["inner_back"] = np.concatenate([head, head, rest], 1)
    pair = np.arange(512) // 128
    part = np.arange(512) % 128 // 64
    which = np.arange(512) % 64 // 8
    m1 = pair * 8 + which
    q = np.arange(512) % 8
    tc, ts = turn(np.outer(np.arange(64), m1), NY)
    out["back_cos"] = tc.astype(np.float32)
    out["back_sin"] = (ts * np.where(part == 0, 1.0, -1.0)).astype(np.float32)
    j = np.tile(np.repeat(np.arange(32), 4), 2)
    own = np.repeat([0, 4], 128) + np.tile(np.arange(4), 64)
    c32, s32 = turn(np.outer(j, m1), 32)
    weight = np.where(part == 0, c32, -s32)
    weight = np.where((part == 1) & (m1 == 0), 1.0, weight)
    out["blocks_back"] = halves(weight * (own[:, None] == q[None, :]))
    return out


def split(value):
    head = value.astype(BF)
    rest = (value - head.astype(F32)).astype(BF)
    return head, rest


NN = (((1,), (0,)), ((), ()))
NT = (((1,), (1,)), ((), ()))


def dot(left, right, dims=NN):
    return lax.dot_general(left, right, dims, preferred_element_type=F32)


def product_rows(table_head, table_rest, value):
    head, rest = split(value)
    both = dot(table_head, jnp.concatenate([head, rest], 1))
    return both[:, :128] + both[:, 128:] + dot(table_rest, head)


def product_lanes(value, table):
    both = dot(jnp.concatenate(split(value), 1), table)
    return both[:, :128] + both[:, 128:]


def product_right(value, table_head, table_rest):
    head, rest = split(value)
    return dot(head, table_head) + (dot(rest, table_head) + dot(head, table_rest))


def roll(value, shift, axis):
    return pltpu.roll(value, shift % value.shape[axis], axis)


def lanes_of(shape):
    return lax.broadcasted_iota(jnp.int32, shape, 1)


def rows_of(shape):
    return lax.broadcasted_iota(jnp.int32, shape, 0)


def position():
    return lax.axis_index("gx") * GY + lax.axis_index("gy")


def wrap_hop(shifts):
    row = position() & (ROWS - 1)
    shifts = jnp.broadcast_to(shifts[0:1, :], (GY, 128))
    return ((shifts >> 6) + (((shifts & (ROWS - 1)) + row) >> 6)) & (GY - 1)


def turn_rows(block, hop, way):
    for bit in range(5):
        moved = roll(block, way << bit, 0)
        block = jnp.where((hop >> bit) & 1 == 1, moved, block)
    return block


def turn_by_shift(block, shifts, way):
    off = jnp.broadcast_to(shifts[0:1, :], (ROWS, 128)) & (ROWS - 1)
    off = jnp.where(jnp.zeros((ROWS, 128), jnp.int32) + lax.axis_index("gx") == GX - 1, off, 0)
    for bit in range(6):
        moved = roll(block, way << bit, 0)
        block = jnp.where((off >> bit) & 1 == 1, moved, block)
    return block


def interface(left, right, normal, parts=3):
    speed = jnp.maximum(jnp.abs(left[3]), jnp.abs(right[3])) + 1.0
    fluxes = []
    for part in range(parts):
        f_left = left[part] * left[3]
        f_right = right[part] * right[3]
        if part == normal:
            f_left = f_left + left[0]
            f_right = f_right + right[0]
        fluxes.append(0.5 * (f_left + f_right) - 0.5 * speed * (right[part] - left[part]))
    return fluxes


def with_speed(fields, normal):
    return (*fields, fields[normal] / fields[0])


def inner_fluxes(state, parts):
    lane = lanes_of((ROWS, COLS))
    row = rows_of((ROWS, COLS))
    mid = with_speed(state, 1)
    west = interface([roll(v, 1, 1) for v in mid], mid, 1, parts)
    mid = with_speed(state, 2)
    south = interface([roll(v, 1, 0) for v in mid], mid, 2, parts)
    return [jnp.where(lane == 0, 0.0, v) for v in west], [jnp.where(row == 0, 0.0, v) for v in south]


def pack_kernel(shifts, rho, mx, my, after, out):
    del after
    state = (rho[...], mx[...], my[...])
    (west,), (south,) = inner_fluxes(state, 1)
    change = roll(west, -1, 1) - west + roll(south, -1, 0) - south
    partial = state[0] - time_step * change - middle
    row = rows_of((8, COLS))
    edges = jnp.zeros((8, COLS), F32)
    for f in range(3):
        edges = jnp.where(row == f, state[f][0:1, :], edges)
        edges = jnp.where(row == 3 + f, state[f][ROWS - 1 : ROWS, :], edges)
    tall = jnp.concatenate([partial, edges, jnp.zeros((56, COLS), F32)], 0).T
    lane = lanes_of((ROWS, 128))
    low = jnp.zeros((ROWS, 128), F32)
    high = jnp.zeros((ROWS, 128), F32)
    for f in range(3):
        low = jnp.where(lane == 72 + f, state[f][:, 0:1], low)
        high = jnp.where(lane == 75 + f, state[f][:, COLS - 1 : COLS], high)
    out[0:ROWS, :] = tall[0:ROWS] + low + turn_by_shift(high, shifts, -1)
    out[ROWS:, :] = tall[ROWS:]


def finish_kernel(shifts, rho, mx, my, arrived, lines, rho_out, mx_out, my_out, potential):
    state = (rho[...], mx[...], my[...])
    lane = lanes_of((ROWS, COLS))
    row = rows_of((ROWS, COLS))
    west, south = inner_fluxes(state, 3)
    across = arrived[...].T[32:40]
    beside = arrived[0:ROWS, :]
    beside_high = turn_by_shift(beside, shifts, 1)
    new = []
    for f in range(3):
        east = jnp.where(lane == COLS - 1, beside_high[:, 41 + f : 42 + f], roll(west[f], -1, 1))
        north = jnp.where(row == ROWS - 1, across[3 + f : 4 + f, :], roll(south[f], -1, 0))
        west_f = jnp.where(lane == 0, beside[:, 38 + f : 39 + f], west[f])
        south_f = jnp.where(row == 0, across[f : f + 1, :], south[f])
        new.append(state[f] - time_step * (east - west_f + north - south_f))
    rho_out[...] = new[0]
    mx_out[...] = new[1] + time_step * 2.0 * omega_rate * state[2]
    tall = lines[...].T
    potential[:, :128] = tall[:ROWS]
    potential[:, 128:] = tall[ROWS:]
    my_out[...] = new[2] - time_step * (2.0 - shear_rate) * omega_rate * state[1]


def circle(turns):
    quarter = jnp.floor(turns * 4.0 + 0.5)
    x = (turns - quarter * 0.25) * (2.0 * np.pi)
    y = x * x
    s = x * (1.0 + y * (-1 / 6 + y * (1 / 120 + y * (-1 / 5040 + y * (1 / 362880)))))
    c = 1.0 + y * (-1 / 2 + y * (1 / 24 + y * (-1 / 720 + y * (1 / 40320 - y * (1 / 3628800)))))
    k = quarter.astype(jnp.int32)
    swap = k & 1 == 1
    sine = jnp.where(swap, c, s)
    cosine = jnp.where(swap, s, c)
    return jnp.where((k + 1) & 2 == 2, -cosine, cosine), jnp.where(k & 2 == 2, -sine, sine)


def tables_kernel(shifts, there_cos, there_sin, back_cos, back_sin, weights, wrap_cos, wrap_sin):
    def line_of(shape):
        lane = lanes_of(shape)
        line = (lane & 63) >> 3
        wave = lax.axis_index("gx") * 4 + line + GY * lax.axis_index("gy")
        return lane, jnp.where(line < 4, wave, NY // 2)

    lane, wave = line_of((8, 128))
    sigma = ((wave * shifts[...]) & (NY - 1)).astype(F32)[0:1]
    sign = jnp.where(lane < 64, 1.0, -1.0)[0:1]

    def phase(rows, of_row, of_lane):
        shape = (rows, 128)
        cell = of_row(rows_of(shape)) + of_lane * COLS * (lanes_of(shape) & 7)
        return circle(sigma * cell.astype(F32) * (1.0 / (NX * NY)))

    def fill(cos_out, sin_out, coarse, fine):
        c1, s1 = coarse
        c2, s2 = fine
        size = c2.shape[0]
        for k in range(256 // size):
            at = slice(k * size, k * size + size)
            ck, sk = c1[k : k + 1], s1[k : k + 1]
            cos_out[at, :] = ck * c2 - sk * s2
            sin_out[at, :] = (sk * c2 + ck * s2) * sign

    fill(there_cos, there_sin, phase(16, lambda r: 16 * r, 0), phase(16, lambda r: r, 1))
    fill(
        back_cos,
        back_sin,
        phase(8, lambda r: (r >> 2) * 128 + (r & 3), 0),
        phase(32, lambda r: 4 * r, 1),
    )
    shape = (256, 128)
    lane, wave = line_of(shape)
    n = (lane & 7) + 8 * rows_of(shape)
    n = jnp.where(n < NX // 2, n, n - NX)
    kx = 2.0 * np.pi / NX * (n.astype(F32) + sigma * (1.0 / NY))
    ky = 2.0 * np.pi / NY * wave.astype(F32)
    size = jnp.sqrt(kx * kx + ky * ky)
    anchor = (wave == 0) & (n == 0)
    size = jnp.where(anchor, 1.0, size)
    single = (wave == 0) | (wave == NY // 2)
    scale = jnp.where(single, 1.0, 2.0) / (NX * NY)
    weights[...] = jnp.where(anchor, 0.0, -jnp.exp(-thickness * size) / size) * scale
    c, s = circle(jnp.broadcast_to(sigma * (1.0 / NY), (8, 128)))
    last = lanes_of((8, 128)) & 7 == 7
    wrap_cos[...] = jnp.where(last, c, 1.0)
    wrap_sin[...] = jnp.where(last, s * sign, 0.0)


def edge_fluxes(shifts, arrived, parts):
    narrow = lanes_of((32, 128))
    last = arrived[224:256, :]
    wrapped = turn_rows(last, wrap_hop(shifts), -1)
    last = jnp.where((narrow >= 75) & (narrow < 78), wrapped, last)
    tall = jnp.concatenate([arrived[0:224, :], last], 0).T
    lane = lanes_of((8, 256))
    upper = tall[64:72]
    before = jnp.where(lane % 32 == 0, roll(upper, -31, 1), roll(upper, 1, 1))
    south = interface(
        with_speed([before[3 + f : 4 + f] for f in range(3)], 2),
        with_speed([upper[f : f + 1] for f in range(3)], 2),
        2,
        parts,
    )
    valid = jnp.zeros((1, 256), jnp.int32) + position() < ROWS
    side = tall[72:80]
    before = roll(side, 32, 1)
    left = [before[3 + f : 4 + f] for f in range(3)]
    right = [side[f : f + 1] for f in range(3)]
    left[0] = jnp.where(valid, left[0], 1.0)
    right[0] = jnp.where(valid, right[0], 1.0)
    west = interface(with_speed(left, 1), with_speed(right, 1), 1, parts)
    west = [jnp.where(valid, v, 0.0) for v in west]
    line = lanes_of((1, 256))
    north = [jnp.where(line % 32 == 31, roll(v, 31, 1), roll(v, -1, 1)) for v in south]
    return tall, west, south, north


def forward_kernel(shifts, arrived, blocks_h, blocks_l, twist_cos, twist_sin, inner_h, inner_l, out, fluxes):
    tall, west, south, north = edge_fluxes(shifts, arrived, 3)
    rows16 = rows_of((16, 256))
    held = jnp.zeros((16, 256), F32)
    for at, value in enumerate(south + north + west + [roll(v, -32, 1) for v in west]):
        held = jnp.where(rows16 == at, value, held)
    fluxes[...] = held
    narrow = lanes_of((32, 128))
    rows64 = rows_of((64, 256))
    density = tall[0:64]
    density = density + jnp.where(rows64 == 0, time_step * south[0], 0.0)
    density = density - jnp.where(rows64 == 63, time_step * north[0], 0.0)
    edge = jnp.where(rows16 == 0, time_step * west[0], 0.0)
    first = product_right(jnp.concatenate([density, edge], 0), blocks_h[...], blocks_l[...])
    tc = twist_cos[...]
    ts = twist_sin[...]
    re, im = first[:64, :256], first[:64, 256:]
    main = jnp.concatenate([re * tc + im * ts, im * tc - re * ts], 0)
    re, im = first[64:65, :256], first[64:65, 256:]
    here = rows64 == position()
    edge = jnp.concatenate(
        [jnp.where(here, re * tc + im * ts, 0.0), jnp.where(here, im * tc - re * ts, 0.0)], 0
    )
    head, rest = split(jnp.concatenate([main, edge], 1))
    waves = dot(inner_h[...], jnp.concatenate([head, rest], 0)) + dot(inner_l[...], head)
    rows32 = rows_of((32, 128))
    for g in range(8):
        place = 32 * (g % 4)
        pieces = []
        for start in (0, 256):
            tile = slice(start + g // 4 * 128, start + g // 4 * 128 + 128)
            real = waves[0:32, tile]
            imag = waves[32:64, tile]
            if g == 0:
                imag = jnp.where((rows32 == 0) & (narrow < 8), waves[64:65, tile], imag)
            pieces.append((real, imag))
        both = roll(pieces[1][1], 96 - place, 1)
        both = jnp.where(narrow < 96, roll(pieces[0][1], 64 - place, 1), both)
        both = jnp.where(narrow < 64, roll(pieces[1][0], 32 - place, 1), both)
        both = jnp.where(narrow < 32, roll(pieces[0][0], -place, 1), both)
        out[g * 32 : (g + 1) * 32, :] = both


def radial_kernel(
    shifts,
    arrived,
    fluxes,
    theta_cos,
    theta_sin,
    theta_cos_back,
    theta_sin_back,
    weights,
    wrap_cos,
    wrap_sin,
    groups_h,
    groups_l,
    radial_cos,
    radial_sin,
    cells,
    cells_back,
    groups_back_h,
    groups_back_l,
    return_cos,
    return_sin,
    out,
):
    shape = (256, 128)
    half = functools.partial(roll, shift=64, axis=1)

    def apart(value):
        lane = lanes_of(value.shape)
        first = jnp.zeros(value.shape, jnp.int32) + position() == 0
        value = jnp.where(lane % 64 < 32, value, 0.0)
        fifth = roll(value, -32, 1)
        slot = (lane >= 64) & (lane < 72) & first
        return jnp.where((lane >= 32) & (lane < 40), fifth, jnp.where(slot, 0.0, value))

    lane = lanes_of(shape)
    row = rows_of(shape)
    sign = jnp.where(lane < 64, 1.0, -1.0)
    value = arrived[...]
    edge = jnp.sum(value[0:ROWS], axis=0, keepdims=True)
    edge = apart(roll(jnp.broadcast_to(edge, (8, 128)), -32, 1))
    lane8 = lanes_of((8, 128))
    beside = jnp.where(lane8 % 8 == 7, roll(edge, 7, 1), roll(edge, -1, 1))
    beside = beside * wrap_cos[...] + half(beside) * wrap_sin[...]
    value = apart(value)
    value = value + jnp.where(row == 0, edge[0:1], 0.0) - jnp.where(row == 255, beside[0:1], 0.0)
    value = value * theta_cos[...] + half(value) * theta_sin[...]
    value = product_lanes(value, cells[...])
    value = value * radial_cos[...] + half(value) * radial_sin[...]
    both = product_rows(groups_h[...], groups_l[...], value)
    value = both[:256] + sign * half(both[256:])
    mean_mode = (row == 0) & (lane == 0) & (jnp.zeros(shape, jnp.int32) + position() == 0)
    value = value + jnp.where(mean_mode, middle * NX * NY, 0.0)
    value = value * weights[...]
    both = product_rows(groups_back_h[...], groups_back_l[...], value)
    value = both[:256] - sign * half(both[256:])
    value = value * return_cos[...] - half(value) * return_sin[...]
    value = product_lanes(value, cells_back[...])
    value = value * theta_cos_back[...] - half(value) * theta_sin_back[...]
    first = jnp.zeros(shape, jnp.int32) + position() == 0
    value = jnp.where((lane >= 64) & (lane < 72) & first, roll(value, 32, 1), value)
    narrow = lanes_of((32, 128))
    none = jnp.zeros((32, 128), F32)
    back = jnp.concatenate(
        [
            jnp.concatenate([none, fluxes[:, k : k + 128], none, none, none[:16]], 0).T
            for k in (0, 128)
        ],
        0,
    )
    last = back[224:256]
    wrapped = turn_rows(last, wrap_hop(shifts), 1)
    ride = [back[32 * k : 32 * k + 32] for k in range(7)]
    ride.append(jnp.where((narrow >= 41) & (narrow < 44), wrapped, last))
    blocks = [value[32 * k : 32 * k + 32] for k in range(8)]
    for bit in (1, 2, 4):
        swapped = list(blocks)
        for k in range(8):
            if k & bit == 0:
                a, b = blocks[k], blocks[k + bit]
                low = narrow & bit == 0
                swapped[k] = jnp.where(low, a, roll(b, bit, 1))
                swapped[k + bit] = jnp.where(low, roll(a, -bit, 1), b)
        blocks = swapped
    spare = (narrow >= 32) & (narrow < 44)
    for k in range(8):
        out[32 * k : 32 * k + 32, :] = jnp.where(spare, ride[k], blocks[k])


def backward_kernel(arrived, inner, back_cos, back_sin, blocks_h, blocks_l, out):
    lane = lanes_of((32, 128))
    low = lane % 64 < 32
    pairs = []
    for h in range(4):
        even = arrived[64 * h : 64 * h + 32, :]
        odd = arrived[64 * h + 32 : 64 * h + 64, :]
        pairs.append(jnp.where(low, even, roll(odd, 32, 1)))
    value = jnp.concatenate(pairs, 1)
    head, rest = split(value)
    both = dot(inner[...], jnp.concatenate([head, rest, head], 0))
    wide = lanes_of((64, 128))
    row = rows_of((64, 128))
    sign = jnp.where(wide < 64, 1.0, -1.0)
    parity = jnp.where(row % 2 == 0, 1.0, -1.0)
    turned = []
    for h in range(4):
        tile = slice(128 * h, 128 * h + 128)
        part = both[:64, tile] - sign * roll(both[64:, tile], 64, 1)
        part = part * back_cos[:, tile] - roll(part, 64, 1) * back_sin[:, tile]
        if h == 0:
            part = jnp.where((wide >= 64) & (wide < 72), parity * pairs[0][0:1, :], part)
        turned.append(part)
    head, rest = split(jnp.concatenate(turned, 1))
    full = dot(blocks_h[...], jnp.concatenate([head, rest], 0), NT)
    full = full + roll(full, 64, 1)
    full = full + dot(blocks_l[...], jnp.concatenate([head, head], 0), NT)
    square = lanes_of((128, 128))
    out[...] = jnp.where(square < 64, full[:128], full[128:])


VMEM = pl.BlockSpec(memory_space=pltpu.VMEM)


def call(kernel, shapes, *args, name):
    many = isinstance(shapes, list)
    outs = [jax.ShapeDtypeStruct(s, F32) for s in (shapes if many else [shapes])]
    return pl.pallas_call(
        kernel,
        out_shape=outs if many else outs[0],
        in_specs=[VMEM] * len(args),
        out_specs=[VMEM] * len(outs) if many else VMEM,
        name=name,
        compiler_params=pltpu.CompilerParams(vmem_limit_bytes=32 * 1024 * 1024),
        cost_estimate=pl.CostEstimate(
            flops=20_000_000_000, bytes_accessed=1_000_000, transcendentals=0
        ),
    )(*args)


def shards(density, xmomentum, ymomentum, shear_shift):
    t = host_tables()
    rho, mx, my = density[0], xmomentum[0], ymomentum[0]
    shifts = jnp.broadcast_to(shear_shift[0], (8, 128))
    everyone = ("gx", "gy")
    block = (ROWS, COLS)
    table = (256, 128)
    small = (8, 128)
    tables = call(tables_kernel, [table] * 5 + [small] * 2, shifts, name="tables")
    columns = call(pack_kernel, table, shifts, rho, mx, my, tables[-1], name="pack")
    columns = lax.all_to_all(columns, everyone, 0, 0, tiled=True)
    waves, fluxes = call(
        forward_kernel,
        [table, (16, 256)],
        shifts,
        columns,
        *t["blocks"],
        t["twist_cos"],
        t["twist_sin"],
        *t["inner"],
        name="forward",
    )
    waves = lax.all_to_all(waves, everyone, 0, 0, tiled=True)
    solved = call(
        radial_kernel,
        table,
        shifts,
        waves,
        fluxes,
        *tables,
        *t["groups"],
        t["radial_cos"],
        t["radial_sin"],
        t["cells"],
        t["cells_back"],
        *t["groups_back"],
        t["return_cos"],
        t["return_sin"],
        name="radial",
    )
    solved = lax.all_to_all(solved, everyone, 0, 0, tiled=True)
    lines = call(
        backward_kernel,
        (128, 128),
        solved,
        t["inner_back"],
        t["back_cos"],
        t["back_sin"],
        *t["blocks_back"],
        name="backward",
    )
    lines = lax.all_to_all(lines, "gy", 0, 0, tiled=True)
    rho_new, mx_new, my_new, potential = call(
        finish_kernel, [block] * 4, shifts, rho, mx, my, solved, lines, name="finish"
    )
    return rho_new[None], mx_new[None], my_new[None], potential[None]


def solution(mesh):
    spec = P(None, "gy", "gx")
    return jax.shard_map(
        shards,
        mesh=mesh,
        in_specs=(spec, spec, spec, P()),
        out_specs=(spec, spec, spec, spec),
        check_vma=False,
    )
```

```python
import functools

import jax
import jax.numpy as jnp
import ml_dtypes
import numpy as np
from jax import lax
from jax.experimental import pallas as pl
from jax.experimental.pallas import tpu as pltpu
from jax.sharding import PartitionSpec as P

NX = 2048
NY = 2048
ROWS = 64
COLS = 256
GX = 8
GY = 32

time_step = 0.15
omega_rate = 0.5
shear_rate = 1.5
thickness = 0.5
middle = 1.0

BF = jnp.bfloat16
F32 = jnp.float32


def halves(table):
    table = np.asarray(table, np.float32)
    head = table.astype(ml_dtypes.bfloat16)
    rest = (table - head.astype(np.float32)).astype(ml_dtypes.bfloat16)
    return head, rest


def both_parts(table):
    head, rest = halves(table)
    return np.block([[head, rest], [head, np.zeros_like(rest)]])


def turn(index, length):
    angle = 2.0 * np.pi * (np.asarray(index) % length) / length
    return np.cos(angle), np.sin(angle)


@functools.cache
def host_tables():
    out = {}
    eye8 = np.eye(8)
    cos32, sin32 = turn(np.outer(np.arange(32), np.arange(32)), 32)

    def spread(table):
        return np.einsum("jm,ab->ajmb", table, eye8).reshape(256, 256)

    out["blocks"] = halves(np.concatenate([spread(cos32), spread(-sin32)], 1))
    m1 = np.repeat(np.arange(32), 8)
    tc, ts = turn(np.outer(np.arange(64), m1), NY)
    out["twist_cos"] = tc.astype(np.float32)
    out["twist_sin"] = ts.astype(np.float32)
    c64, s64 = turn(np.outer(np.arange(32), np.arange(64)), 64)
    last = np.zeros((16, 128))
    last[0, :64] = 1.0 - 2.0 * (np.arange(64) % 2)
    head, rest = halves(
        np.concatenate([np.concatenate([c64, s64], 1), np.concatenate([-s64, c64], 1), last])
    )
    out["inner"] = np.concatenate([head, head], 1), rest
    rows = np.arange(256)
    c256, s256 = turn(np.outer(rows, rows), 256)
    out["groups"] = halves(np.concatenate([c256, s256]))
    lane = np.arange(128)
    sign = np.where(lane < 64, 1.0, -1.0)
    tc, ts = turn(np.outer(rows, lane % 8), NX)
    out["radial_cos"] = tc.astype(np.float32)
    out["radial_sin"] = (ts * sign).astype(np.float32)
    c8, s8 = turn(np.outer(np.arange(8), np.arange(8)), 8)
    lines = np.eye(8)
    ck, sk = np.kron(lines, c8), np.kron(lines, s8)
    out["cells"] = both_parts(np.block([[ck, -sk], [sk, ck]]))
    out["cells_back"] = both_parts(np.block([[ck, sk], [-sk, ck]]))
    order = rows // 128 * 128 + rows // 32 % 4 + 4 * (rows % 32)
    c256, s256 = turn(np.outer(order, rows), 256)
    out["groups_back"] = halves(np.concatenate([c256, s256]))
    tc, ts = turn(np.outer(order, lane % 8), NX)
    out["return_cos"] = tc.astype(np.float32)
    out["return_sin"] = (ts * sign).astype(np.float32)
    c64, s64 = turn(np.outer(np.arange(64), np.arange(32)), 64)
    head, rest = halves(np.concatenate([c64, s64]))
    out["inner_back"] = np.concatenate([head, head, rest], 1)
    pair = np.arange(512) // 128
    part = np.arange(512) % 128 // 64
    which = np.arange(512) % 64 // 8
    m1 = pair * 8 + which
    q = np.arange(512) % 8
    tc, ts = turn(np.outer(np.arange(64), m1), NY)
    out["back_cos"] = tc.astype(np.float32)
    out["back_sin"] = (ts * np.where(part == 0, 1.0, -1.0)).astype(np.float32)
    j = np.tile(np.repeat(np.arange(32), 4), 2)
    own = np.repeat([0, 4], 128) + np.tile(np.arange(4), 64)
    c32, s32 = turn(np.outer(j, m1), 32)
    weight = np.where(part == 0, c32, -s32)
    weight = np.where((part == 1) & (m1 == 0), 1.0, weight)
    out["blocks_back"] = halves(weight * (own[:, None] == q[None, :]))
    return out


def split(value):
    head = value.astype(BF)
    rest = (value - head.astype(F32)).astype(BF)
    return head, rest


NN = (((1,), (0,)), ((), ()))
NT = (((1,), (1,)), ((), ()))


def dot(left, right, dims=NN):
    return lax.dot_general(left, right, dims, preferred_element_type=F32)


def product_rows(table_head, table_rest, value):
    head, rest = split(value)
    both = dot(table_head, jnp.concatenate([head, rest], 1))
    return both[:, :128] + both[:, 128:] + dot(table_rest, head)


def product_lanes(value, table):
    both = dot(jnp.concatenate(split(value), 1), table)
    return both[:, :128] + both[:, 128:]


def product_right(value, table_head, table_rest):
    head, rest = split(value)
    return dot(head, table_head) + (dot(rest, table_head) + dot(head, table_rest))


def roll(value, shift, axis):
    return pltpu.roll(value, shift % value.shape[axis], axis)


def lanes_of(shape):
    return lax.broadcasted_iota(jnp.int32, shape, 1)


def rows_of(shape):
    return lax.broadcasted_iota(jnp.int32, shape, 0)


def position():
    return lax.axis_index("gx") * GY + lax.axis_index("gy")


def wrap_hop(shifts):
    row = position() & (ROWS - 1)
    shifts = jnp.broadcast_to(shifts[0:1, :], (GY, 128))
    return ((shifts >> 6) + (((shifts & (ROWS - 1)) + row) >> 6)) & (GY - 1)


def turn_rows(block, hop, way):
    for bit in range(5):
        moved = roll(block, way << bit, 0)
        block = jnp.where((hop >> bit) & 1 == 1, moved, block)
    return block


def turn_by_shift(block, shifts, way):
    off = jnp.broadcast_to(shifts[0:1, :], (ROWS, 128)) & (ROWS - 1)
    off = jnp.where(jnp.zeros((ROWS, 128), jnp.int32) + lax.axis_index("gx") == GX - 1, off, 0)
    for bit in range(6):
        moved = roll(block, way << bit, 0)
        block = jnp.where((off >> bit) & 1 == 1, moved, block)
    return block


def interface(left, right, normal, parts=3):
    speed = jnp.maximum(jnp.abs(left[3]), jnp.abs(right[3])) + 1.0
    fluxes = []
    for part in range(parts):
        f_left = left[part] * left[3]
        f_right = right[part] * right[3]
        if part == normal:
            f_left = f_left + left[0]
            f_right = f_right + right[0]
        fluxes.append(0.5 * (f_left + f_right) - 0.5 * speed * (right[part] - left[part]))
    return fluxes


def with_speed(fields, normal):
    return (*fields, fields[normal] / fields[0])


def inner_fluxes(state, parts):
    lane = lanes_of((ROWS, COLS))
    row = rows_of((ROWS, COLS))
    mid = with_speed(state, 1)
    west = interface([roll(v, 1, 1) for v in mid], mid, 1, parts)
    mid = with_speed(state, 2)
    south = interface([roll(v, 1, 0) for v in mid], mid, 2, parts)
    return [jnp.where(lane == 0, 0.0, v) for v in west], [jnp.where(row == 0, 0.0, v) for v in south]


def pack_kernel(shifts, rho, mx, my, after, out):
    del after
    state = (rho[...], mx[...], my[...])
    (west,), (south,) = inner_fluxes(state, 1)
    change = roll(west, -1, 1) - west + roll(south, -1, 0) - south
    partial = state[0] - time_step * change - middle
    row = rows_of((8, COLS))
    edges = jnp.zeros((8, COLS), F32)
    for f in range(3):
        edges = jnp.where(row == f, state[f][0:1, :], edges)
        edges = jnp.where(row == 3 + f, state[f][ROWS - 1 : ROWS, :], edges)
    tall = jnp.concatenate([partial, edges, jnp.zeros((56, COLS), F32)], 0).T
    lane = lanes_of((ROWS, 128))
    low = jnp.zeros((ROWS, 128), F32)
    high = jnp.zeros((ROWS, 128), F32)
    for f in range(3):
        low = jnp.where(lane == 72 + f, state[f][:, 0:1], low)
        high = jnp.where(lane == 75 + f, state[f][:, COLS - 1 : COLS], high)
    out[0:ROWS, :] = tall[0:ROWS] + low + turn_by_shift(high, shifts, -1)
    out[ROWS:, :] = tall[ROWS:]


def finish_kernel(shifts, rho, mx, my, arrived, lines, rho_out, mx_out, my_out, potential):
    state = (rho[...], mx[...], my[...])
    lane = lanes_of((ROWS, COLS))
    row = rows_of((ROWS, COLS))
    west, south = inner_fluxes(state, 3)
    across = arrived[...].T[32:40]
    beside = arrived[0:ROWS, :]
    beside_high = turn_by_shift(beside, shifts, 1)
    new = []
    for f in range(3):
        east = jnp.where(lane == COLS - 1, beside_high[:, 41 + f : 42 + f], roll(west[f], -1, 1))
        north = jnp.where(row == ROWS - 1, across[3 + f : 4 + f, :], roll(south[f], -1, 0))
        west_f = jnp.where(lane == 0, beside[:, 38 + f : 39 + f], west[f])
        south_f = jnp.where(row == 0, across[f : f + 1, :], south[f])
        new.append(state[f] - time_step * (east - west_f + north - south_f))
    rho_out[...] = new[0]
    mx_out[...] = new[1] + time_step * 2.0 * omega_rate * state[2]
    tall = lines[...].T
    potential[:, :128] = tall[:ROWS]
    potential[:, 128:] = tall[ROWS:]
    my_out[...] = new[2] - time_step * (2.0 - shear_rate) * omega_rate * state[1]


def circle(turns):
    quarter = jnp.floor(turns * 4.0 + 0.5)
    x = (turns - quarter * 0.25) * (2.0 * np.pi)
    y = x * x
    s = x * (1.0 + y * (-1 / 6 + y * (1 / 120 + y * (-1 / 5040 + y * (1 / 362880)))))
    c = 1.0 + y * (-1 / 2 + y * (1 / 24 + y * (-1 / 720 + y * (1 / 40320 - y * (1 / 3628800)))))
    k = quarter.astype(jnp.int32)
    swap = k & 1 == 1
    sine = jnp.where(swap, c, s)
    cosine = jnp.where(swap, s, c)
    return jnp.where((k + 1) & 2 == 2, -cosine, cosine), jnp.where(k & 2 == 2, -sine, sine)


def waves_kernel(waves):
    line = (lanes_of((8, 128)) & 63) >> 3
    wave = lax.axis_index("gx") * 4 + line + GY * lax.axis_index("gy")
    waves[...] = jnp.where(line < 4, wave, NY // 2)


def tables_kernel(
    shifts, waves, there_cos, there_sin, back_cos, back_sin, weights, wrap_cos, wrap_sin
):
    lane = lanes_of((8, 128))
    sigma = ((waves[...] * shifts[...]) & (NY - 1)).astype(F32)[0:1]
    sign = jnp.where(lane < 64, 1.0, -1.0)[0:1]

    def phase(rows, of_row, of_lane):
        shape = (rows, 128)
        cell = of_row(rows_of(shape)) + of_lane * COLS * (lanes_of(shape) & 7)
        return circle(sigma * cell.astype(F32) * (1.0 / (NX * NY)))

    def fill(cos_out, sin_out, coarse, fine):
        c1, s1 = coarse
        c2, s2 = fine
        size = c2.shape[0]
        for k in range(256 // size):
            at = slice(k * size, k * size + size)
            ck, sk = c1[k : k + 1], s1[k : k + 1]
            cos_out[at, :] = ck * c2 - sk * s2
            sin_out[at, :] = (sk * c2 + ck * s2) * sign

    fill(there_cos, there_sin, phase(16, lambda r: 16 * r, 0), phase(16, lambda r: r, 1))
    fill(
        back_cos,
        back_sin,
        phase(8, lambda r: (r >> 2) * 128 + (r & 3), 0),
        phase(32, lambda r: 4 * r, 1),
    )
    shape = (256, 128)
    lane = lanes_of(shape)
    wave = jnp.broadcast_to(waves[0:1, :], shape)
    n = (lane & 7) + 8 * rows_of(shape)
    n = jnp.where(n < NX // 2, n, n - NX)
    kx = 2.0 * np.pi / NX * (n.astype(F32) + sigma * (1.0 / NY))
    ky = 2.0 * np.pi / NY * wave.astype(F32)
    size = jnp.sqrt(kx * kx + ky * ky)
    anchor = (wave == 0) & (n == 0)
    size = jnp.where(anchor, 1.0, size)
    single = (wave == 0) | (wave == NY // 2)
    scale = jnp.where(single, 1.0, 2.0) / (NX * NY)
    weights[...] = jnp.where(anchor, 0.0, -jnp.exp(-thickness * size) / size) * scale
    c, s = circle(jnp.broadcast_to(sigma * (1.0 / NY), (8, 128)))
    last = lanes_of((8, 128)) & 7 == 7
    wrap_cos[...] = jnp.where(last, c, 1.0)
    wrap_sin[...] = jnp.where(last, s * sign, 0.0)


def edge_fluxes(shifts, arrived, parts):
    narrow = lanes_of((32, 128))
    last = arrived[224:256, :]
    wrapped = turn_rows(last, wrap_hop(shifts), -1)
    last = jnp.where((narrow >= 75) & (narrow < 78), wrapped, last)
    tall = jnp.concatenate([arrived[0:224, :], last], 0).T
    lane = lanes_of((8, 256))
    upper = tall[64:72]
    before = jnp.where(lane % 32 == 0, roll(upper, -31, 1), roll(upper, 1, 1))
    south = interface(
        with_speed([before[3 + f : 4 + f] for f in range(3)], 2),
        with_speed([upper[f : f + 1] for f in range(3)], 2),
        2,
        parts,
    )
    valid = jnp.zeros((1, 256), jnp.int32) + position() < ROWS
    side = tall[72:80]
    before = roll(side, 32, 1)
    left = [before[3 + f : 4 + f] for f in range(3)]
    right = [side[f : f + 1] for f in range(3)]
    left[0] = jnp.where(valid, left[0], 1.0)
    right[0] = jnp.where(valid, right[0], 1.0)
    west = interface(with_speed(left, 1), with_speed(right, 1), 1, parts)
    west = [jnp.where(valid, v, 0.0) for v in west]
    line = lanes_of((1, 256))
    north = [jnp.where(line % 32 == 31, roll(v, 31, 1), roll(v, -1, 1)) for v in south]
    return tall, west, south, north


def forward_kernel(shifts, arrived, blocks_h, blocks_l, twist_cos, twist_sin, inner_h, inner_l, out, fluxes):
    tall, west, south, north = edge_fluxes(shifts, arrived, 3)
    rows16 = rows_of((16, 256))
    held = jnp.zeros((16, 256), F32)
    for at, value in enumerate(south + north + west + [roll(v, -32, 1) for v in west]):
        held = jnp.where(rows16 == at, value, held)
    fluxes[...] = held
    narrow = lanes_of((32, 128))
    rows64 = rows_of((64, 256))
    density = tall[0:64]
    density = density + jnp.where(rows64 == 0, time_step * south[0], 0.0)
    density = density - jnp.where(rows64 == 63, time_step * north[0], 0.0)
    edge = jnp.where(rows16 == 0, time_step * west[0], 0.0)
    first = product_right(jnp.concatenate([density, edge], 0), blocks_h[...], blocks_l[...])
    tc = twist_cos[...]
    ts = twist_sin[...]
    re, im = first[:64, :256], first[:64, 256:]
    main = jnp.concatenate([re * tc + im * ts, im * tc - re * ts], 0)
    re, im = first[64:65, :256], first[64:65, 256:]
    here = rows64 == position()
    edge = jnp.concatenate(
        [jnp.where(here, re * tc + im * ts, 0.0), jnp.where(here, im * tc - re * ts, 0.0)], 0
    )
    head, rest = split(jnp.concatenate([main, edge], 1))
    waves = dot(inner_h[...], jnp.concatenate([head, rest], 0)) + dot(inner_l[...], head)
    rows32 = rows_of((32, 128))
    for g in range(8):
        place = 32 * (g % 4)
        pieces = []
        for start in (0, 256):
            tile = slice(start + g // 4 * 128, start + g // 4 * 128 + 128)
            real = waves[0:32, tile]
            imag = waves[32:64, tile]
            if g == 0:
                imag = jnp.where((rows32 == 0) & (narrow < 8), waves[64:65, tile], imag)
            pieces.append((real, imag))
        both = roll(pieces[1][1], 96 - place, 1)
        both = jnp.where(narrow < 96, roll(pieces[0][1], 64 - place, 1), both)
        both = jnp.where(narrow < 64, roll(pieces[1][0], 32 - place, 1), both)
        both = jnp.where(narrow < 32, roll(pieces[0][0], -place, 1), both)
        out[g * 32 : (g + 1) * 32, :] = both


def radial_kernel(
    shifts,
    arrived,
    fluxes,
    theta_cos,
    theta_sin,
    theta_cos_back,
    theta_sin_back,
    weights,
    wrap_cos,
    wrap_sin,
    groups_h,
    groups_l,
    radial_cos,
    radial_sin,
    cells,
    cells_back,
    groups_back_h,
    groups_back_l,
    return_cos,
    return_sin,
    out,
):
    shape = (256, 128)
    half = functools.partial(roll, shift=64, axis=1)

    def apart(value):
        lane = lanes_of(value.shape)
        first = jnp.zeros(value.shape, jnp.int32) + position() == 0
        value = jnp.where(lane % 64 < 32, value, 0.0)
        fifth = roll(value, -32, 1)
        slot = (lane >= 64) & (lane < 72) & first
        return jnp.where((lane >= 32) & (lane < 40), fifth, jnp.where(slot, 0.0, value))

    lane = lanes_of(shape)
    row = rows_of(shape)
    sign = jnp.where(lane < 64, 1.0, -1.0)
    value = arrived[...]
    edge = jnp.sum(value[0:ROWS], axis=0, keepdims=True)
    edge = apart(roll(jnp.broadcast_to(edge, (8, 128)), -32, 1))
    lane8 = lanes_of((8, 128))
    beside = jnp.where(lane8 % 8 == 7, roll(edge, 7, 1), roll(edge, -1, 1))
    beside = beside * wrap_cos[...] + half(beside) * wrap_sin[...]
    value = apart(value)
    value = value + jnp.where(row == 0, edge[0:1], 0.0) - jnp.where(row == 255, beside[0:1], 0.0)
    value = value * theta_cos[...] + half(value) * theta_sin[...]
    value = product_lanes(value, cells[...])
    value = value * radial_cos[...] + half(value) * radial_sin[...]
    both = product_rows(groups_h[...], groups_l[...], value)
    value = both[:256] + sign * half(both[256:])
    mean_mode = (row == 0) & (lane == 0) & (jnp.zeros(shape, jnp.int32) + position() == 0)
    value = value + jnp.where(mean_mode, middle * NX * NY, 0.0)
    value = value * weights[...]
    both = product_rows(groups_back_h[...], groups_back_l[...], value)
    value = both[:256] - sign * half(both[256:])
    value = value * return_cos[...] - half(value) * return_sin[...]
    value = product_lanes(value, cells_back[...])
    value = value * theta_cos_back[...] - half(value) * theta_sin_back[...]
    first = jnp.zeros(shape, jnp.int32) + position() == 0
    value = jnp.where((lane >= 64) & (lane < 72) & first, roll(value, 32, 1), value)
    narrow = lanes_of((32, 128))
    none = jnp.zeros((32, 128), F32)
    back = jnp.concatenate(
        [
            jnp.concatenate([none, fluxes[:, k : k + 128], none, none, none[:16]], 0).T
            for k in (0, 128)
        ],
        0,
    )
    last = back[224:256]
    wrapped = turn_rows(last, wrap_hop(shifts), 1)
    ride = [back[32 * k : 32 * k + 32] for k in range(7)]
    ride.append(jnp.where((narrow >= 41) & (narrow < 44), wrapped, last))
    blocks = [value[32 * k : 32 * k + 32] for k in range(8)]
    for bit in (1, 2, 4):
        swapped = list(blocks)
        for k in range(8):
            if k & bit == 0:
                a, b = blocks[k], blocks[k + bit]
                low = narrow & bit == 0
                swapped[k] = jnp.where(low, a, roll(b, bit, 1))
                swapped[k + bit] = jnp.where(low, roll(a, -bit, 1), b)
        blocks = swapped
    spare = (narrow >= 32) & (narrow < 44)
    for k in range(8):
        out[32 * k : 32 * k + 32, :] = jnp.where(spare, ride[k], blocks[k])


def backward_kernel(arrived, inner, back_cos, back_sin, blocks_h, blocks_l, out):
    lane = lanes_of((32, 128))
    low = lane % 64 < 32
    pairs = []
    for h in range(4):
        even = arrived[64 * h : 64 * h + 32, :]
        odd = arrived[64 * h + 32 : 64 * h + 64, :]
        pairs.append(jnp.where(low, even, roll(odd, 32, 1)))
    value = jnp.concatenate(pairs, 1)
    head, rest = split(value)
    both = dot(inner[...], jnp.concatenate([head, rest, head], 0))
    wide = lanes_of((64, 128))
    row = rows_of((64, 128))
    sign = jnp.where(wide < 64, 1.0, -1.0)
    parity = jnp.where(row % 2 == 0, 1.0, -1.0)
    turned = []
    for h in range(4):
        tile = slice(128 * h, 128 * h + 128)
        part = both[:64, tile] - sign * roll(both[64:, tile], 64, 1)
        part = part * back_cos[:, tile] - roll(part, 64, 1) * back_sin[:, tile]
        if h == 0:
            part = jnp.where((wide >= 64) & (wide < 72), parity * pairs[0][0:1, :], part)
        turned.append(part)
    head, rest = split(jnp.concatenate(turned, 1))
    full = dot(blocks_h[...], jnp.concatenate([head, rest], 0), NT)
    full = full + roll(full, 64, 1)
    full = full + dot(blocks_l[...], jnp.concatenate([head, head], 0), NT)
    square = lanes_of((128, 128))
    out[...] = jnp.where(square < 64, full[:128], full[128:])


VMEM = pl.BlockSpec(memory_space=pltpu.VMEM)


def call(kernel, shapes, *args, name, work=20_000, kind=F32):
    many = isinstance(shapes, list)
    outs = [jax.ShapeDtypeStruct(s, kind) for s in (shapes if many else [shapes])]
    return pl.pallas_call(
        kernel,
        out_shape=outs if many else outs[0],
        in_specs=[VMEM] * len(args),
        out_specs=[VMEM] * len(outs) if many else VMEM,
        name=name,
        compiler_params=pltpu.CompilerParams(vmem_limit_bytes=32 * 1024 * 1024),
        cost_estimate=pl.CostEstimate(
            flops=work * 1_000_000, bytes_accessed=1_000_000, transcendentals=0
        ),
    )(*args)


def shards(density, xmomentum, ymomentum, shear_shift):
    t = host_tables()
    rho, mx, my = density[0], xmomentum[0], ymomentum[0]
    shifts = jnp.broadcast_to(shear_shift[0], (8, 128))
    everyone = ("gx", "gy")
    block = (ROWS, COLS)
    table = (256, 128)
    small = (8, 128)
    numbers = call(waves_kernel, small, name="waves", kind=jnp.int32)
    tables = call(tables_kernel, [table] * 5 + [small] * 2, shifts, numbers, name="tables", work=1)
    columns = call(pack_kernel, table, shifts, rho, mx, my, tables[-1], name="pack")
    columns = lax.all_to_all(columns, everyone, 0, 0, tiled=True)
    waves, fluxes = call(
        forward_kernel,
        [table, (16, 256)],
        shifts,
        columns,
        *t["blocks"],
        t["twist_cos"],
        t["twist_sin"],
        *t["inner"],
        name="forward",
    )
    waves = lax.all_to_all(waves, everyone, 0, 0, tiled=True)
    solved = call(
        radial_kernel,
        table,
        shifts,
        waves,
        fluxes,
        *tables,
        *t["groups"],
        t["radial_cos"],
        t["radial_sin"],
        t["cells"],
        t["cells_back"],
        *t["groups_back"],
        t["return_cos"],
        t["return_sin"],
        name="radial",
    )
    solved = lax.all_to_all(solved, everyone, 0, 0, tiled=True)
    lines = call(
        backward_kernel,
        (128, 128),
        solved,
        t["inner_back"],
        t["back_cos"],
        t["back_sin"],
        *t["blocks_back"],
        name="backward",
    )
    lines = lax.all_to_all(lines, "gy", 0, 0, tiled=True)
    rho_new, mx_new, my_new, potential = call(
        finish_kernel, [block] * 4, shifts, rho, mx, my, solved, lines, name="finish"
    )
    return rho_new[None], mx_new[None], my_new[None], potential[None]


def solution(mesh):
    spec = P(None, "gy", "gx")
    return jax.shard_map(
        shards,
        mesh=mesh,
        in_specs=(spec, spec, spec, P()),
        out_specs=(spec, spec, spec, spec),
        check_vma=False,
    )
```

```python
import functools

import jax
import jax.numpy as jnp
import ml_dtypes
import numpy as np
from jax import lax
from jax.experimental import pallas as pl
from jax.experimental.pallas import tpu as pltpu
from jax.sharding import PartitionSpec as P

NX = 2048
NY = 2048
ROWS = 64
COLS = 256
GX = 8
GY = 32

time_step = 0.15
omega_rate = 0.5
shear_rate = 1.5
thickness = 0.5
middle = 1.0

BF = jnp.bfloat16
F32 = jnp.float32


def halves(table):
    table = np.asarray(table, np.float32)
    head = table.astype(ml_dtypes.bfloat16)
    rest = (table - head.astype(np.float32)).astype(ml_dtypes.bfloat16)
    return head, rest


def both_parts(table):
    head, rest = halves(table)
    return np.block([[head, rest], [head, np.zeros_like(rest)]])


def turn(index, length):
    angle = 2.0 * np.pi * (np.asarray(index) % length) / length
    return np.cos(angle), np.sin(angle)


@functools.cache
def host_tables():
    out = {}
    eye8 = np.eye(8)
    cos32, sin32 = turn(np.outer(np.arange(32), np.arange(32)), 32)

    def spread(table):
        return np.einsum("jm,ab->ajmb", table, eye8).reshape(256, 256)

    out["blocks"] = halves(np.concatenate([spread(cos32), spread(-sin32)], 1))
    m1 = np.repeat(np.arange(32), 8)
    tc, ts = turn(np.outer(np.arange(64), m1), NY)
    out["twist_cos"] = tc.astype(np.float32)
    out["twist_sin"] = ts.astype(np.float32)
    c64, s64 = turn(np.outer(np.arange(32), np.arange(64)), 64)
    last = np.zeros((16, 128))
    last[0, :64] = 1.0 - 2.0 * (np.arange(64) % 2)
    head, rest = halves(
        np.concatenate([np.concatenate([c64, s64], 1), np.concatenate([-s64, c64], 1), last])
    )
    out["inner"] = np.concatenate([head, head], 1), rest
    rows = np.arange(256)
    c256, s256 = turn(np.outer(rows, rows), 256)
    out["groups"] = halves(np.concatenate([c256, s256]))
    lane = np.arange(128)
    sign = np.where(lane < 64, 1.0, -1.0)
    tc, ts = turn(np.outer(rows, lane % 8), NX)
    out["radial_cos"] = tc.astype(np.float32)
    out["radial_sin"] = (ts * sign).astype(np.float32)
    c8, s8 = turn(np.outer(np.arange(8), np.arange(8)), 8)
    lines = np.eye(8)
    ck, sk = np.kron(lines, c8), np.kron(lines, s8)
    out["cells"] = both_parts(np.block([[ck, -sk], [sk, ck]]))
    out["cells_back"] = both_parts(np.block([[ck, sk], [-sk, ck]]))
    order = rows // 128 * 128 + rows // 32 % 4 + 4 * (rows % 32)
    c256, s256 = turn(np.outer(order, rows), 256)
    out["groups_back"] = halves(np.concatenate([c256, s256]))
    tc, ts = turn(np.outer(order, lane % 8), NX)
    out["return_cos"] = tc.astype(np.float32)
    out["return_sin"] = (ts * sign).astype(np.float32)
    c64, s64 = turn(np.outer(np.arange(64), np.arange(32)), 64)
    head, rest = halves(np.concatenate([c64, s64]))
    out["inner_back"] = np.concatenate([head, head, rest], 1)
    pair = np.arange(512) // 128
    part = np.arange(512) % 128 // 64
    which = np.arange(512) % 64 // 8
    m1 = pair * 8 + which
    q = np.arange(512) % 8
    tc, ts = turn(np.outer(np.arange(64), m1), NY)
    out["back_cos"] = tc.astype(np.float32)
    out["back_sin"] = (ts * np.where(part == 0, 1.0, -1.0)).astype(np.float32)
    j = np.tile(np.repeat(np.arange(32), 4), 2)
    own = np.repeat([0, 4], 128) + np.tile(np.arange(4), 64)
    c32, s32 = turn(np.outer(j, m1), 32)
    weight = np.where(part == 0, c32, -s32)
    weight = np.where((part == 1) & (m1 == 0), 1.0, weight)
    out["blocks_back"] = halves(weight * (own[:, None] == q[None, :]))
    return out


def split(value):
    head = value.astype(BF)
    rest = (value - head.astype(F32)).astype(BF)
    return head, rest


NN = (((1,), (0,)), ((), ()))
NT = (((1,), (1,)), ((), ()))


def dot(left, right, dims=NN):
    return lax.dot_general(left, right, dims, preferred_element_type=F32)


def product_rows(table_head, table_rest, value):
    head, rest = split(value)
    both = dot(table_head, jnp.concatenate([head, rest], 1))
    return both[:, :128] + both[:, 128:] + dot(table_rest, head)


def product_lanes(value, table):
    both = dot(jnp.concatenate(split(value), 1), table)
    return both[:, :128] + both[:, 128:]


def product_right(value, table_head, table_rest):
    head, rest = split(value)
    return dot(head, table_head) + (dot(rest, table_head) + dot(head, table_rest))


def roll(value, shift, axis):
    return pltpu.roll(value, shift % value.shape[axis], axis)


def lanes_of(shape):
    return lax.broadcasted_iota(jnp.int32, shape, 1)


def rows_of(shape):
    return lax.broadcasted_iota(jnp.int32, shape, 0)


def position():
    return lax.axis_index("gx") * GY + lax.axis_index("gy")


def wrap_hop(shifts):
    row = position() & (ROWS - 1)
    shifts = jnp.broadcast_to(shifts[0:1, :], (GY, 128))
    return ((shifts >> 6) + (((shifts & (ROWS - 1)) + row) >> 6)) & (GY - 1)


def turn_rows(block, hop, way):
    for bit in range(5):
        moved = roll(block, way << bit, 0)
        block = jnp.where((hop >> bit) & 1 == 1, moved, block)
    return block


def turn_by_shift(block, shifts, way):
    off = jnp.broadcast_to(shifts[0:1, :], (ROWS, 128)) & (ROWS - 1)
    off = jnp.where(jnp.zeros((ROWS, 128), jnp.int32) + lax.axis_index("gx") == GX - 1, off, 0)
    for bit in range(6):
        moved = roll(block, way << bit, 0)
        block = jnp.where((off >> bit) & 1 == 1, moved, block)
    return block


def interface(left, right, normal, parts=3):
    speed = jnp.maximum(jnp.abs(left[3]), jnp.abs(right[3])) + 1.0
    fluxes = []
    for part in range(parts):
        f_left = left[part] * left[3]
        f_right = right[part] * right[3]
        if part == normal:
            f_left = f_left + left[0]
            f_right = f_right + right[0]
        fluxes.append(0.5 * (f_left + f_right) - 0.5 * speed * (right[part] - left[part]))
    return fluxes


def with_speed(fields, normal):
    return (*fields, fields[normal] / fields[0])


def inner_fluxes(state, parts):
    lane = lanes_of((ROWS, COLS))
    row = rows_of((ROWS, COLS))
    mid = with_speed(state, 1)
    west = interface([roll(v, 1, 1) for v in mid], mid, 1, parts)
    mid = with_speed(state, 2)
    south = interface([roll(v, 1, 0) for v in mid], mid, 2, parts)
    return [jnp.where(lane == 0, 0.0, v) for v in west], [jnp.where(row == 0, 0.0, v) for v in south]


def pack_kernel(shifts, rho, mx, my, after, out):
    del after
    state = (rho[...], mx[...], my[...])
    (west,), (south,) = inner_fluxes(state, 1)
    change = roll(west, -1, 1) - west + roll(south, -1, 0) - south
    partial = state[0] - time_step * change - middle
    row = rows_of((8, COLS))
    edges = jnp.zeros((8, COLS), F32)
    for f in range(3):
        edges = jnp.where(row == f, state[f][0:1, :], edges)
        edges = jnp.where(row == 3 + f, state[f][ROWS - 1 : ROWS, :], edges)
    tall = jnp.concatenate([partial, edges, jnp.zeros((56, COLS), F32)], 0).T
    lane = lanes_of((ROWS, 128))
    low = jnp.zeros((ROWS, 128), F32)
    high = jnp.zeros((ROWS, 128), F32)
    for f in range(3):
        low = jnp.where(lane == 72 + f, state[f][:, 0:1], low)
        high = jnp.where(lane == 75 + f, state[f][:, COLS - 1 : COLS], high)
    out[0:ROWS, :] = tall[0:ROWS] + low + turn_by_shift(high, shifts, -1)
    out[ROWS:, :] = tall[ROWS:]


def finish_kernel(shifts, rho, mx, my, arrived, lines, rho_out, mx_out, my_out, potential):
    state = (rho[...], mx[...], my[...])
    lane = lanes_of((ROWS, COLS))
    row = rows_of((ROWS, COLS))
    west, south = inner_fluxes(state, 3)
    across = arrived[...].T[32:40]
    beside = arrived[0:ROWS, :]
    beside_high = turn_by_shift(beside, shifts, 1)
    new = []
    for f in range(3):
        east = jnp.where(lane == COLS - 1, beside_high[:, 41 + f : 42 + f], roll(west[f], -1, 1))
        north = jnp.where(row == ROWS - 1, across[3 + f : 4 + f, :], roll(south[f], -1, 0))
        west_f = jnp.where(lane == 0, beside[:, 38 + f : 39 + f], west[f])
        south_f = jnp.where(row == 0, across[f : f + 1, :], south[f])
        new.append(state[f] - time_step * (east - west_f + north - south_f))
    rho_out[...] = new[0]
    mx_out[...] = new[1] + time_step * 2.0 * omega_rate * state[2]
    tall = lines[...].T
    potential[:, :128] = tall[:ROWS]
    potential[:, 128:] = tall[ROWS:]
    my_out[...] = new[2] - time_step * (2.0 - shear_rate) * omega_rate * state[1]


def circle(turns):
    quarter = jnp.floor(turns * 4.0 + 0.5)
    x = (turns - quarter * 0.25) * (2.0 * np.pi)
    y = x * x
    s = x * (1.0 + y * (-1 / 6 + y * (1 / 120 + y * (-1 / 5040 + y * (1 / 362880)))))
    c = 1.0 + y * (-1 / 2 + y * (1 / 24 + y * (-1 / 720 + y * (1 / 40320 - y * (1 / 3628800)))))
    k = quarter.astype(jnp.int32)
    swap = k & 1 == 1
    sine = jnp.where(swap, c, s)
    cosine = jnp.where(swap, s, c)
    return jnp.where((k + 1) & 2 == 2, -cosine, cosine), jnp.where(k & 2 == 2, -sine, sine)


def waves_kernel(waves):
    line = (lanes_of((8, 128)) & 63) >> 3
    wave = lax.axis_index("gx") * 4 + line + GY * lax.axis_index("gy")
    waves[...] = jnp.where(line < 4, wave, NY // 2)


def tables_kernel(
    shifts, waves, there_cos, there_sin, back_cos, back_sin, weights, wrap_cos, wrap_sin
):
    lane = lanes_of((8, 128))
    sigma = ((waves[...] * shifts[...]) & (NY - 1)).astype(F32)[0:1]
    sign = jnp.where(lane < 64, 1.0, -1.0)[0:1]

    def phase(rows, of_row, of_lane):
        shape = (rows, 128)
        cell = of_row(rows_of(shape)) + of_lane * COLS * (lanes_of(shape) & 7)
        return circle(sigma * cell.astype(F32) * (1.0 / (NX * NY)))

    def fill(cos_out, sin_out, coarse, fine):
        c1, s1 = coarse
        c2, s2 = fine
        size = c2.shape[0]
        for k in range(256 // size):
            at = slice(k * size, k * size + size)
            ck, sk = c1[k : k + 1], s1[k : k + 1]
            cos_out[at, :] = ck * c2 - sk * s2
            sin_out[at, :] = (sk * c2 + ck * s2) * sign

    fill(there_cos, there_sin, phase(16, lambda r: 16 * r, 0), phase(16, lambda r: r, 1))
    fill(
        back_cos,
        back_sin,
        phase(8, lambda r: (r >> 2) * 128 + (r & 3), 0),
        phase(32, lambda r: 4 * r, 1),
    )
    shape = (256, 128)
    lane = lanes_of(shape)
    wave = jnp.broadcast_to(waves[0:1, :], shape)
    n = (lane & 7) + 8 * rows_of(shape)
    n = jnp.where(n < NX // 2, n, n - NX)
    kx = 2.0 * np.pi / NX * (n.astype(F32) + sigma * (1.0 / NY))
    ky = 2.0 * np.pi / NY * wave.astype(F32)
    size = jnp.sqrt(kx * kx + ky * ky)
    anchor = (wave == 0) & (n == 0)
    size = jnp.where(anchor, 1.0, size)
    single = (wave == 0) | (wave == NY // 2)
    scale = jnp.where(single, 1.0, 2.0) / (NX * NY)
    weights[...] = jnp.where(anchor, 0.0, -jnp.exp(-thickness * size) / size) * scale
    c, s = circle(jnp.broadcast_to(sigma * (1.0 / NY), (8, 128)))
    last = lanes_of((8, 128)) & 7 == 7
    wrap_cos[...] = jnp.where(last, c, 1.0)
    wrap_sin[...] = jnp.where(last, s * sign, 0.0)


def edge_fluxes(shifts, arrived, parts):
    narrow = lanes_of((32, 128))
    last = arrived[224:256, :]
    wrapped = turn_rows(last, wrap_hop(shifts), -1)
    last = jnp.where((narrow >= 75) & (narrow < 78), wrapped, last)
    tall = jnp.concatenate([arrived[0:224, :], last], 0).T
    lane = lanes_of((8, 256))
    upper = tall[64:72]
    before = jnp.where(lane % 32 == 0, roll(upper, -31, 1), roll(upper, 1, 1))
    south = interface(
        with_speed([before[3 + f : 4 + f] for f in range(3)], 2),
        with_speed([upper[f : f + 1] for f in range(3)], 2),
        2,
        parts,
    )
    valid = jnp.zeros((1, 256), jnp.int32) + position() < ROWS
    side = tall[72:80]
    before = roll(side, 32, 1)
    left = [before[3 + f : 4 + f] for f in range(3)]
    right = [side[f : f + 1] for f in range(3)]
    left[0] = jnp.where(valid, left[0], 1.0)
    right[0] = jnp.where(valid, right[0], 1.0)
    west = interface(with_speed(left, 1), with_speed(right, 1), 1, parts)
    west = [jnp.where(valid, v, 0.0) for v in west]
    line = lanes_of((1, 256))
    north = [jnp.where(line % 32 == 31, roll(v, 31, 1), roll(v, -1, 1)) for v in south]
    return tall, west, south, north


def forward_kernel(shifts, arrived, blocks_h, blocks_l, twist_cos, twist_sin, inner_h, inner_l, out, fluxes):
    tall, west, south, north = edge_fluxes(shifts, arrived, 3)
    rows16 = rows_of((16, 256))
    held = jnp.zeros((16, 256), F32)
    for at, value in enumerate(south + north + west + [roll(v, -32, 1) for v in west]):
        held = jnp.where(rows16 == at, value, held)
    fluxes[...] = held
    narrow = lanes_of((32, 128))
    rows64 = rows_of((64, 256))
    density = tall[0:64]
    density = density + jnp.where(rows64 == 0, time_step * south[0], 0.0)
    density = density - jnp.where(rows64 == 63, time_step * north[0], 0.0)
    edge = jnp.where(rows16 == 0, time_step * west[0], 0.0)
    first = product_right(jnp.concatenate([density, edge], 0), blocks_h[...], blocks_l[...])
    tc = twist_cos[...]
    ts = twist_sin[...]
    re, im = first[:64, :256], first[:64, 256:]
    main = jnp.concatenate([re * tc + im * ts, im * tc - re * ts], 0)
    re, im = first[64:65, :256], first[64:65, 256:]
    here = rows64 == position()
    edge = jnp.concatenate(
        [jnp.where(here, re * tc + im * ts, 0.0), jnp.where(here, im * tc - re * ts, 0.0)], 0
    )
    head, rest = split(jnp.concatenate([main, edge], 1))
    waves = dot(inner_h[...], jnp.concatenate([head, rest], 0)) + dot(inner_l[...], head)
    rows32 = rows_of((32, 128))
    for g in range(8):
        place = 32 * (g % 4)
        pieces = []
        for start in (0, 256):
            tile = slice(start + g // 4 * 128, start + g // 4 * 128 + 128)
            real = waves[0:32, tile]
            imag = waves[32:64, tile]
            if g == 0:
                imag = jnp.where((rows32 == 0) & (narrow < 8), waves[64:65, tile], imag)
            pieces.append((real, imag))
        both = roll(pieces[1][1], 96 - place, 1)
        both = jnp.where(narrow < 96, roll(pieces[0][1], 64 - place, 1), both)
        both = jnp.where(narrow < 64, roll(pieces[1][0], 32 - place, 1), both)
        both = jnp.where(narrow < 32, roll(pieces[0][0], -place, 1), both)
        out[g * 32 : (g + 1) * 32, :] = both


def radial_kernel(
    shifts,
    arrived,
    fluxes,
    theta_cos,
    theta_sin,
    theta_cos_back,
    theta_sin_back,
    weights,
    wrap_cos,
    wrap_sin,
    groups_h,
    groups_l,
    radial_cos,
    radial_sin,
    cells,
    cells_back,
    groups_back_h,
    groups_back_l,
    return_cos,
    return_sin,
    out,
):
    shape = (256, 128)
    half = functools.partial(roll, shift=64, axis=1)

    def apart(value):
        lane = lanes_of(value.shape)
        first = jnp.zeros(value.shape, jnp.int32) + position() == 0
        fifth = roll(value, -32, 1)
        none = ((lane >= 64) & (lane < 72) & first) | ((lane >= 96) & (lane < 104))
        return jnp.where((lane >= 32) & (lane < 40), fifth, jnp.where(none, 0.0, value))

    lane = lanes_of(shape)
    row = rows_of(shape)
    sign = jnp.where(lane < 64, 1.0, -1.0)
    value = arrived[...]
    edge = jnp.sum(value[0:ROWS], axis=0, keepdims=True)
    edge = apart(roll(jnp.broadcast_to(edge, (8, 128)), -32, 1))
    lane8 = lanes_of((8, 128))
    beside = jnp.where(lane8 % 8 == 7, roll(edge, 7, 1), roll(edge, -1, 1))
    beside = beside * wrap_cos[...] + half(beside) * wrap_sin[...]
    value = apart(value)
    value = value + jnp.where(row == 0, edge[0:1], 0.0) - jnp.where(row == 255, beside[0:1], 0.0)
    value = value * theta_cos[...] + half(value) * theta_sin[...]
    value = product_lanes(value, cells[...])
    value = value * radial_cos[...] + half(value) * radial_sin[...]
    both = product_rows(groups_h[...], groups_l[...], value)
    value = both[:256] + sign * half(both[256:])
    mean_mode = (row == 0) & (lane == 0) & (jnp.zeros(shape, jnp.int32) + position() == 0)
    value = value + jnp.where(mean_mode, middle * NX * NY, 0.0)
    value = value * weights[...]
    both = product_rows(groups_back_h[...], groups_back_l[...], value)
    value = both[:256] - sign * half(both[256:])
    value = value * return_cos[...] - half(value) * return_sin[...]
    value = product_lanes(value, cells_back[...])
    value = value * theta_cos_back[...] - half(value) * theta_sin_back[...]
    first = jnp.zeros(shape, jnp.int32) + position() == 0
    value = jnp.where((lane >= 64) & (lane < 72) & first, roll(value, 32, 1), value)
    narrow = lanes_of((32, 128))
    none = jnp.zeros((32, 128), F32)
    back = jnp.concatenate(
        [
            jnp.concatenate([none, fluxes[:, k : k + 128], none, none, none[:16]], 0).T
            for k in (0, 128)
        ],
        0,
    )
    last = back[224:256]
    wrapped = turn_rows(last, wrap_hop(shifts), 1)
    ride = [back[32 * k : 32 * k + 32] for k in range(7)]
    ride.append(jnp.where((narrow >= 41) & (narrow < 44), wrapped, last))
    blocks = [value[32 * k : 32 * k + 32] for k in range(8)]
    for bit in (1, 2, 4):
        swapped = list(blocks)
        for k in range(8):
            if k & bit == 0:
                a, b = blocks[k], blocks[k + bit]
                low = narrow & bit == 0
                swapped[k] = jnp.where(low, a, roll(b, bit, 1))
                swapped[k + bit] = jnp.where(low, roll(a, -bit, 1), b)
        blocks = swapped
    spare = (narrow >= 32) & (narrow < 44)
    for k in range(8):
        out[32 * k : 32 * k + 32, :] = jnp.where(spare, ride[k], blocks[k])


def backward_kernel(arrived, inner, back_cos, back_sin, blocks_h, blocks_l, out):
    lane = lanes_of((32, 128))
    low = lane % 64 < 32
    pairs = []
    for h in range(4):
        even = arrived[64 * h : 64 * h + 32, :]
        odd = arrived[64 * h + 32 : 64 * h + 64, :]
        pairs.append(jnp.where(low, even, roll(odd, 32, 1)))
    value = jnp.concatenate(pairs, 1)
    head, rest = split(value)
    both = dot(inner[...], jnp.concatenate([head, rest, head], 0))
    wide = lanes_of((64, 128))
    row = rows_of((64, 128))
    sign = jnp.where(wide < 64, 1.0, -1.0)
    parity = jnp.where(row % 2 == 0, 1.0, -1.0)
    turned = []
    for h in range(4):
        tile = slice(128 * h, 128 * h + 128)
        part = both[:64, tile] - sign * roll(both[64:, tile], 64, 1)
        part = part * back_cos[:, tile] - roll(part, 64, 1) * back_sin[:, tile]
        if h == 0:
            part = jnp.where((wide >= 64) & (wide < 72), parity * pairs[0][0:1, :], part)
        turned.append(part)
    head, rest = split(jnp.concatenate(turned, 1))
    full = dot(blocks_h[...], jnp.concatenate([head, rest], 0), NT)
    full = full + roll(full, 64, 1)
    full = full + dot(blocks_l[...], jnp.concatenate([head, head], 0), NT)
    square = lanes_of((128, 128))
    out[...] = jnp.where(square < 64, full[:128], full[128:])


VMEM = pl.BlockSpec(memory_space=pltpu.VMEM)


def call(kernel, shapes, *args, name, work=20_000, kind=F32):
    many = isinstance(shapes, list)
    outs = [jax.ShapeDtypeStruct(s, kind) for s in (shapes if many else [shapes])]
    return pl.pallas_call(
        kernel,
        out_shape=outs if many else outs[0],
        in_specs=[VMEM] * len(args),
        out_specs=[VMEM] * len(outs) if many else VMEM,
        name=name,
        compiler_params=pltpu.CompilerParams(vmem_limit_bytes=32 * 1024 * 1024),
        cost_estimate=pl.CostEstimate(
            flops=work * 1_000_000, bytes_accessed=1_000_000, transcendentals=0
        ),
    )(*args)


def shards(density, xmomentum, ymomentum, shear_shift):
    t = host_tables()
    rho, mx, my = density[0], xmomentum[0], ymomentum[0]
    shifts = jnp.broadcast_to(shear_shift[0], (8, 128))
    everyone = ("gx", "gy")
    block = (ROWS, COLS)
    table = (256, 128)
    small = (8, 128)
    numbers = call(waves_kernel, small, name="waves", kind=jnp.int32)
    tables = call(tables_kernel, [table] * 5 + [small] * 2, shifts, numbers, name="tables", work=1)
    columns = call(pack_kernel, table, shifts, rho, mx, my, tables[-1], name="pack")
    columns = lax.all_to_all(columns, everyone, 0, 0, tiled=True)
    waves, fluxes = call(
        forward_kernel,
        [table, (16, 256)],
        shifts,
        columns,
        *t["blocks"],
        t["twist_cos"],
        t["twist_sin"],
        *t["inner"],
        name="forward",
    )
    waves = lax.all_to_all(waves, everyone, 0, 0, tiled=True)
    solved = call(
        radial_kernel,
        table,
        shifts,
        waves,
        fluxes,
        *tables,
        *t["groups"],
        t["radial_cos"],
        t["radial_sin"],
        t["cells"],
        t["cells_back"],
        *t["groups_back"],
        t["return_cos"],
        t["return_sin"],
        name="radial",
    )
    solved = lax.all_to_all(solved, everyone, 0, 0, tiled=True)
    lines = call(
        backward_kernel,
        (128, 128),
        solved,
        t["inner_back"],
        t["back_cos"],
        t["back_sin"],
        *t["blocks_back"],
        name="backward",
    )
    lines = lax.all_to_all(lines, "gy", 0, 0, tiled=True)
    rho_new, mx_new, my_new, potential = call(
        finish_kernel, [block] * 4, shifts, rho, mx, my, solved, lines, name="finish"
    )
    return rho_new[None], mx_new[None], my_new[None], potential[None]


def solution(mesh):
    spec = P(None, "gy", "gx")
    return jax.shard_map(
        shards,
        mesh=mesh,
        in_specs=(spec, spec, spec, P()),
        out_specs=(spec, spec, spec, spec),
        check_vma=False,
    )
```
